256 devices in a mesh: sec: 2 (over y_hi), gy: 16 (over y_lo, z), gx: 8 (over x, core).
Axes of the slice: x: 4, y: 4 (y_hi: 2, y_lo: 2; y = y_hi * 2 + y_lo), z: 8, core: 2. Of those that a mesh axis runs over, the one named last changes fastest.
Arguments:
- spectrum: float32 [36, 20, 512, 1024], P(None, None, ('sec', 'gy'), 'gx'), may hold values from 0.1 to 1
- sea_mask: int32 [512, 1024], P(('sec', 'gy', 'gx')), may hold values 0 or 1
- ocean_state: float32 [3, 768, 1536], P(None, ('sec', 'gy', 'gx')), may hold values from -3 to 3
- depth: float32 [768, 1536], P(('sec', 'gy', 'gx')), may hold values from 0.5 to 2
Outputs:
- spectrum_out: float32 [36, 20, 512, 1024], P(None, None, ('sec', 'gy'), 'gx')
- ocean_out: float32 [3, 768, 1536], P(None, ('sec', 'gy', 'gx'))
The draws below stay inside these ranges and needn't reach their ends.
All inputs are finite; a program needn't handle non-finite values. No bound on the sum of `sea_mask` on one device may be relied on, other than what follows from the above.
Results may differ from the reference program's by a relative error of at most 0.0001.
Values sent between devices are 32-bit elements; how exact they have to be, the bound alone decides.
A program may use at most 128 MiB of HBM per device.

```python
import math
import jax
import jax.numpy as jnp
from jax import lax

NDIR = 36
NFREQ = 20
NXW = 1024
ITERS = 4
NYW = 512
NYO = 768
NXO = 1536


def plant(array, key, least, top_value):
    shape = array.shape
    index_at = [jax.random.randint(jax.random.fold_in(key, axis), (), 0, shape[axis]) for axis in range(len(shape))]
    array = array.at[tuple(index_at)].set(least)
    longest = shape.index(max(shape))
    index_at[longest] = (index_at[longest] + 1) % shape[longest]
    return array.at[tuple(index_at)].set(top_value)


def level_of(rng, extent, split, least, top_value):
    factor_of = 1.0
    for dim, shards_of in split:
        steps = jax.random.uniform(jax.random.fold_in(jax.random.fold_in(rng, 6), dim), (shards_of,), jnp.float32, least / len(split), top_value / len(split))
        factor_of = factor_of * jnp.repeat(jnp.exp(steps), extent[dim] // shards_of).reshape((-1,) + (1,) * (len(extent) - 1 - dim))
    return factor_of


def noise(stream_key, dims, deviation, reach, cuts=(), kind=jnp.bfloat16):
    values = deviation * jax.random.normal(stream_key, dims, jnp.float32)
    if cuts:
        values = values * level_of(stream_key, dims, cuts, -0.22, 0.18)
    return jnp.clip(values, -reach, reach).astype(kind)


def setup_inputs(seed: int = 0) -> dict:
    splits = jax.random.split(jax.random.key(seed), 5)
    return {
        "spectrum": jnp.clip(jnp.exp(math.log(1.0) - 2.3025851 * jax.random.uniform(splits[0], (NDIR, NFREQ, NYW, NXW), jnp.float32) ** level_of(splits[0], (NDIR, NFREQ, NYW, NXW), ((2, 32), (3, 8)), -0.2, 0.2)), 0.1, 1.0),
        "sea_mask": plant((jax.random.randint(splits[1], (NYW, NXW), 0, 5) < 4).astype(jnp.int32), jax.random.fold_in(splits[1], 1), 0, 1),
        "ocean_state": noise(splits[2], (3, NYO, NXO), 0.5, 3.0, ((1, 256),), jnp.float32),
        "depth": jnp.clip(jnp.exp(math.log(2.0) - 1.3862944 * jax.random.uniform(splits[3], (NYO, NXO), jnp.float32) ** level_of(splits[3], (NYO, NXO), ((0, 256),), -0.2, 0.2)), 0.5, 2.0),
    }


TWO_THIRDS = 2.0 / 3.0
ONE_THIRD = 1.0 / 3.0
GRAVITY_STEP = 0.3
CORIOLIS_STEP = 0.2
STRESS_GAIN = 2.0
TURN_GAIN = 0.2
SPEED_BASE = 0.35
SPEED_RATIO = 0.9


def to_wave_grid(field):
    def along_rows(values):
        shape = values.shape
        groups = values.reshape(shape[:-2] + (shape[-2] // 3, 3, shape[-1]))
        first = groups[..., 0, :]
        middle = groups[..., 1, :]
        last = groups[..., 2, :]
        lower = TWO_THIRDS * first + ONE_THIRD * middle
        upper = ONE_THIRD * middle + TWO_THIRDS * last
        return jnp.stack([lower, upper], axis=-2).reshape(shape[:-2] + (2 * (shape[-2] // 3), shape[-1]))
    rowwise = along_rows(field)
    return jnp.swapaxes(along_rows(jnp.swapaxes(rowwise, -1, -2)), -1, -2)


def to_ocean_grid(field):
    def along_rows(values):
        shape = values.shape
        groups = values.reshape(shape[:-2] + (shape[-2] // 2, 2, shape[-1]))
        first = groups[..., 0, :]
        second = groups[..., 1, :]
        middle = 0.5 * first + 0.5 * second
        return jnp.stack([first, middle, second], axis=-2).reshape(shape[:-2] + (3 * (shape[-2] // 2), shape[-1]))
    rowwise = along_rows(field)
    return jnp.swapaxes(along_rows(jnp.swapaxes(rowwise, -1, -2)), -1, -2)


def mask_to_ocean(field):
    def along_rows(values):
        shape = values.shape
        groups = values.reshape(shape[:-2] + (shape[-2] // 2, 2, shape[-1]))
        first = groups[..., 0, :]
        second = groups[..., 1, :]
        return jnp.stack([first, first, second], axis=-2).reshape(shape[:-2] + (3 * (shape[-2] // 2), shape[-1]))
    rowwise = along_rows(field)
    return jnp.swapaxes(along_rows(jnp.swapaxes(rowwise, -1, -2)), -1, -2)


def gradients(padded):
    along_x = (padded[..., 1:-1, 2:] - padded[..., 1:-1, :-2]) * 0.5
    along_y = (padded[..., 2:, 1:-1] - padded[..., :-2, 1:-1]) * 0.5
    return along_x, along_y


def wave_tables(ndir, nfreq):
    index_dir = jnp.arange(ndir, dtype=jnp.float32)
    heading = 2.0 * math.pi * (index_dir + 0.5) / ndir
    index_freq = jnp.arange(nfreq, dtype=jnp.float32)
    speed = SPEED_BASE * jnp.power(SPEED_RATIO, index_freq)
    cosine = jnp.cos(heading)
    sine = jnp.sin(heading)
    east_speed = cosine[:, None] * speed[None, :]
    north_speed = sine[:, None] * speed[None, :]
    stress_table = jnp.stack([0.5 * cosine * cosine, 0.5 * sine * cosine, 0.5 * sine * sine]) / (ndir * nfreq)
    return east_speed, north_speed, stress_table


def wave_update(masked, south_rows, north_rows, wave_mask, vorticity, divergence, east_speed, north_speed, stress_table):
    def parts(speed):
        return (jnp.maximum(speed, 0.0)[:, :, None, None], jnp.minimum(speed, 0.0)[:, :, None, None], jnp.abs(speed)[:, :, None, None])
    east_pos, east_neg, east_abs = parts(east_speed)
    north_pos, north_neg, north_abs = parts(north_speed)
    west_cells = jnp.pad(masked, ((0, 0), (0, 0), (0, 0), (1, 0)))[..., :-1]
    east_cells = jnp.pad(masked, ((0, 0), (0, 0), (0, 0), (0, 1)))[..., 1:]
    east_term = east_pos * west_cells - east_abs * masked - east_neg * east_cells
    north_term = north_pos * south_rows - north_abs * masked - north_neg * north_rows
    turning = TURN_GAIN * jnp.tanh(vorticity)
    turn_pos = jnp.maximum(turning, 0.0)[None, None]
    turn_neg = jnp.minimum(turning, 0.0)[None, None]
    turn_abs = jnp.abs(turning)[None, None]
    turn_term = turn_pos * jnp.roll(masked, 1, axis=0) - turn_abs * masked - turn_neg * jnp.roll(masked, -1, axis=0)
    shifting = TURN_GAIN * jnp.tanh(divergence)
    shift_pos = jnp.maximum(shifting, 0.0)[None, None]
    shift_neg = jnp.minimum(shifting, 0.0)[None, None]
    faces = shift_pos * masked[:, :-1] + shift_neg * masked[:, 1:]
    padded_faces = jnp.pad(faces, ((0, 0), (1, 1), (0, 0), (0, 0)))
    shift_term = padded_faces[:, :-1] - padded_faces[:, 1:]
    updated = ((((masked + east_term) + north_term) + turn_term) + shift_term) * wave_mask[None, None]
    stress = jnp.einsum("kjrx,sk->srx", updated, stress_table, precision=lax.Precision.HIGHEST)
    return updated, stress


def zero_rim(stack):
    return jnp.pad(stack, ((0, 0), (1, 1), (1, 1)))


def reference(spectrum, sea_mask, ocean_state, depth):
    wave_mask = sea_mask.astype(jnp.float32)
    ocean_mask = mask_to_ocean(wave_mask)
    state = ocean_state * ocean_mask[None]
    surface, eastward, northward = state[0], state[1], state[2]
    along_x, along_y = gradients(zero_rim(state[1:3]))
    vorticity = to_wave_grid(along_x[1] - along_y[0])
    divergence = to_wave_grid(along_x[0] + along_y[1])
    east_speed, north_speed, stress_table = wave_tables(NDIR, NFREQ)
    block_rows = 8

    def one_block(block, carry):
        result, stress = carry
        start = (block * block_rows).astype(jnp.int32)
        center = lax.dynamic_slice_in_dim(spectrum, start, block_rows, 2) * lax.dynamic_slice_in_dim(wave_mask, start, block_rows, 0)[None, None]
        top = jnp.maximum(start - 1, 0).astype(jnp.int32)
        bottom = jnp.minimum(start + block_rows, NYW - 1).astype(jnp.int32)
        above = lax.dynamic_slice_in_dim(spectrum, top, 1, 2) * lax.dynamic_slice_in_dim(wave_mask, top, 1, 0)[None, None] * jnp.where(start > 0, 1.0, 0.0)
        below = lax.dynamic_slice_in_dim(spectrum, bottom, 1, 2) * lax.dynamic_slice_in_dim(wave_mask, bottom, 1, 0)[None, None] * jnp.where(start + block_rows < NYW, 1.0, 0.0)
        south_rows = jnp.concatenate([above, center[:, :, :-1]], axis=2)
        north_rows = jnp.concatenate([center[:, :, 1:], below], axis=2)
        updated, rows_stress = wave_update(
            center, south_rows, north_rows,
            lax.dynamic_slice_in_dim(wave_mask, start, block_rows, 0),
            lax.dynamic_slice_in_dim(vorticity, start, block_rows, 0),
            lax.dynamic_slice_in_dim(divergence, start, block_rows, 0),
            east_speed, north_speed, stress_table)
        result = lax.dynamic_update_slice_in_dim(result, updated, start, 2)
        stress = lax.dynamic_update_slice_in_dim(stress, rows_stress, start, 1)
        return result, stress

    spectrum_out, stress = lax.fori_loop(0, NYW // block_rows, one_block, (jnp.zeros_like(spectrum), jnp.zeros((3, NYW, NXW), jnp.float32)))
    along_x, along_y = gradients(zero_rim(to_ocean_grid(stress)))
    force_x = -STRESS_GAIN * (along_x[0] + along_y[1]) / depth
    force_y = -STRESS_GAIN * (along_x[1] + along_y[2]) / depth
    for step in range(ITERS):
        along_x, along_y = gradients(zero_rim(jnp.stack([depth * eastward, depth * northward])))
        surface = (surface - GRAVITY_STEP * (along_x[0] + along_y[1])) * ocean_mask
        along_x, along_y = gradients(zero_rim(surface[None]))
        new_east = (eastward + GRAVITY_STEP * (CORIOLIS_STEP * northward - along_x[0]) + force_x) * ocean_mask
        new_north = (northward + GRAVITY_STEP * (-CORIOLIS_STEP * eastward - along_y[0]) + force_y) * ocean_mask
        eastward, northward = new_east, new_north
    return spectrum_out, jnp.stack([surface, eastward, northward])
```

```python
import functools
import math

import jax
import jax.numpy as jnp
from jax import lax
from jax.experimental import pallas as pl
from jax.experimental.pallas import tpu as pltpu
from jax.sharding import PartitionSpec as P

ITERS = 4
GRAVITY_STEP = 0.3
CORIOLIS_STEP = 0.2
STRESS_GAIN = 2.0
TURN_GAIN = 0.2
SPEED_BASE = 0.35
SPEED_RATIO = 0.9

NDIR = 36
NFREQ = 20
ROWS = 16
LANES = 128
CELLS = NDIR * NFREQ * ROWS
PER_DIR = NFREQ * ROWS
QUARTER = NDIR // 4
HALF = NDIR // 2 * NFREQ
PEERS = 8
SLOTS = 16
MARGIN_O = 24
MARGIN_W = 16
SPEEDS = [SPEED_BASE * SPEED_RATIO**j for j in range(NFREQ)]
STEP_ANGLE = 2.0 * math.pi / NDIR
MESH = pl.DeviceIdType.MESH
AROUND = [(1, 0), (-1, 0), (0, 1), (0, -1), (1, 1), (1, -1), (-1, 1), (-1, -1)]


def iota(shape, dim):
    return lax.broadcasted_iota(jnp.int32, shape, dim)


def next_angle(cosine, sine):
    turn_c, turn_s = math.cos(STEP_ANGLE), math.sin(STEP_ANGLE)
    return cosine * turn_c - sine * turn_s, sine * turn_c + cosine * turn_s


def first_angle():
    return jnp.float32(math.cos(0.5 * STEP_ANGLE)), jnp.float32(math.sin(0.5 * STEP_ANGLE))


def exact_dot(values, weights):
    rows = values.shape[0]
    high = values.astype(jnp.bfloat16)
    rest = values - high.astype(jnp.float32)
    middle = rest.astype(jnp.bfloat16)
    low = (rest - middle.astype(jnp.float32)).astype(jnp.bfloat16)
    stacked = jnp.concatenate([high, middle, low], axis=0)
    product = jnp.dot(stacked, weights, preferred_element_type=jnp.float32)
    return product[:rows] + product[rows : 2 * rows] + product[2 * rows :]


def ocean_shift(values, amount):
    return pltpu.roll(values, amount % values.shape[1], 1)


def along_x(values):
    return (ocean_shift(values, -1) - ocean_shift(values, 1)) * 0.5


def along_y(classes):
    above = [classes[1], classes[2], pltpu.roll(classes[0], SLOTS - 1, 0)]
    below = [pltpu.roll(classes[2], 1, 0), classes[0], classes[1]]
    return [(above[c] - below[c]) * 0.5 for c in range(3)]


def coupled_kernel(
    groups_y,
    groups,
    spectrum,
    sea_mask,
    ocean_state,
    depth,
    ocean_out,
    fields_out,
    rows_out,
    cols_out,
    cells,
    raw,
    raw_mask,
    pack,
    window,
    flux,
    flux_cols,
    flux_rows,
    stress,
    result,
    result_send,
    result_land,
    rows_send,
    cols_send,
    load_sem,
    pack_sem,
    band_sem,
    flux_sem,
    stress_sem,
    result_sem,
    halo_sem,
    local_sem,
):
    x = lax.axis_index("gx")
    y = lax.axis_index("sec") * groups_y + lax.axis_index("gy")

    def exists(dy, dx):
        checks = []
        if dy > 0:
            checks.append(y < groups - 1)
        if dy < 0:
            checks.append(y > 0)
        if dx > 0:
            checks.append(x < PEERS - 1)
        if dx < 0:
            checks.append(x > 0)
        answer = checks[0]
        for check in checks[1:]:
            answer = jnp.logical_and(answer, check)
        return answer

    def device(dy, dx):
        row = y + dy
        return (row // groups_y, lax.rem(row, groups_y), x + dx)

    def peer(step):
        return (lax.axis_index("sec"), lax.axis_index("gy"), lax.rem(x + step, PEERS))

    def load(direction):
        span = pl.ds(pl.multiple_of(direction * PER_DIR, PER_DIR), PER_DIR)
        return pltpu.make_async_copy(spectrum.at[span], cells.at[span], load_sem.at[direction])

    def start_load(i, carry):
        for q in range(4):
            load(q * QUARTER + i).start()
        return carry

    lax.fori_loop(0, QUARTER, start_load, 0)

    barrier = pltpu.get_barrier_semaphore()
    for step in range(1, PEERS):
        pl.semaphore_signal(barrier, inc=1, device_id=peer(step), device_id_type=MESH)
    greeted = PEERS - 1
    for dy, dx in AROUND:
        if dy != 0:
            here = exists(dy, dx)

            @pl.when(here)
            def _():
                pl.semaphore_signal(barrier, inc=1, device_id=device(dy, dx), device_id_type=MESH)

            greeted = greeted + here.astype(jnp.int32)

    raw[...] = jnp.zeros_like(raw)
    raw_mask[...] = jnp.zeros_like(raw_mask)
    width = ocean_state.shape[2]
    for f in range(3):
        raw[3 * f : 3 * f + 3, :width] = ocean_state[f]
    raw[9:12, :width] = depth[...]
    raw_mask[12:14, : sea_mask.shape[1]] = sea_mask[...].astype(jnp.float32)
    even = ocean_shift(raw[...], MARGIN_O)
    odd = ocean_shift(raw[...], MARGIN_O - 64)
    mask_rows = ocean_shift(raw_mask[...], MARGIN_W)
    is_ocean = iota((SLOTS, LANES), 0) < 12
    for dest in range(PEERS):
        source = odd if dest % 2 else even
        origin = 384 * (dest // 2) + (128 if dest % 2 else 0)
        for tile in range(2):
            pack[dest, tile] = jnp.where(
                is_ocean,
                source[:, origin + LANES * tile : origin + LANES * (tile + 1)],
                mask_rows[:, LANES * (dest + tile) : LANES * (dest + tile + 1)],
            )

    slab = jnp.zeros((2, 2 * SLOTS, LANES), jnp.float32)
    window[:, 11 * SLOTS : 13 * SLOTS, :] = slab
    edge = jnp.zeros((2, 3 * SLOTS, LANES), jnp.float32)

    @pl.when(y == 0)
    def _():
        window[:, 13 * SLOTS : 16 * SLOTS, :] = edge
        flux_rows[0] = jnp.zeros((3, 8, LANES), jnp.float32)
        stress[:, :, 24:32, :] = jnp.zeros((3, 3, 8, LANES), jnp.float32)

    @pl.when(y == groups - 1)
    def _():
        window[:, 8 * SLOTS : 11 * SLOTS, :] = edge
        flux_rows[1] = jnp.zeros((3, 8, LANES), jnp.float32)
        stress[:, :, 16:24, :] = jnp.zeros((3, 3, 8, LANES), jnp.float32)

    @pl.when(x == 0)
    def _():
        flux_cols[0] = jnp.zeros((3, ROWS, LANES), jnp.float32)
        stress[2] = jnp.zeros((3, 32, LANES), jnp.float32)

    @pl.when(x == PEERS - 1)
    def _():
        flux_cols[1] = jnp.zeros((3, ROWS, LANES), jnp.float32)
        stress[1] = jnp.zeros((3, 32, LANES), jnp.float32)

    mine = pl.ds(pl.multiple_of(x * SLOTS, SLOTS), SLOTS)

    def pack_copy(step):
        dest = peer(step)
        return pltpu.make_async_remote_copy(
            src_ref=pack.at[dest[2]],
            dst_ref=window.at[:, mine, :],
            send_sem=pack_sem.at[0, step],
            recv_sem=pack_sem.at[1, step],
            device_id=dest,
            device_id_type=MESH,
        )

    pl.semaphore_wait(barrier, greeted)
    for step in range(1, PEERS):
        pack_copy(step).start()
    window[:, mine, :] = pack[x]

    def sums(direction):
        base = direction * PER_DIR
        total = weighted = None
        for j in range(NFREQ):
            value = cells[pl.ds(pl.multiple_of(base + j * ROWS, ROWS), ROWS), :]
            total = value if j == 0 else total + value
            scaled = value * SPEEDS[j]
            weighted = scaled if j == 0 else weighted + scaled
        return total, weighted

    def gather(i, carry):
        (cosine, sine), plain, fluxes = carry
        for q in range(4):
            load(q * QUARTER + i).wait()
        scale = 0.5 / (NDIR * NFREQ)
        cc, cs, ss = cosine * cosine * scale, cosine * sine * scale, sine * sine * scale
        totals, weighted = zip(*[sums(q * QUARTER + i) for q in range(4)])
        pair = (totals[0] + totals[2]) - (totals[1] + totals[3])
        plain = (
            plain[0] + ((totals[0] + totals[2]) + (totals[1] + totals[3])),
            plain[1] + (cc - ss) * pair,
            plain[2] + (2.0 * cs) * pair,
        )
        straight, crossed = (cc, cs, ss), (ss, -cs, cc)
        west, east, south, north = fluxes
        west = tuple(
            west[s] + (cosine * straight[s]) * weighted[0] + (sine * crossed[s]) * weighted[3] for s in range(3)
        )
        east = tuple(
            east[s] + (cosine * straight[s]) * weighted[2] + (sine * crossed[s]) * weighted[1] for s in range(3)
        )
        south = tuple(
            south[s] + (sine * straight[s]) * weighted[0] + (cosine * crossed[s]) * weighted[1] for s in range(3)
        )
        north = tuple(
            north[s] + (sine * straight[s]) * weighted[2] + (cosine * crossed[s]) * weighted[3] for s in range(3)
        )
        return next_angle(cosine, sine), plain, (west, east, south, north)

    zero = jnp.zeros((ROWS, LANES), jnp.float32)
    triple = (zero, zero, zero)
    state = (first_angle(), triple, (triple, triple, triple, triple))
    state = lax.fori_loop(0, QUARTER // 2, gather, state)

    for step in range(1, PEERS):
        pack_copy(step).wait_recv()

    def band_copy(n):
        dy = 1 if n == 0 else -1
        source = pl.ds((5 if n == 0 else 0) * SLOTS, 3 * SLOTS)
        target = pl.ds((13 if n == 0 else 8) * SLOTS, 3 * SLOTS)
        return pltpu.make_async_remote_copy(
            src_ref=window.at[:, source, :],
            dst_ref=window.at[:, target, :],
            send_sem=band_sem.at[0, n],
            recv_sem=band_sem.at[1, n],
            device_id=device(dy, 0),
            device_id_type=MESH,
        )

    vertical = (exists(1, 0), exists(-1, 0))
    from_side = (exists(-1, 0), exists(1, 0))
    for n in range(2):

        @pl.when(vertical[n])
        def _():
            band_copy(n).start()

    _, plain, fluxes = lax.fori_loop(QUARTER // 2, QUARTER, gather, state)
    for side in range(4):
        for s in range(3):
            flux[side, s] = fluxes[side][s]

    def flux_copy(n):
        if n < 2:
            source, target, dest = flux.at[n], flux_cols.at[n], device(0, 1 if n == 0 else -1)
        else:
            span = pl.ds(8 if n == 2 else 0, 8)
            source, target, dest = flux.at[n, :, span, :], flux_rows.at[n - 2], device(1 if n == 2 else -1, 0)
        return pltpu.make_async_remote_copy(
            src_ref=source,
            dst_ref=target,
            send_sem=flux_sem.at[0, n],
            recv_sem=flux_sem.at[1, n],
            device_id=dest,
            device_id_type=MESH,
        )

    sends = (exists(0, 1), exists(0, -1), exists(1, 0), exists(-1, 0))
    receives = (exists(0, -1), exists(0, 1), exists(-1, 0), exists(1, 0))
    for n in range(4):

        @pl.when(sends[n])
        def _():
            flux_copy(n).start()

    lane = iota((ROWS, LANES), 1)

    def pack_rows(n, carry):
        span = pl.ds(pl.multiple_of(n * 8, 8), 8)
        rows_send[0, span, :] = cells[pl.ds(n * (8 * ROWS) + (ROWS - 1), 8, stride=ROWS), :]
        rows_send[1, span, :] = cells[pl.ds(n * (8 * ROWS) + HALF * ROWS, 8, stride=ROWS), :]
        return carry

    lax.fori_loop(0, HALF // 8, pack_rows, 0)

    def edge_lanes(direction, last):
        base = direction * PER_DIR
        tile = zero
        for j in range(NFREQ):
            value = cells[pl.ds(pl.multiple_of(base + j * ROWS, ROWS), ROWS), :]
            tile = jnp.where(lane == j, pltpu.roll(value, (j + 1 if last else j) % LANES, 1) if (last or j) else value, tile)
        return tile

    def pack_cols(n, carry):
        group, part = n // 6, lax.rem(n, 6)
        eastward = jnp.where(n < QUARTER, n, n + 2 * QUARTER)
        shift = part * NFREQ
        keep = part > 0
        cols_send[0, group] = jnp.where(keep, cols_send[0, group], zero) + pltpu.roll(edge_lanes(eastward, True), shift, 1)
        cols_send[1, group] = jnp.where(keep, cols_send[1, group], zero) + pltpu.roll(
            edge_lanes(n + QUARTER, False), shift, 1
        )
        return carry

    cols_send[...] = jnp.zeros_like(cols_send)
    lax.fori_loop(0, 2 * QUARTER, pack_cols, 0)

    def halo_copy(n):
        source = cols_send.at[n] if n < 2 else rows_send.at[n - 2]
        target = cols_out.at[n] if n < 2 else rows_out.at[n - 2]
        dest = (device(0, 1), device(0, -1), device(1, 0), device(-1, 0))[n]
        return pltpu.make_async_remote_copy(
            src_ref=source,
            dst_ref=target,
            send_sem=halo_sem.at[0, n],
            recv_sem=halo_sem.at[1, n],
            device_id=dest,
            device_id_type=MESH,
        )

    def halo_fill(n):
        source = cols_send.at[n] if n < 2 else rows_send.at[n - 2]
        target = cols_out.at[n] if n < 2 else rows_out.at[n - 2]
        return pltpu.make_async_copy(source, target, local_sem.at[n])

    for n in range(4):

        @pl.when(sends[n])
        def _():
            halo_copy(n).start()

        @pl.when(jnp.logical_not(receives[n]))
        def _():
            halo_fill(n).start()

    for n in range(2):

        @pl.when(from_side[n])
        def _():
            band_copy(n).wait_recv()

    def window_rows(first):
        return jnp.concatenate([window[t, pl.ds(first, SLOTS, stride=SLOTS), :] for t in range(2)], axis=1)

    wide = (2 * LANES, 2 * LANES)
    wave_masks = [window_rows(12), window_rows(13)]
    spread = (iota(wide, 0) == (2 * iota(wide, 1)) // 3).astype(jnp.bfloat16)
    masks = jnp.dot(
        jnp.concatenate(wave_masks, axis=0).astype(jnp.bfloat16), spread, preferred_element_type=jnp.float32
    )
    ocean_mask = [masks[:SLOTS], masks[:SLOTS], masks[SLOTS:]]
    surface = [window_rows(c) * ocean_mask[c] for c in range(3)]
    eastward = [window_rows(3 + c) * ocean_mask[c] for c in range(3)]
    northward = [window_rows(6 + c) * ocean_mask[c] for c in range(3)]
    bottom = [window_rows(9 + c) for c in range(3)]

    east_y, north_y = along_y(eastward), along_y(northward)
    vorticity = [along_x(northward[c]) - east_y[c] for c in range(3)]
    divergence = [along_x(eastward[c]) + north_y[c] for c in range(3)]
    coarse = []
    for field in (vorticity, divergence):
        coarse.append((2.0 * field[0] + field[1])[:8])
        coarse.append((field[1] + 2.0 * field[2])[:8])
    narrow = (2 * LANES, LANES)
    fine, wave = iota(narrow, 0), iota(narrow, 1) + MARGIN_W
    group = 3 * (wave // 2)
    ends = jnp.where(wave % 2 == 0, group, group + 2)
    weights = jnp.where(fine == ends, 2.0, jnp.where(fine == group + 1, 1.0, 0.0)).astype(jnp.bfloat16)
    coarse = exact_dot(jnp.concatenate(coarse, axis=0), weights) * (1.0 / 9.0)
    for n in range(2):
        for c in range(2):
            place = pl.ds(ROWS * n + c, 8, stride=2)
            fields_out[place, :] = TURN_GAIN * jnp.tanh(coarse[16 * n + 8 * c : 16 * n + 8 * c + 8])

    center = [ocean_shift(wave_masks[c], -MARGIN_W)[:, :LANES] for c in range(2)]
    west_mask = [ocean_shift(wave_masks[c], 1 - MARGIN_W)[:, :LANES] for c in range(2)]
    east_mask = [ocean_shift(wave_masks[c], -1 - MARGIN_W)[:, :LANES] for c in range(2)]
    south_mask = [pltpu.roll(center[1], 1, 0), center[0]]
    north_mask = [center[1], pltpu.roll(center[0], SLOTS - 1, 0)]
    for c in range(2):
        fields_out[pl.ds(2 * ROWS + c, 8, stride=2), :] = center[c][:8]
        for n, other in enumerate((west_mask, east_mask, south_mask, north_mask)):
            fields_out[pl.ds((3 + n) * ROWS + c, 8, stride=2), :] = (center[c] * other[c])[:8]

    def field(n):
        return fields_out[ROWS * n : ROWS * (n + 1), :]

    turning = field(0)
    turn_abs = jnp.abs(turning)
    wave_mask = field(2)
    scale = 0.25 / (NDIR * NFREQ)
    base, along, across = plain[0] * scale, plain[1] * 0.5, plain[2] * 0.5
    turn_c, turn_s = math.cos(2.0 * STEP_ANGLE), math.sin(2.0 * STEP_ANGLE)
    signed = jnp.where(turning > 0.0, turn_s, -turn_s)
    along_turn = along * turn_c - across * signed
    across_turn = across * turn_c + along * signed
    stay = 1.0 - turn_abs
    along = stay * along + turn_abs * along_turn
    across = stay * across + turn_abs * across_turn
    local = [base + along, across, base - along]
    local = [local[s] - ((fluxes[0][s] + fluxes[1][s]) + (fluxes[2][s] + fluxes[3][s])) for s in range(3)]

    for n in range(4):

        @pl.when(receives[n])
        def _():
            flux_copy(n).wait_recv()

    row = iota((ROWS, LANES), 0)
    for s in range(3):
        from_west = jnp.where(lane == 0, pltpu.roll(flux_cols[0, s], 1, 1), pltpu.roll(fluxes[0][s], 1, 1))
        from_east = jnp.where(
            lane == LANES - 1, pltpu.roll(flux_cols[1, s], LANES - 1, 1), pltpu.roll(fluxes[1][s], LANES - 1, 1)
        )
        from_south = jnp.where(row == 0, flux_rows[0, s, 7:8, :], pltpu.roll(fluxes[2][s], 1, 0))
        from_north = jnp.where(row == ROWS - 1, flux_rows[1, s, 0:1, :], pltpu.roll(fluxes[3][s], ROWS - 1, 0))
        stress[0, s, 0:ROWS, :] = (
            wave_mask * local[s]
            + field(3) * from_west
            + field(4) * from_east
            + field(5) * from_south
            + field(6) * from_north
        )

    def stress_copy(n):
        dy, dx = AROUND[n]
        source = pl.ds({0: 0, 1: 8, -1: 0}[dy], 16 if dy == 0 else 8)
        target = pl.ds({0: 0, 1: 24, -1: 16}[dy], 16 if dy == 0 else 8)
        return pltpu.make_async_remote_copy(
            src_ref=stress.at[0, :, source, :],
            dst_ref=stress.at[{0: 0, 1: 2, -1: 1}[dx], :, target, :],
            send_sem=stress_sem.at[0, n],
            recv_sem=stress_sem.at[1, n],
            device_id=device(dy, dx),
            device_id_type=MESH,
        )

    for n, (dy, dx) in enumerate(AROUND):

        @pl.when(exists(dy, dx))
        def _():
            stress_copy(n).start()

    safe = [jnp.where(bottom[c] > 0.0, bottom[c], 1.0) for c in range(3)]
    inverse = [-STRESS_GAIN / safe[c] for c in range(3)]

    def raise_surface(surface, eastward, northward):
        flow_y = along_y([bottom[c] * northward[c] for c in range(3)])
        return [
            (surface[c] - GRAVITY_STEP * (along_x(bottom[c] * eastward[c]) + flow_y[c])) * ocean_mask[c]
            for c in range(3)
        ]

    def push(surface, eastward, northward):
        slope = along_y(surface)
        new_east = [
            eastward[c] + GRAVITY_STEP * (CORIOLIS_STEP * northward[c] - along_x(surface[c])) for c in range(3)
        ]
        new_north = [northward[c] + GRAVITY_STEP * (-CORIOLIS_STEP * eastward[c] - slope[c]) for c in range(3)]
        return new_east, new_north

    surface = raise_surface(surface, eastward, northward)
    pushed = push(surface, eastward, northward)
    wave_lane, fine = iota(wide, 0), iota(wide, 1)
    wave_lane = jnp.where(
        wave_lane < LANES,
        wave_lane + MARGIN_W,
        jnp.where(wave_lane < LANES + 64, wave_lane + MARGIN_W, wave_lane - 2 * LANES + MARGIN_W),
    )
    first = 2 * (fine // 3)
    part = fine % 3
    hits = jnp.where(wave_lane == first, 1.0, 0.0) * jnp.where(part == 0, 1.0, jnp.where(part == 1, 0.5, 0.0)) + jnp.where(
        wave_lane == first + 1, 1.0, 0.0
    ) * jnp.where(part == 2, 1.0, jnp.where(part == 1, 0.5, 0.0))
    prolong = hits.astype(jnp.bfloat16)

    for n, (dy, dx) in enumerate(AROUND):

        @pl.when(exists(-dy, -dx))
        def _():
            stress_copy(n).wait_recv()

    side_lane = iota((SLOTS, LANES), 1)
    pieces = []
    for s in range(3):
        for c in range(2):
            own, right, left = [stress[n, s, pl.ds(c, SLOTS, stride=2), :] for n in range(3)]
            pieces.append(jnp.concatenate([own, jnp.where(side_lane < 64, right, left)], axis=1))
    spread_stress = exact_dot(jnp.concatenate(pieces, axis=0), prolong)
    tensor = []
    for s in range(3):
        low = spread_stress[2 * SLOTS * s : 2 * SLOTS * s + SLOTS]
        high = spread_stress[2 * SLOTS * s + SLOTS : 2 * SLOTS * (s + 1)]
        tensor.append([low, 0.5 * low + 0.5 * high, high])
    cross_y, normal_y = along_y(tensor[1]), along_y(tensor[2])
    force_x = [inverse[c] * (along_x(tensor[0][c]) + cross_y[c]) for c in range(3)]
    force_y = [inverse[c] * (along_x(tensor[1][c]) + normal_y[c]) for c in range(3)]

    for step in range(ITERS):
        if step > 0:
            surface = raise_surface(surface, eastward, northward)
            pushed = push(surface, eastward, northward)
        eastward = [(pushed[0][c] + force_x[c]) * ocean_mask[c] for c in range(3)]
        northward = [(pushed[1][c] + force_y[c]) * ocean_mask[c] for c in range(3)]

    is_even = lax.rem(x, 2) == 0
    for f, values in enumerate((surface, eastward, northward)):
        for c in range(3):
            own = values[c][:8]
            placed = jnp.where(is_even, ocean_shift(own, -MARGIN_O), ocean_shift(own, 64 - MARGIN_O))
            for t in range(2):
                result[t, 8 * (3 * f + c) : 8 * (3 * f + c) + 8, :] = placed[:, LANES * t : LANES * (t + 1)]
    for dest in range(PEERS):
        for t in range(2):
            result_send[dest, t, 0:8, :] = result[t, pl.ds(dest, 8, stride=8), :]
            result_send[dest, t, 8:9, :] = result[t, 64 + dest : 65 + dest, :]

    def result_copy(step):
        dest = peer(step)
        return pltpu.make_async_remote_copy(
            src_ref=result_send.at[dest[2]],
            dst_ref=result_land.at[x],
            send_sem=result_sem.at[0, step],
            recv_sem=result_sem.at[1, step],
            device_id=dest,
            device_id_type=MESH,
        )

    for step in range(1, PEERS):
        result_copy(step).start()
    result_land[x] = result_send[x]
    for step in range(1, PEERS):
        result_copy(step).wait_recv()
    low_half = iota((SLOTS, LANES), 1) < 64
    for q in range(PEERS // 2):
        left, right = 2 * q, 2 * q + 1
        tiles = (
            result_land[left, 0],
            jnp.where(low_half, result_land[left, 1], result_land[right, 0]),
            result_land[right, 1],
        )
        for t in range(3):
            lanes = pl.ds((3 * q + t) * LANES, LANES)
            for f in range(3):
                ocean_out[f, :, lanes] = tiles[t][3 * f : 3 * f + 3]

    for step in range(1, PEERS):
        pack_copy(step).wait_send()
        result_copy(step).wait_send()
    for n in range(2):

        @pl.when(vertical[n])
        def _():
            band_copy(n).wait_send()

    for n, (dy, dx) in enumerate(AROUND):

        @pl.when(exists(dy, dx))
        def _():
            stress_copy(n).wait_send()

    for n in range(4):

        @pl.when(sends[n])
        def _():
            flux_copy(n).wait_send()
            halo_copy(n).wait_send()

        @pl.when(receives[n])
        def _():
            halo_copy(n).wait_recv()

        @pl.when(jnp.logical_not(receives[n]))
        def _():
            halo_fill(n).wait()


def wave_kernel(spectrum, fields, rows_in, cols_in, out, cells, updated, rows, cols, load_sem, store_sem, halo_sem):
    def span_of(direction):
        return pl.ds(pl.multiple_of(direction * PER_DIR, PER_DIR), PER_DIR)

    def load(direction):
        span = span_of(direction)
        return pltpu.make_async_copy(spectrum.at[span], cells.at[span], load_sem.at[direction])

    def store(direction):
        span = span_of(direction)
        return pltpu.make_async_copy(updated.at[span], out.at[span], store_sem.at[direction])

    halos = [pltpu.make_async_copy(rows_in, rows, halo_sem.at[0]), pltpu.make_async_copy(cols_in, cols, halo_sem.at[1])]
    for q in range(4):
        load(q * QUARTER + QUARTER - 1).start()
    for q in range(4):
        load(q * QUARTER).start()
    for copy in halos:
        copy.start()

    def start_load(i, carry):
        for q in range(4):
            load(q * QUARTER + i).start()
        return carry

    lax.fori_loop(1, QUARTER - 1, start_load, 0)

    def field(n):
        return fields[ROWS * n : ROWS * (n + 1), :]

    turning, shifting, mask = field(0), field(1), field(2)
    turn_left = turning > 0.0
    shift_up = shifting > 0.0
    turn_part = mask * jnp.abs(turning)
    stay = mask - turn_part
    shift_part = mask * shifting
    sides = [field(3), field(4), field(5), field(6)]
    lane = iota((ROWS, LANES), 1)
    row = iota((ROWS, LANES), 0)

    for q in range(4):
        load(q * QUARTER + QUARTER - 1).wait()
    for q in range(4):
        load(q * QUARTER).wait()
    for copy in halos:
        copy.wait()

    def cell(direction, j):
        return cells[pl.ds(pl.multiple_of(direction * PER_DIR + j * ROWS, ROWS), ROWS), :]

    def one_direction(i, q, cosine, sine):
        direction = q * QUARTER + i
        before = jnp.where(direction == 0, NDIR - 1, direction - 1)
        after = jnp.where(direction == NDIR - 1, 0, direction + 1)
        from_west, from_south = q in (0, 3), q in (0, 1)
        speed_x, speed_y = (cosine, sine) if q % 2 == 0 else (sine, cosine)
        coefficient_x = sides[0 if from_west else 1] * speed_x
        coefficient_y = sides[2 if from_south else 3] * speed_y
        leave = mask * (speed_x + speed_y)
        place = (i if q == 0 else QUARTER + i) if from_west else (i if q == 1 else QUARTER + i)
        side = 0 if from_west else 1
        columns = pltpu.roll(cols[side, place // 6], lax.rem(LANES - lax.rem(place, 6) * NFREQ, LANES), 1)
        first_row = (direction if from_south else direction - 2 * QUARTER) * NFREQ
        value = cell(direction, 0)
        last_face = None
        for j in range(NFREQ):
            if from_west:
                beside = pltpu.roll(value, 1, 1)
                rim = pltpu.roll(columns, LANES - j, 1) if j else columns
                beside = jnp.where(lane == 0, rim, beside)
            else:
                beside = pltpu.roll(value, LANES - 1, 1)
                rim = pltpu.roll(columns, LANES - 1 - j, 1)
                beside = jnp.where(lane == LANES - 1, rim, beside)
            rim_row = rows[0 if from_south else 1, pl.ds(first_row + j, 1), :]
            if from_south:
                along = jnp.where(row == 0, rim_row, pltpu.roll(value, 1, 0))
            else:
                along = jnp.where(row == ROWS - 1, rim_row, pltpu.roll(value, ROWS - 1, 0))
            moved = coefficient_x * beside + coefficient_y * along - leave * value
            total = stay * value + SPEEDS[j] * moved
            total = total + turn_part * jnp.where(turn_left, cell(before, j), cell(after, j))
            if last_face is not None:
                total = total + last_face
            if j < NFREQ - 1:
                following = cell(direction, j + 1)
                last_face = shift_part * jnp.where(shift_up, value, following)
                total = total - last_face
                value = following
            updated[pl.ds(pl.multiple_of(direction * PER_DIR + j * ROWS, ROWS), ROWS), :] = total

    def one_step(i, angle):
        @pl.when(i < QUARTER - 2)
        def _():
            for q in range(4):
                load(q * QUARTER + i + 1).wait()

        for q in range(4):
            one_direction(i, q, *angle)
            store(q * QUARTER + i).start()
        return next_angle(*angle)

    lax.fori_loop(0, QUARTER, one_step, first_angle())

    def finish(direction, carry):
        store(direction).wait()
        return carry

    lax.fori_loop(0, NDIR, finish, 0)


def shards(mesh_shape, spectrum, sea_mask, ocean_state, depth):
    groups_y = mesh_shape["gy"]
    groups = groups_y * mesh_shape["sec"]
    cells = spectrum.reshape(CELLS, LANES)
    vmem = pl.BlockSpec(memory_space=pltpu.VMEM)
    anywhere = pl.BlockSpec(memory_space=pl.ANY)
    f32 = jnp.float32
    dma = pltpu.SemaphoreType.DMA
    ocean_out, fields, rows, cols = pl.pallas_call(
        functools.partial(coupled_kernel, groups_y, groups),
        out_shape=(
            jax.ShapeDtypeStruct(ocean_state.shape, f32),
            jax.ShapeDtypeStruct((7 * ROWS, LANES), f32),
            jax.ShapeDtypeStruct((2, HALF, LANES), f32),
            jax.ShapeDtypeStruct((2, 3, ROWS, LANES), f32),
        ),
        in_specs=[anywhere, vmem, vmem, vmem],
        out_specs=(vmem, vmem, anywhere, anywhere),
        scratch_shapes=[
            pltpu.VMEM((CELLS, LANES), f32),
            pltpu.VMEM((SLOTS, 1792), f32),
            pltpu.VMEM((SLOTS, 1280), f32),
            pltpu.VMEM((PEERS, 2, SLOTS, LANES), f32),
            pltpu.VMEM((2, SLOTS * SLOTS, LANES), f32),
            pltpu.VMEM((4, 3, ROWS, LANES), f32),
            pltpu.VMEM((2, 3, ROWS, LANES), f32),
            pltpu.VMEM((2, 3, 8, LANES), f32),
            pltpu.VMEM((3, 3, 32, LANES), f32),
            pltpu.VMEM((2, 72, LANES), f32),
            pltpu.VMEM((PEERS, 2, SLOTS, LANES), f32),
            pltpu.VMEM((PEERS, 2, SLOTS, LANES), f32),
            pltpu.VMEM((2, HALF, LANES), f32),
            pltpu.VMEM((2, 3, ROWS, LANES), f32),
            dma((NDIR,)),
            dma((2, PEERS)),
            dma((2, 2)),
            dma((2, 4)),
            dma((2, 8)),
            dma((2, PEERS)),
            dma((2, 4)),
            dma((4,)),
        ],
        compiler_params=pltpu.CompilerParams(
            collective_id=0, has_side_effects=True, vmem_limit_bytes=32 * 1024 * 1024
        ),
        name="coupled",
    )(cells, sea_mask, ocean_state, depth)
    spectrum_out = pl.pallas_call(
        wave_kernel,
        out_shape=jax.ShapeDtypeStruct((CELLS, LANES), f32),
        in_specs=[anywhere, vmem, anywhere, anywhere],
        out_specs=anywhere,
        scratch_shapes=[
            pltpu.VMEM((CELLS, LANES), f32),
            pltpu.VMEM((CELLS, LANES), f32),
            pltpu.VMEM((2, HALF, LANES), f32),
            pltpu.VMEM((2, 3, ROWS, LANES), f32),
            dma((NDIR,)),
            dma((NDIR,)),
            dma((2,)),
        ],
        compiler_params=pltpu.CompilerParams(vmem_limit_bytes=32 * 1024 * 1024),
        name="wave",
    )(cells, fields, rows, cols)
    return (spectrum_out.reshape(spectrum.shape), ocean_out)


def solution(mesh):
    return jax.shard_map(
        functools.partial(shards, dict(mesh.shape)),
        mesh=mesh,
        in_specs=(
            P(None, None, ("sec", "gy"), "gx"),
            P(("sec", "gy", "gx"), None),
            P(None, ("sec", "gy", "gx"), None),
            P(("sec", "gy", "gx"), None),
        ),
        out_specs=(P(None, None, ("sec", "gy"), "gx"), P(None, ("sec", "gy", "gx"), None)),
        check_vma=False,
    )
```

```python
import functools
import math

import jax
import jax.numpy as jnp
from jax import lax
from jax.experimental import pallas as pl
from jax.experimental.pallas import tpu as pltpu
from jax.sharding import PartitionSpec as P

ITERS = 4
GRAVITY_STEP = 0.3
CORIOLIS_STEP = 0.2
STRESS_GAIN = 2.0
TURN_GAIN = 0.2
SPEED_BASE = 0.35
SPEED_RATIO = 0.9

NDIR = 36
NFREQ = 20
ROWS = 16
LANES = 128
CELLS = NDIR * NFREQ * ROWS
PER_DIR = NFREQ * ROWS
QUARTER = NDIR // 4
PITCH = 24
VMEM_LIMIT = 60 * 1024 * 1024
HALF = NDIR // 2 * NFREQ
PEERS = 8
SLOTS = 16
MARGIN_O = 24
MARGIN_W = 16
SPEEDS = [SPEED_BASE * SPEED_RATIO**j for j in range(NFREQ)]
STEP_ANGLE = 2.0 * math.pi / NDIR
MESH = pl.DeviceIdType.MESH
AROUND = [(1, 0), (-1, 0), (0, 1), (0, -1), (1, 1), (1, -1), (-1, 1), (-1, -1)]


def iota(shape, dim):
    return lax.broadcasted_iota(jnp.int32, shape, dim)


def next_angle(cosine, sine):
    turn_c, turn_s = math.cos(STEP_ANGLE), math.sin(STEP_ANGLE)
    return cosine * turn_c - sine * turn_s, sine * turn_c + cosine * turn_s


def first_angle():
    return jnp.float32(math.cos(0.5 * STEP_ANGLE)), jnp.float32(math.sin(0.5 * STEP_ANGLE))


def exact_dot(values, weights):
    rows = values.shape[0]
    high = values.astype(jnp.bfloat16)
    rest = values - high.astype(jnp.float32)
    middle = rest.astype(jnp.bfloat16)
    low = (rest - middle.astype(jnp.float32)).astype(jnp.bfloat16)
    stacked = jnp.concatenate([high, middle, low], axis=0)
    product = jnp.dot(stacked, weights, preferred_element_type=jnp.float32)
    return product[:rows] + product[rows : 2 * rows] + product[2 * rows :]


def ocean_shift(values, amount):
    return pltpu.roll(values, amount % values.shape[1], 1)


def along_x(values):
    return (ocean_shift(values, -1) - ocean_shift(values, 1)) * 0.5


def along_y(classes):
    above = [classes[1], classes[2], pltpu.roll(classes[0], SLOTS - 1, 0)]
    below = [pltpu.roll(classes[2], 1, 0), classes[0], classes[1]]
    return [(above[c] - below[c]) * 0.5 for c in range(3)]


def coupled_kernel(
    groups_y,
    groups,
    spectrum,
    sea_mask,
    ocean_state,
    depth,
    ocean_out,
    fields_out,
    rows_out,
    cols_out,
    cells,
    raw,
    raw_mask,
    pack,
    window,
    flux,
    flux_cols,
    flux_rows,
    stress,
    result,
    result_send,
    result_land,
    rows_send,
    cols_send,
    load_sem,
    pack_sem,
    band_sem,
    flux_sem,
    stress_sem,
    result_sem,
    halo_sem,
    local_sem,
):
    x = lax.axis_index("gx")
    y = lax.axis_index("sec") * groups_y + lax.axis_index("gy")

    def exists(dy, dx):
        checks = []
        if dy > 0:
            checks.append(y < groups - 1)
        if dy < 0:
            checks.append(y > 0)
        if dx > 0:
            checks.append(x < PEERS - 1)
        if dx < 0:
            checks.append(x > 0)
        answer = checks[0]
        for check in checks[1:]:
            answer = jnp.logical_and(answer, check)
        return answer

    def device(dy, dx):
        row = y + dy
        return (row // groups_y, lax.rem(row, groups_y), x + dx)

    def peer(step):
        return (lax.axis_index("sec"), lax.axis_index("gy"), lax.rem(x + step, PEERS))

    def load(direction):
        span = pl.ds(pl.multiple_of(direction * PER_DIR, PER_DIR), PER_DIR)
        return pltpu.make_async_copy(spectrum.at[span], cells.at[span], load_sem.at[direction])

    def start_load(i, carry):
        for q in range(4):
            load(q * QUARTER + i).start()
        return carry

    lax.fori_loop(0, QUARTER, start_load, 0)

    barrier = pltpu.get_barrier_semaphore()
    for step in range(1, PEERS):
        pl.semaphore_signal(barrier, inc=1, device_id=peer(step), device_id_type=MESH)
    greeted = PEERS - 1
    for dy, dx in AROUND:
        if dy != 0:
            here = exists(dy, dx)

            @pl.when(here)
            def _():
                pl.semaphore_signal(barrier, inc=1, device_id=device(dy, dx), device_id_type=MESH)

            greeted = greeted + here.astype(jnp.int32)

    raw[...] = jnp.zeros_like(raw)
    raw_mask[...] = jnp.zeros_like(raw_mask)
    width = ocean_state.shape[2]
    for f in range(3):
        raw[3 * f : 3 * f + 3, :width] = ocean_state[f]
    raw[9:12, :width] = depth[...]
    raw_mask[12:14, : sea_mask.shape[1]] = sea_mask[...].astype(jnp.float32)
    even = ocean_shift(raw[...], MARGIN_O)
    odd = ocean_shift(raw[...], MARGIN_O - 64)
    mask_rows = ocean_shift(raw_mask[...], MARGIN_W)
    is_ocean = iota((SLOTS, LANES), 0) < 12
    for dest in range(PEERS):
        source = odd if dest % 2 else even
        origin = 384 * (dest // 2) + (128 if dest % 2 else 0)
        for tile in range(2):
            pack[dest, tile] = jnp.where(
                is_ocean,
                source[:, origin + LANES * tile : origin + LANES * (tile + 1)],
                mask_rows[:, LANES * (dest + tile) : LANES * (dest + tile + 1)],
            )

    slab = jnp.zeros((2, 2 * SLOTS, LANES), jnp.float32)
    window[:, 11 * SLOTS : 13 * SLOTS, :] = slab
    edge = jnp.zeros((2, 3 * SLOTS, LANES), jnp.float32)

    @pl.when(y == 0)
    def _():
        window[:, 13 * SLOTS : 16 * SLOTS, :] = edge
        flux_rows[0] = jnp.zeros((3, 8, LANES), jnp.float32)
        stress[:, :, 24:32, :] = jnp.zeros((3, 3, 8, LANES), jnp.float32)

    @pl.when(y == groups - 1)
    def _():
        window[:, 8 * SLOTS : 11 * SLOTS, :] = edge
        flux_rows[1] = jnp.zeros((3, 8, LANES), jnp.float32)
        stress[:, :, 16:24, :] = jnp.zeros((3, 3, 8, LANES), jnp.float32)

    @pl.when(x == 0)
    def _():
        flux_cols[0] = jnp.zeros((3, ROWS, LANES), jnp.float32)
        stress[2] = jnp.zeros((3, 32, LANES), jnp.float32)

    @pl.when(x == PEERS - 1)
    def _():
        flux_cols[1] = jnp.zeros((3, ROWS, LANES), jnp.float32)
        stress[1] = jnp.zeros((3, 32, LANES), jnp.float32)

    mine = pl.ds(pl.multiple_of(x * SLOTS, SLOTS), SLOTS)

    def pack_copy(step):
        dest = peer(step)
        return pltpu.make_async_remote_copy(
            src_ref=pack.at[dest[2]],
            dst_ref=window.at[:, mine, :],
            send_sem=pack_sem.at[0, step],
            recv_sem=pack_sem.at[1, step],
            device_id=dest,
            device_id_type=MESH,
        )

    pl.semaphore_wait(barrier, greeted)
    for step in range(1, PEERS):
        pack_copy(step).start()
    window[:, mine, :] = pack[x]

    def sums(direction):
        base = direction * PER_DIR
        total = weighted = None
        for j in range(NFREQ):
            value = cells[pl.ds(pl.multiple_of(base + j * ROWS, ROWS), ROWS), :]
            total = value if j == 0 else total + value
            scaled = value * SPEEDS[j]
            weighted = scaled if j == 0 else weighted + scaled
        return total, weighted

    def gather(i, carry):
        (cosine, sine), plain, fluxes = carry
        for q in range(4):
            load(q * QUARTER + i).wait()
        scale = 0.5 / (NDIR * NFREQ)
        cc, cs, ss = cosine * cosine * scale, cosine * sine * scale, sine * sine * scale
        totals, weighted = zip(*[sums(q * QUARTER + i) for q in range(4)])
        pair = (totals[0] + totals[2]) - (totals[1] + totals[3])
        plain = (
            plain[0] + ((totals[0] + totals[2]) + (totals[1] + totals[3])),
            plain[1] + (cc - ss) * pair,
            plain[2] + (2.0 * cs) * pair,
        )
        straight, crossed = (cc, cs, ss), (ss, -cs, cc)
        west, east, south, north = fluxes
        west = tuple(
            west[s] + (cosine * straight[s]) * weighted[0] + (sine * crossed[s]) * weighted[3] for s in range(3)
        )
        east = tuple(
            east[s] + (cosine * straight[s]) * weighted[2] + (sine * crossed[s]) * weighted[1] for s in range(3)
        )
        south = tuple(
            south[s] + (sine * straight[s]) * weighted[0] + (cosine * crossed[s]) * weighted[1] for s in range(3)
        )
        north = tuple(
            north[s] + (sine * straight[s]) * weighted[2] + (cosine * crossed[s]) * weighted[3] for s in range(3)
        )
        return next_angle(cosine, sine), plain, (west, east, south, north)

    zero = jnp.zeros((ROWS, LANES), jnp.float32)
    triple = (zero, zero, zero)
    state = (first_angle(), triple, (triple, triple, triple, triple))
    state = lax.fori_loop(0, QUARTER // 2, gather, state)

    for step in range(1, PEERS):
        pack_copy(step).wait_recv()

    def band_copy(n):
        dy = 1 if n == 0 else -1
        source = pl.ds((5 if n == 0 else 0) * SLOTS, 3 * SLOTS)
        target = pl.ds((13 if n == 0 else 8) * SLOTS, 3 * SLOTS)
        return pltpu.make_async_remote_copy(
            src_ref=window.at[:, source, :],
            dst_ref=window.at[:, target, :],
            send_sem=band_sem.at[0, n],
            recv_sem=band_sem.at[1, n],
            device_id=device(dy, 0),
            device_id_type=MESH,
        )

    vertical = (exists(1, 0), exists(-1, 0))
    from_side = (exists(-1, 0), exists(1, 0))
    for n in range(2):

        @pl.when(vertical[n])
        def _():
            band_copy(n).start()

    _, plain, fluxes = lax.fori_loop(QUARTER // 2, QUARTER, gather, state)
    for side in range(4):
        for s in range(3):
            flux[side, s] = fluxes[side][s]

    def flux_copy(n):
        if n < 2:
            source, target, dest = flux.at[n], flux_cols.at[n], device(0, 1 if n == 0 else -1)
        else:
            span = pl.ds(8 if n == 2 else 0, 8)
            source, target, dest = flux.at[n, :, span, :], flux_rows.at[n - 2], device(1 if n == 2 else -1, 0)
        return pltpu.make_async_remote_copy(
            src_ref=source,
            dst_ref=target,
            send_sem=flux_sem.at[0, n],
            recv_sem=flux_sem.at[1, n],
            device_id=dest,
            device_id_type=MESH,
        )

    sends = (exists(0, 1), exists(0, -1), exists(1, 0), exists(-1, 0))
    receives = (exists(0, -1), exists(0, 1), exists(-1, 0), exists(1, 0))
    for n in range(4):

        @pl.when(sends[n])
        def _():
            flux_copy(n).start()

    lane = iota((ROWS, LANES), 1)

    def pack_rows(n, carry):
        span = pl.ds(pl.multiple_of(n * 8, 8), 8)
        rows_send[0, span, :] = cells[pl.ds(n * (8 * ROWS) + (ROWS - 1), 8, stride=ROWS), :]
        rows_send[1, span, :] = cells[pl.ds(n * (8 * ROWS) + HALF * ROWS, 8, stride=ROWS), :]
        return carry

    lax.fori_loop(0, HALF // 8, pack_rows, 0)

    def edge_lanes(direction, last):
        base = direction * PER_DIR
        tile = zero
        for j in range(NFREQ):
            value = cells[pl.ds(pl.multiple_of(base + j * ROWS, ROWS), ROWS), :]
            tile = jnp.where(lane == 2 * j + last, pltpu.roll(value, 2 * j + 2 * last, 1) if (last or j) else value, tile)
        return tile

    def pack_cols(n, carry):
        group, part = n // 3, lax.rem(n, 3)
        eastward = jnp.where(n < QUARTER, n, n + 2 * QUARTER)
        shift = part * (2 * NFREQ)
        keep = part > 0
        cols_send[0, group] = jnp.where(keep, cols_send[0, group], zero) + pltpu.roll(edge_lanes(eastward, 1), shift, 1)
        cols_send[1, group] = jnp.where(keep, cols_send[1, group], zero) + pltpu.roll(
            edge_lanes(n + QUARTER, 0), shift, 1
        )
        return carry

    cols_send[...] = jnp.zeros_like(cols_send)
    lax.fori_loop(0, 2 * QUARTER, pack_cols, 0)

    def halo_copy(n):
        source = cols_send.at[n] if n < 2 else rows_send.at[n - 2]
        target = cols_out.at[n] if n < 2 else rows_out.at[n - 2]
        dest = (device(0, 1), device(0, -1), device(1, 0), device(-1, 0))[n]
        return pltpu.make_async_remote_copy(
            src_ref=source,
            dst_ref=target,
            send_sem=halo_sem.at[0, n],
            recv_sem=halo_sem.at[1, n],
            device_id=dest,
            device_id_type=MESH,
        )

    def halo_fill(n):
        source = cols_send.at[n] if n < 2 else rows_send.at[n - 2]
        target = cols_out.at[n] if n < 2 else rows_out.at[n - 2]
        return pltpu.make_async_copy(source, target, local_sem.at[n])

    for n in range(4):

        @pl.when(sends[n])
        def _():
            halo_copy(n).start()

        @pl.when(jnp.logical_not(receives[n]))
        def _():
            halo_fill(n).start()

    for n in range(2):

        @pl.when(from_side[n])
        def _():
            band_copy(n).wait_recv()

    def window_rows(first):
        return jnp.concatenate([window[t, pl.ds(first, SLOTS, stride=SLOTS), :] for t in range(2)], axis=1)

    wide = (2 * LANES, 2 * LANES)
    wave_masks = [window_rows(12), window_rows(13)]
    spread = (iota(wide, 0) == (2 * iota(wide, 1)) // 3).astype(jnp.bfloat16)
    masks = jnp.dot(
        jnp.concatenate(wave_masks, axis=0).astype(jnp.bfloat16), spread, preferred_element_type=jnp.float32
    )
    ocean_mask = [masks[:SLOTS], masks[:SLOTS], masks[SLOTS:]]
    surface = [window_rows(c) * ocean_mask[c] for c in range(3)]
    eastward = [window_rows(3 + c) * ocean_mask[c] for c in range(3)]
    northward = [window_rows(6 + c) * ocean_mask[c] for c in range(3)]
    bottom = [window_rows(9 + c) for c in range(3)]

    east_y, north_y = along_y(eastward), along_y(northward)
    vorticity = [along_x(northward[c]) - east_y[c] for c in range(3)]
    divergence = [along_x(eastward[c]) + north_y[c] for c in range(3)]
    coarse = []
    for field in (vorticity, divergence):
        coarse.append((2.0 * field[0] + field[1])[:8])
        coarse.append((field[1] + 2.0 * field[2])[:8])
    narrow = (2 * LANES, LANES)
    fine, wave = iota(narrow, 0), iota(narrow, 1) + MARGIN_W
    group = 3 * (wave // 2)
    ends = jnp.where(wave % 2 == 0, group, group + 2)
    weights = jnp.where(fine == ends, 2.0, jnp.where(fine == group + 1, 1.0, 0.0)).astype(jnp.bfloat16)
    coarse = exact_dot(jnp.concatenate(coarse, axis=0), weights) * (1.0 / 9.0)
    for n in range(2):
        for c in range(2):
            place = pl.ds(ROWS * n + c, 8, stride=2)
            fields_out[place, :] = TURN_GAIN * jnp.tanh(coarse[16 * n + 8 * c : 16 * n + 8 * c + 8])

    center = [ocean_shift(wave_masks[c], -MARGIN_W)[:, :LANES] for c in range(2)]
    west_mask = [ocean_shift(wave_masks[c], 1 - MARGIN_W)[:, :LANES] for c in range(2)]
    east_mask = [ocean_shift(wave_masks[c], -1 - MARGIN_W)[:, :LANES] for c in range(2)]
    south_mask = [pltpu.roll(center[1], 1, 0), center[0]]
    north_mask = [center[1], pltpu.roll(center[0], SLOTS - 1, 0)]
    for c in range(2):
        fields_out[pl.ds(2 * ROWS + c, 8, stride=2), :] = center[c][:8]
        for n, other in enumerate((west_mask, east_mask, south_mask, north_mask)):
            fields_out[pl.ds((3 + n) * ROWS + c, 8, stride=2), :] = (center[c] * other[c])[:8]

    def field(n):
        return fields_out[ROWS * n : ROWS * (n + 1), :]

    turning = field(0)
    turn_abs = jnp.abs(turning)
    wave_mask = field(2)
    scale = 0.25 / (NDIR * NFREQ)
    base, along, across = plain[0] * scale, plain[1] * 0.5, plain[2] * 0.5
    turn_c, turn_s = math.cos(2.0 * STEP_ANGLE), math.sin(2.0 * STEP_ANGLE)
    signed = jnp.where(turning > 0.0, turn_s, -turn_s)
    along_turn = along * turn_c - across * signed
    across_turn = across * turn_c + along * signed
    stay = 1.0 - turn_abs
    along = stay * along + turn_abs * along_turn
    across = stay * across + turn_abs * across_turn
    local = [base + along, across, base - along]
    local = [local[s] - ((fluxes[0][s] + fluxes[1][s]) + (fluxes[2][s] + fluxes[3][s])) for s in range(3)]

    for n in range(4):

        @pl.when(receives[n])
        def _():
            flux_copy(n).wait_recv()

    row = iota((ROWS, LANES), 0)
    for s in range(3):
        from_west = jnp.where(lane == 0, pltpu.roll(flux_cols[0, s], 1, 1), pltpu.roll(fluxes[0][s], 1, 1))
        from_east = jnp.where(
            lane == LANES - 1, pltpu.roll(flux_cols[1, s], LANES - 1, 1), pltpu.roll(fluxes[1][s], LANES - 1, 1)
        )
        from_south = jnp.where(row == 0, flux_rows[0, s, 7:8, :], pltpu.roll(fluxes[2][s], 1, 0))
        from_north = jnp.where(row == ROWS - 1, flux_rows[1, s, 0:1, :], pltpu.roll(fluxes[3][s], ROWS - 1, 0))
        stress[0, s, 0:ROWS, :] = (
            wave_mask * local[s]
            + field(3) * from_west
            + field(4) * from_east
            + field(5) * from_south
            + field(6) * from_north
        )

    def stress_copy(n):
        dy, dx = AROUND[n]
        source = pl.ds({0: 0, 1: 8, -1: 0}[dy], 16 if dy == 0 else 8)
        target = pl.ds({0: 0, 1: 24, -1: 16}[dy], 16 if dy == 0 else 8)
        return pltpu.make_async_remote_copy(
            src_ref=stress.at[0, :, source, :],
            dst_ref=stress.at[{0: 0, 1: 2, -1: 1}[dx], :, target, :],
            send_sem=stress_sem.at[0, n],
            recv_sem=stress_sem.at[1, n],
            device_id=device(dy, dx),
            device_id_type=MESH,
        )

    for n, (dy, dx) in enumerate(AROUND):

        @pl.when(exists(dy, dx))
        def _():
            stress_copy(n).start()

    safe = [jnp.where(bottom[c] > 0.0, bottom[c], 1.0) for c in range(3)]
    inverse = [-STRESS_GAIN / safe[c] for c in range(3)]

    def raise_surface(surface, eastward, northward):
        flow_y = along_y([bottom[c] * northward[c] for c in range(3)])
        return [
            (surface[c] - GRAVITY_STEP * (along_x(bottom[c] * eastward[c]) + flow_y[c])) * ocean_mask[c]
            for c in range(3)
        ]

    def push(surface, eastward, northward):
        slope = along_y(surface)
        new_east = [
            eastward[c] + GRAVITY_STEP * (CORIOLIS_STEP * northward[c] - along_x(surface[c])) for c in range(3)
        ]
        new_north = [northward[c] + GRAVITY_STEP * (-CORIOLIS_STEP * eastward[c] - slope[c]) for c in range(3)]
        return new_east, new_north

    surface = raise_surface(surface, eastward, northward)
    pushed = push(surface, eastward, northward)
    wave_lane, fine = iota(wide, 0), iota(wide, 1)
    wave_lane = jnp.where(
        wave_lane < LANES,
        wave_lane + MARGIN_W,
        jnp.where(wave_lane < LANES + 64, wave_lane + MARGIN_W, wave_lane - 2 * LANES + MARGIN_W),
    )
    first = 2 * (fine // 3)
    part = fine % 3
    hits = jnp.where(wave_lane == first, 1.0, 0.0) * jnp.where(part == 0, 1.0, jnp.where(part == 1, 0.5, 0.0)) + jnp.where(
        wave_lane == first + 1, 1.0, 0.0
    ) * jnp.where(part == 2, 1.0, jnp.where(part == 1, 0.5, 0.0))
    prolong = hits.astype(jnp.bfloat16)

    for n, (dy, dx) in enumerate(AROUND):

        @pl.when(exists(-dy, -dx))
        def _():
            stress_copy(n).wait_recv()

    side_lane = iota((SLOTS, LANES), 1)
    pieces = []
    for s in range(3):
        for c in range(2):
            own, right, left = [stress[n, s, pl.ds(c, SLOTS, stride=2), :] for n in range(3)]
            pieces.append(jnp.concatenate([own, jnp.where(side_lane < 64, right, left)], axis=1))
    spread_stress = exact_dot(jnp.concatenate(pieces, axis=0), prolong)
    tensor = []
    for s in range(3):
        low = spread_stress[2 * SLOTS * s : 2 * SLOTS * s + SLOTS]
        high = spread_stress[2 * SLOTS * s + SLOTS : 2 * SLOTS * (s + 1)]
        tensor.append([low, 0.5 * low + 0.5 * high, high])
    cross_y, normal_y = along_y(tensor[1]), along_y(tensor[2])
    force_x = [inverse[c] * (along_x(tensor[0][c]) + cross_y[c]) for c in range(3)]
    force_y = [inverse[c] * (along_x(tensor[1][c]) + normal_y[c]) for c in range(3)]

    for step in range(ITERS):
        if step > 0:
            surface = raise_surface(surface, eastward, northward)
            pushed = push(surface, eastward, northward)
        eastward = [(pushed[0][c] + force_x[c]) * ocean_mask[c] for c in range(3)]
        northward = [(pushed[1][c] + force_y[c]) * ocean_mask[c] for c in range(3)]

    is_even = lax.rem(x, 2) == 0
    for f, values in enumerate((surface, eastward, northward)):
        for c in range(3):
            own = values[c][:8]
            placed = jnp.where(is_even, ocean_shift(own, -MARGIN_O), ocean_shift(own, 64 - MARGIN_O))
            for t in range(2):
                result[t, 8 * (3 * f + c) : 8 * (3 * f + c) + 8, :] = placed[:, LANES * t : LANES * (t + 1)]
    for dest in range(PEERS):
        for t in range(2):
            result_send[dest, t, 0:8, :] = result[t, pl.ds(dest, 8, stride=8), :]
            result_send[dest, t, 8:9, :] = result[t, 64 + dest : 65 + dest, :]

    def result_copy(step):
        dest = peer(step)
        return pltpu.make_async_remote_copy(
            src_ref=result_send.at[dest[2]],
            dst_ref=result_land.at[x],
            send_sem=result_sem.at[0, step],
            recv_sem=result_sem.at[1, step],
            device_id=dest,
            device_id_type=MESH,
        )

    for step in range(1, PEERS):
        result_copy(step).start()
    result_land[x] = result_send[x]
    for step in range(1, PEERS):
        result_copy(step).wait_recv()
    low_half = iota((SLOTS, LANES), 1) < 64
    for q in range(PEERS // 2):
        left, right = 2 * q, 2 * q + 1
        tiles = (
            result_land[left, 0],
            jnp.where(low_half, result_land[left, 1], result_land[right, 0]),
            result_land[right, 1],
        )
        for t in range(3):
            lanes = pl.ds((3 * q + t) * LANES, LANES)
            for f in range(3):
                ocean_out[f, :, lanes] = tiles[t][3 * f : 3 * f + 3]

    for step in range(1, PEERS):
        pack_copy(step).wait_send()
        result_copy(step).wait_send()
    for n in range(2):

        @pl.when(vertical[n])
        def _():
            band_copy(n).wait_send()

    for n, (dy, dx) in enumerate(AROUND):

        @pl.when(exists(dy, dx))
        def _():
            stress_copy(n).wait_send()

    for n in range(4):

        @pl.when(sends[n])
        def _():
            flux_copy(n).wait_send()
            halo_copy(n).wait_send()

        @pl.when(receives[n])
        def _():
            halo_copy(n).wait_recv()

        @pl.when(jnp.logical_not(receives[n]))
        def _():
            halo_fill(n).wait()


def wave_kernel(spectrum, fields, rows_in, cols_in, out, cells, updated, beside, rows, cols, load_sem, store_sem, halo_sem):
    def load(direction):
        return pltpu.make_async_copy(
            spectrum.at[pl.ds(direction * NFREQ, NFREQ)],
            cells.at[pl.ds(direction * NFREQ, NFREQ), pl.ds(8, ROWS), :],
            load_sem.at[direction],
        )

    def store(direction):
        span = pl.ds(direction * NFREQ, NFREQ)
        return pltpu.make_async_copy(updated.at[span], out.at[span], store_sem.at[direction])

    halos = [pltpu.make_async_copy(rows_in, rows, halo_sem.at[0]), pltpu.make_async_copy(cols_in, cols, halo_sem.at[1])]
    for copy in halos:
        copy.start()
    for q in range(4):
        load(q * QUARTER + QUARTER - 1).start()
    for q in range(4):
        load(q * QUARTER).start()

    def start_load(i, carry):
        for q in range(4):
            load(q * QUARTER + i).start()
        return carry

    lax.fori_loop(1, QUARTER - 1, start_load, 0)
    flat = cells.reshape((NDIR * NFREQ + 1) * PITCH, LANES)

    def half(n, h):
        return fields[ROWS * n + 8 * h : ROWS * n + 8 * h + 8, :]

    def turn_part(h):
        return half(2, h) * jnp.abs(half(0, h))

    lane = iota((8, LANES), 1)
    for copy in halos:
        copy.wait()

    def place_rows(n, carry):
        span = pl.ds(pl.multiple_of(n * 8, 8), 8)
        flat[pl.ds(n * (8 * PITCH) + 7, 8, stride=PITCH), :] = rows[0, span, :]
        flat[pl.ds(n * (8 * PITCH) + (HALF + 1) * PITCH, 8, stride=PITCH), :] = rows[1, span, :]
        return carry

    lax.fori_loop(0, HALF // 8, place_rows, 0)

    def cell(direction, j, offset):
        return flat[pl.ds(direction * (NFREQ * PITCH) + (j * PITCH + 8 + offset), 8), :]

    odd = lax.rem(lane, 2) == 1

    def rims(i, h):
        columns = []
        for place in (i, QUARTER + i):
            group, part = place // 3, lax.rem(place, 3)
            span = slice(8 * h, 8 * h + 8)
            merged = jnp.where(odd, cols[0, group, span, :], cols[1, group, span, :])
            columns.append(pltpu.roll(merged, lax.rem(LANES - part * (2 * NFREQ), LANES), 1))
        return columns

    def prepare(i, h, j, columns):
        rim = [pltpu.roll(column, LANES - 1 - 2 * j, 1) for column in columns]
        for q in range(4):
            value = cell(q * QUARTER + i, j, 8 * h)
            if q in (0, 3):
                moved = jnp.where(lane == 0, rim[q // 2], pltpu.roll(value, 1, 1))
            else:
                moved = jnp.where(lane == LANES - 1, rim[q // 2], pltpu.roll(value, LANES - 1, 1))
            beside[q * NFREQ + j, 8 * h : 8 * h + 8, :] = moved

    def update(i, cosine, sine):
        following_step = jnp.minimum(i + 1, QUARTER - 1)
        for h in range(2):
            columns = rims(following_step, h)
            turn_left = half(0, h) > 0.0
            shift_up = half(1, h) > 0.0
            mask = half(2, h)
            turned = turn_part(h)
            stay = mask - turned
            shifted = mask * half(1, h)
            leave = mask * (cosine + sine)
            factors = []
            for q in range(4):
                speed_x, speed_y = (cosine, sine) if q % 2 == 0 else (sine, cosine)
                factors.append((half(3 if q in (0, 3) else 4, h) * speed_x, half(5 if q in (0, 1) else 6, h) * speed_y))
            values = [cell(q * QUARTER + i, 0, 8 * h) for q in range(4)]
            faces = [None] * 4
            for j in range(NFREQ):
                keep = stay - SPEEDS[j] * leave
                for q in range(4):
                    direction = q * QUARTER + i
                    before, after = direction - 1, direction + 1
                    if q == 0:
                        before = jnp.where(i == 0, NDIR - 1, before)
                    if q == 3:
                        after = jnp.where(i == QUARTER - 1, 0, after)
                    along = cell(direction, j, 8 * h + (-1 if q in (0, 1) else 1))
                    moved = factors[q][0] * beside[q * NFREQ + j, 8 * h : 8 * h + 8, :] + factors[q][1] * along
                    total = keep * values[q] + SPEEDS[j] * moved
                    total = total + turned * jnp.where(turn_left, cell(before, j, 8 * h), cell(after, j, 8 * h))
                    if j > 0:
                        total = total + faces[q]
                    if j < NFREQ - 1:
                        following = cell(direction, j + 1, 8 * h)
                        faces[q] = shifted * jnp.where(shift_up, values[q], following)
                        total = total - faces[q]
                        values[q] = following
                    updated[direction * NFREQ + j, 8 * h : 8 * h + 8, :] = total
                prepare(following_step, h, j, columns)

    for q in range(4):
        load(q * QUARTER + QUARTER - 1).wait()
    for q in range(4):
        load(q * QUARTER).wait()
    for h in range(2):
        first_columns = rims(0, h)
        for j in range(NFREQ):
            prepare(0, h, j, first_columns)

    def one_step(i, angle):
        @pl.when(i < QUARTER - 2)
        def _():
            for q in range(4):
                load(q * QUARTER + i + 1).wait()

        update(i, *angle)
        for q in range(4):
            store(q * QUARTER + i).start()
        return next_angle(*angle)

    lax.fori_loop(0, QUARTER, one_step, first_angle())

    def finish(direction, carry):
        store(direction).wait()
        return carry

    lax.fori_loop(0, NDIR, finish, 0)


def shards(mesh_shape, spectrum, sea_mask, ocean_state, depth):
    groups_y = mesh_shape["gy"]
    groups = groups_y * mesh_shape["sec"]
    cells = spectrum.reshape(CELLS, LANES)
    vmem = pl.BlockSpec(memory_space=pltpu.VMEM)
    anywhere = pl.BlockSpec(memory_space=pl.ANY)
    f32 = jnp.float32
    dma = pltpu.SemaphoreType.DMA
    ocean_out, fields, rows, cols = pl.pallas_call(
        functools.partial(coupled_kernel, groups_y, groups),
        out_shape=(
            jax.ShapeDtypeStruct(ocean_state.shape, f32),
            jax.ShapeDtypeStruct((7 * ROWS, LANES), f32),
            jax.ShapeDtypeStruct((2, HALF, LANES), f32),
            jax.ShapeDtypeStruct((2, 6, ROWS, LANES), f32),
        ),
        in_specs=[anywhere, vmem, vmem, vmem],
        out_specs=(vmem, vmem, anywhere, anywhere),
        scratch_shapes=[
            pltpu.VMEM((CELLS, LANES), f32),
            pltpu.VMEM((SLOTS, 1792), f32),
            pltpu.VMEM((SLOTS, 1280), f32),
            pltpu.VMEM((PEERS, 2, SLOTS, LANES), f32),
            pltpu.VMEM((2, SLOTS * SLOTS, LANES), f32),
            pltpu.VMEM((4, 3, ROWS, LANES), f32),
            pltpu.VMEM((2, 3, ROWS, LANES), f32),
            pltpu.VMEM((2, 3, 8, LANES), f32),
            pltpu.VMEM((3, 3, 32, LANES), f32),
            pltpu.VMEM((2, 72, LANES), f32),
            pltpu.VMEM((PEERS, 2, SLOTS, LANES), f32),
            pltpu.VMEM((PEERS, 2, SLOTS, LANES), f32),
            pltpu.VMEM((2, HALF, LANES), f32),
            pltpu.VMEM((2, 6, ROWS, LANES), f32),
            dma((NDIR,)),
            dma((2, PEERS)),
            dma((2, 2)),
            dma((2, 4)),
            dma((2, 8)),
            dma((2, PEERS)),
            dma((2, 4)),
            dma((4,)),
        ],
        compiler_params=pltpu.CompilerParams(
            collective_id=0, has_side_effects=True, vmem_limit_bytes=VMEM_LIMIT
        ),
        name="coupled",
    )(cells, sea_mask, ocean_state, depth)
    spectrum_out = pl.pallas_call(
        wave_kernel,
        out_shape=jax.ShapeDtypeStruct((NDIR * NFREQ, ROWS, LANES), f32),
        in_specs=[anywhere, vmem, anywhere, anywhere],
        out_specs=anywhere,
        scratch_shapes=[
            pltpu.VMEM((NDIR * NFREQ + 1, PITCH, LANES), f32),
            pltpu.VMEM((NDIR * NFREQ, ROWS, LANES), f32),
            pltpu.VMEM((4 * NFREQ, ROWS, LANES), f32),
            pltpu.VMEM((2, HALF, LANES), f32),
            pltpu.VMEM((2, 6, ROWS, LANES), f32),
            dma((NDIR,)),
            dma((NDIR,)),
            dma((2,)),
        ],
        compiler_params=pltpu.CompilerParams(vmem_limit_bytes=VMEM_LIMIT),
        name="wave",
    )(spectrum.reshape(NDIR * NFREQ, ROWS, LANES), fields, rows, cols)
    return (spectrum_out.reshape(spectrum.shape), ocean_out)


def solution(mesh):
    return jax.shard_map(
        functools.partial(shards, dict(mesh.shape)),
        mesh=mesh,
        in_specs=(
            P(None, None, ("sec", "gy"), "gx"),
            P(("sec", "gy", "gx"), None),
            P(None, ("sec", "gy", "gx"), None),
            P(("sec", "gy", "gx"), None),
        ),
        out_specs=(P(None, None, ("sec", "gy"), "gx"), P(None, ("sec", "gy", "gx"), None)),
        check_vma=False,
    )
```

```python
import functools
import math

import jax
import jax.numpy as jnp
from jax import lax
from jax.experimental import pallas as pl
from jax.experimental.pallas import tpu as pltpu
from jax.sharding import PartitionSpec as P

ITERS = 4
GRAVITY_STEP = 0.3
CORIOLIS_STEP = 0.2
STRESS_GAIN = 2.0
TURN_GAIN = 0.2
SPEED_BASE = 0.35
SPEED_RATIO = 0.9

NDIR = 36
NFREQ = 20
ROWS = 16
LANES = 128
CELLS = NDIR * NFREQ * ROWS
PER_DIR = NFREQ * ROWS
QUARTER = NDIR // 4
PITCH = 24
VMEM_LIMIT = 60 * 1024 * 1024
HALF = NDIR // 2 * NFREQ
PEERS = 8
SLOTS = 16
MARGIN_O = 24
MARGIN_W = 16
SPEEDS = [SPEED_BASE * SPEED_RATIO**j for j in range(NFREQ)]
STEP_ANGLE = 2.0 * math.pi / NDIR
MESH = pl.DeviceIdType.MESH
AROUND = [(1, 0), (-1, 0), (0, 1), (0, -1), (1, 1), (1, -1), (-1, 1), (-1, -1)]


def iota(shape, dim):
    return lax.broadcasted_iota(jnp.int32, shape, dim)


def next_angle(cosine, sine):
    turn_c, turn_s = math.cos(STEP_ANGLE), math.sin(STEP_ANGLE)
    return cosine * turn_c - sine * turn_s, sine * turn_c + cosine * turn_s


def first_angle():
    return jnp.float32(math.cos(0.5 * STEP_ANGLE)), jnp.float32(math.sin(0.5 * STEP_ANGLE))


def exact_dot(values, weights):
    rows = values.shape[0]
    high = values.astype(jnp.bfloat16)
    rest = values - high.astype(jnp.float32)
    middle = rest.astype(jnp.bfloat16)
    low = (rest - middle.astype(jnp.float32)).astype(jnp.bfloat16)
    stacked = jnp.concatenate([high, middle, low], axis=0)
    product = jnp.dot(stacked, weights, preferred_element_type=jnp.float32)
    return product[:rows] + product[rows : 2 * rows] + product[2 * rows :]


def ocean_shift(values, amount):
    return pltpu.roll(values, amount % values.shape[1], 1)


def along_x(values):
    return (ocean_shift(values, -1) - ocean_shift(values, 1)) * 0.5


def along_y(classes):
    above = [classes[1], classes[2], pltpu.roll(classes[0], SLOTS - 1, 0)]
    below = [pltpu.roll(classes[2], 1, 0), classes[0], classes[1]]
    return [(above[c] - below[c]) * 0.5 for c in range(3)]


def coupled_kernel(
    groups_y,
    groups,
    spectrum,
    sea_mask,
    ocean_state,
    depth,
    ocean_out,
    fields_out,
    rows_out,
    cols_out,
    cells,
    state_in,
    depth_in,
    mask_in,
    raw,
    raw_mask,
    pack,
    window,
    mask_window,
    beside_send,
    across_send,
    beside_land,
    across_land,
    stress,
    result,
    result_send,
    result_land,
    rows_send,
    cols_send,
    input_sem,
    load_sem,
    pack_sem,
    far_sem,
    stress_sem,
    result_sem,
    halo_sem,
    local_sem,
):
    x = lax.axis_index("gx")
    y = lax.axis_index("sec") * groups_y + lax.axis_index("gy")

    def exists(dy, dx):
        checks = []
        if dy > 0:
            checks.append(y < groups - 1)
        if dy < 0:
            checks.append(y > 0)
        if dx > 0:
            checks.append(x < PEERS - 1)
        if dx < 0:
            checks.append(x > 0)
        answer = checks[0]
        for check in checks[1:]:
            answer = jnp.logical_and(answer, check)
        return answer

    def device_at(row, column):
        return (row // groups_y, lax.rem(row, groups_y), column)

    def device(dy, dx):
        return device_at(y + dy, x + dx)

    def peer(step):
        return (lax.axis_index("sec"), lax.axis_index("gy"), lax.rem(x + step, PEERS))

    inputs = [
        pltpu.make_async_copy(ocean_state, state_in, input_sem.at[0]),
        pltpu.make_async_copy(depth, depth_in, input_sem.at[1]),
        pltpu.make_async_copy(sea_mask, mask_in, input_sem.at[2]),
    ]
    for copy in inputs:
        copy.start()

    barrier = pltpu.get_barrier_semaphore()
    for step in range(1, PEERS):
        pl.semaphore_signal(barrier, inc=1, device_id=peer(step), device_id_type=MESH)
    greeted = PEERS - 1
    for dy in (1, -1):
        here = exists(dy, 0)

        @pl.when(here)
        def _():
            for column in range(PEERS):
                pl.semaphore_signal(barrier, inc=1, device_id=device_at(y + dy, column), device_id_type=MESH)

        greeted = greeted + here.astype(jnp.int32) * PEERS

    def load(direction):
        span = pl.ds(pl.multiple_of(direction * PER_DIR, PER_DIR), PER_DIR)
        return pltpu.make_async_copy(spectrum.at[span], cells.at[span], load_sem.at[direction])

    def start_load(i, carry):
        for q in range(4):
            load(q * QUARTER + i).start()
        return carry

    lax.fori_loop(0, QUARTER, start_load, 0)

    window[:, 11 * SLOTS : 13 * SLOTS, :] = jnp.zeros((2, 2 * SLOTS, LANES), jnp.float32)
    edge = jnp.zeros((2, 3 * SLOTS, LANES), jnp.float32)

    @pl.when(y == 0)
    def _():
        window[:, 13 * SLOTS : 16 * SLOTS, :] = edge
        across_land[:, 1] = jnp.zeros((3, 4, 8, LANES), jnp.float32)

    @pl.when(y == groups - 1)
    def _():
        window[:, 8 * SLOTS : 11 * SLOTS, :] = edge
        across_land[:, 0] = jnp.zeros((3, 4, 8, LANES), jnp.float32)

    @pl.when(x == 0)
    def _():
        beside_land[1] = jnp.zeros((5, ROWS, LANES), jnp.float32)
        across_land[2] = jnp.zeros((2, 4, 8, LANES), jnp.float32)

    @pl.when(x == PEERS - 1)
    def _():
        beside_land[0] = jnp.zeros((5, ROWS, LANES), jnp.float32)
        across_land[1] = jnp.zeros((2, 4, 8, LANES), jnp.float32)

    raw[...] = jnp.zeros_like(raw)
    raw_mask[...] = jnp.zeros_like(raw_mask)
    width = state_in.shape[2]
    for copy in inputs:
        copy.wait()
    for f in range(3):
        raw[3 * f : 3 * f + 3, :width] = state_in[f]
    raw[9:12, :width] = depth_in[...]
    raw_mask[12:14, : mask_in.shape[1]] = mask_in[...].astype(jnp.float32)
    even = ocean_shift(raw[...], MARGIN_O)
    odd = ocean_shift(raw[...], MARGIN_O - 64)
    mask_rows = ocean_shift(raw_mask[...], MARGIN_W)
    is_ocean = iota((SLOTS, LANES), 0) < 12
    for dest in range(PEERS):
        source = odd if dest % 2 else even
        origin = 384 * (dest // 2) + (128 if dest % 2 else 0)
        for tile in range(2):
            pack[dest, tile] = jnp.where(
                is_ocean,
                source[:, origin + LANES * tile : origin + LANES * (tile + 1)],
                mask_rows[:, LANES * (dest + tile) : LANES * (dest + tile + 1)],
            )

    def slot(n):
        return pl.ds(pl.multiple_of(n * SLOTS, SLOTS), SLOTS)

    def pack_copy(step):
        dest = peer(step)
        return pltpu.make_async_remote_copy(
            src_ref=pack.at[dest[2]],
            dst_ref=window.at[:, slot(x), :],
            send_sem=pack_sem.at[0, step],
            recv_sem=pack_sem.at[1, step],
            device_id=dest,
            device_id_type=MESH,
        )

    upward = x >= PEERS - 3
    far = jnp.logical_or(jnp.logical_and(upward, y < groups - 1), jnp.logical_and(x <= 2, y > 0))
    far_row = jnp.where(upward, y + 1, y - 1)

    def far_copy(column):
        return pltpu.make_async_remote_copy(
            src_ref=pack.at[column],
            dst_ref=window.at[:, slot(x + PEERS), :],
            send_sem=far_sem.at[0, column],
            recv_sem=far_sem.at[1, x],
            device_id=device_at(far_row, column),
            device_id_type=MESH,
        )

    def far_arrival(column):
        return pltpu.make_async_remote_copy(
            src_ref=pack.at[column],
            dst_ref=window.at[:, slot(column + PEERS), :],
            send_sem=far_sem.at[0, column],
            recv_sem=far_sem.at[1, column],
            device_id=peer(1),
            device_id_type=MESH,
        )

    pl.semaphore_wait(barrier, greeted)

    @pl.when(far)
    def _():
        for column in range(PEERS):
            far_copy(column).start()

    for step in range(1, PEERS):
        pack_copy(step).start()
    window[:, slot(x), :] = pack[x]

    lane = iota((ROWS, LANES), 1)
    row = iota((ROWS, LANES), 0)
    zero = jnp.zeros((ROWS, LANES), jnp.float32)

    def gather(i, carry):
        (cosine, sine), plain, fluxes = carry
        for q in range(4):
            load(q * QUARTER + i).wait()
        totals, weighted, rims = [None] * 4, [None] * 4, [zero, zero]
        for j in range(NFREQ):
            values = []
            for q in range(4):
                base = (q * QUARTER + i) * PER_DIR
                values.append(cells[pl.ds(pl.multiple_of(base + j * ROWS, ROWS), ROWS), :])
                scaled = values[q] * SPEEDS[j]
                totals[q] = values[q] if j == 0 else totals[q] + values[q]
                weighted[q] = scaled if j == 0 else weighted[q] + scaled
            here = jnp.logical_or(lane == 2 * j + 1, lane == 2 * j + 2)
            for n, (east, west) in enumerate(((0, 1), (3, 2))):
                both = jnp.where(lane == LANES - 1, values[east], values[west])
                rims[n] = jnp.where(here, pltpu.roll(both, 2 * j + 2, 1), rims[n])
        for n in range(2):
            place = i + n * QUARTER
            group, part = place // 3, lax.rem(place, 3)
            earlier = jnp.where(part > 0, cols_send[group], zero)
            cols_send[group] = earlier + pltpu.roll(rims[n], part * (2 * NFREQ), 1)
        scale = 0.5 / (NDIR * NFREQ)
        cc, cs, ss = cosine * cosine * scale, cosine * sine * scale, sine * sine * scale
        pair = (totals[0] + totals[2]) - (totals[1] + totals[3])
        plain = (
            plain[0] + ((totals[0] + totals[2]) + (totals[1] + totals[3])),
            plain[1] + (cc - ss) * pair,
            plain[2] + (2.0 * cs) * pair,
        )
        straight, crossed = (cc, cs, ss), (ss, -cs, cc)
        west, east, south, north = fluxes
        west = tuple(
            west[s] + (cosine * straight[s]) * weighted[0] + (sine * crossed[s]) * weighted[3] for s in range(3)
        )
        east = tuple(
            east[s] + (cosine * straight[s]) * weighted[2] + (sine * crossed[s]) * weighted[1] for s in range(3)
        )
        south = tuple(
            south[s] + (sine * straight[s]) * weighted[0] + (cosine * crossed[s]) * weighted[1] for s in range(3)
        )
        north = tuple(
            north[s] + (sine * straight[s]) * weighted[2] + (cosine * crossed[s]) * weighted[3] for s in range(3)
        )
        return next_angle(cosine, sine), plain, (west, east, south, north)

    cols_send[...] = jnp.zeros_like(cols_send)
    triple = (zero, zero, zero)
    carry = (first_angle(), triple, (triple, triple, triple, triple))
    _, plain, fluxes = lax.fori_loop(0, QUARTER, gather, carry)

    def pack_rows(n, carry):
        for m in range(5):
            start = n * 40 + m * 8
            span = pl.ds(pl.multiple_of(start, 8), 8)
            rows_send[0, span, :] = cells[pl.ds(start * ROWS + (ROWS - 1), 8, stride=ROWS), :]
            rows_send[1, span, :] = cells[pl.ds(start * ROWS + HALF * ROWS, 8, stride=ROWS), :]
        return carry

    lax.fori_loop(0, HALF // 40, pack_rows, 0)

    for step in range(1, PEERS):
        pack_copy(step).wait_recv()

    @pl.when(y < groups - 1)
    def _():
        for column in range(3):
            far_arrival(column).wait_recv()

    @pl.when(y > 0)
    def _():
        for column in range(PEERS - 3, PEERS):
            far_arrival(column).wait_recv()

    def window_rows(first):
        return jnp.concatenate([window[t, pl.ds(first, SLOTS, stride=SLOTS), :] for t in range(2)], axis=1)

    wide = (2 * LANES, 2 * LANES)
    wave_masks = [window_rows(12), window_rows(13)]
    spread = (iota(wide, 0) == (2 * iota(wide, 1)) // 3).astype(jnp.bfloat16)
    masks = jnp.dot(
        jnp.concatenate(wave_masks, axis=0).astype(jnp.bfloat16), spread, preferred_element_type=jnp.float32
    )
    ocean_mask = [masks[:SLOTS], masks[:SLOTS], masks[SLOTS:]]
    surface = [window_rows(c) * ocean_mask[c] for c in range(3)]
    eastward = [window_rows(3 + c) * ocean_mask[c] for c in range(3)]
    northward = [window_rows(6 + c) * ocean_mask[c] for c in range(3)]
    bottom = [window_rows(9 + c) for c in range(3)]

    east_y, north_y = along_y(eastward), along_y(northward)
    vorticity = [along_x(northward[c]) - east_y[c] for c in range(3)]
    divergence = [along_x(eastward[c]) + north_y[c] for c in range(3)]
    coarse = []
    for field in (vorticity, divergence):
        coarse.append((2.0 * field[0] + field[1])[:8])
        coarse.append((field[1] + 2.0 * field[2])[:8])
    narrow = (2 * LANES, LANES)
    fine, wave = iota(narrow, 0), iota(narrow, 1) + MARGIN_W
    group = 3 * (wave // 2)
    ends = jnp.where(wave % 2 == 0, group, group + 2)
    weights = jnp.where(fine == ends, 2.0, jnp.where(fine == group + 1, 1.0, 0.0)).astype(jnp.bfloat16)
    coarse = exact_dot(jnp.concatenate(coarse, axis=0), weights) * (1.0 / 9.0)
    for n in range(2):
        for c in range(2):
            place = pl.ds(ROWS * n + c, 8, stride=2)
            fields_out[place, :] = TURN_GAIN * jnp.tanh(coarse[16 * n + 8 * c : 16 * n + 8 * c + 8])

    for c in range(2):
        placed = ocean_shift(wave_masks[c], -MARGIN_W)
        for t in range(2):
            mask_window[t, pl.ds(c, SLOTS, stride=2), :] = placed[:, LANES * t : LANES * (t + 1)]
    around = jnp.concatenate([mask_window[0], mask_window[1]], axis=1)
    west_mask = around * pltpu.roll(around, 1, 1)
    east_mask = around * pltpu.roll(around, 2 * LANES - 1, 1)
    south_mask = around * pltpu.roll(around, 1, 0)
    north_mask = around * pltpu.roll(around, 2 * ROWS - 1, 0)
    for n, values in enumerate((around, west_mask, east_mask, south_mask, north_mask)):
        fields_out[(2 + n) * ROWS : (3 + n) * ROWS, :] = values[:ROWS, :LANES]

    def field(n):
        return fields_out[ROWS * n : ROWS * (n + 1), :]

    turning = field(0)
    turn_abs = jnp.abs(turning)
    scale = 0.25 / (NDIR * NFREQ)
    base, along, across = plain[0] * scale, plain[1] * 0.5, plain[2] * 0.5
    turn_c, turn_s = math.cos(2.0 * STEP_ANGLE), math.sin(2.0 * STEP_ANGLE)
    signed = jnp.where(turning > 0.0, turn_s, -turn_s)
    along_turn = along * turn_c - across * signed
    across_turn = across * turn_c + along * signed
    stay = 1.0 - turn_abs
    along = stay * along + turn_abs * along_turn
    across = stay * across + turn_abs * across_turn
    local = [base + along, across, base - along]
    west, east, south, north = fluxes
    rims = zero
    for s in range(3):
        partial = field(2) * (local[s] - ((west[s] + east[s]) + (south[s] + north[s])))
        partial = partial + field(3) * jnp.where(lane == 0, 0.0, pltpu.roll(west[s], 1, 1))
        partial = partial + field(4) * jnp.where(lane == LANES - 1, 0.0, pltpu.roll(east[s], LANES - 1, 1))
        partial = partial + field(5) * jnp.where(row == 0, 0.0, pltpu.roll(south[s], 1, 0))
        partial = partial + field(6) * jnp.where(row == ROWS - 1, 0.0, pltpu.roll(north[s], ROWS - 1, 0))
        beside_send[s] = partial
        across_send[0, s] = partial[8:]
        across_send[0, s, 0:1, :] = south[s][ROWS - 1 :]
        across_send[1, s] = partial[:8]
        across_send[1, s, 7:8, :] = north[s][:1]
        beside_send[4, s : s + 1, :] = south[s][ROWS - 1 :]
        beside_send[4, 8 + s : 9 + s, :] = north[s][:1]
        rims = jnp.where(lane == LANES - 1 - s, pltpu.roll(west[s], (LANES - s) % LANES, 1) if s else west[s], rims)
        rims = jnp.where(lane == s, pltpu.roll(east[s], s, 1) if s else east[s], rims)
    beside_send[3] = rims
    across_send[0, 3] = rims[8:]
    across_send[1, 3] = rims[:8]

    def stress_copy(n):
        dy, dx = AROUND[n]
        if dy == 0:
            source, target = beside_send, beside_land.at[{1: 1, -1: 0}[dx]]
        else:
            source = across_send.at[{1: 0, -1: 1}[dy]]
            target = across_land.at[{0: 0, 1: 2, -1: 1}[dx], {1: 1, -1: 0}[dy]]
        return pltpu.make_async_remote_copy(
            src_ref=source,
            dst_ref=target,
            send_sem=stress_sem.at[0, n],
            recv_sem=stress_sem.at[1, n],
            device_id=device(dy, dx),
            device_id_type=MESH,
        )

    for n, (dy, dx) in enumerate(AROUND):

        @pl.when(exists(dy, dx))
        def _():
            stress_copy(n).start()

    sends = (exists(0, 1), exists(0, -1), exists(1, 0), exists(-1, 0))
    receives = (exists(0, -1), exists(0, 1), exists(-1, 0), exists(1, 0))

    def halo_ends(n):
        return (cols_send, cols_out.at[n]) if n < 2 else (rows_send.at[n - 2], rows_out.at[n - 2])

    def halo_copy(n):
        source, target = halo_ends(n)
        return pltpu.make_async_remote_copy(
            src_ref=source,
            dst_ref=target,
            send_sem=halo_sem.at[0, n],
            recv_sem=halo_sem.at[1, n],
            device_id=(device(0, 1), device(0, -1), device(1, 0), device(-1, 0))[n],
            device_id_type=MESH,
        )

    def halo_fill(n):
        source, target = halo_ends(n)
        return pltpu.make_async_copy(source, target, local_sem.at[n])

    for n in range(4):

        @pl.when(sends[n])
        def _():
            halo_copy(n).start()

        @pl.when(jnp.logical_not(receives[n]))
        def _():
            halo_fill(n).start()

    safe = [jnp.where(bottom[c] > 0.0, bottom[c], 1.0) for c in range(3)]
    inverse = [-STRESS_GAIN / safe[c] for c in range(3)]

    def raise_surface(surface, eastward, northward):
        flow_y = along_y([bottom[c] * northward[c] for c in range(3)])
        return [
            (surface[c] - GRAVITY_STEP * (along_x(bottom[c] * eastward[c]) + flow_y[c])) * ocean_mask[c]
            for c in range(3)
        ]

    def push(surface, eastward, northward):
        slope = along_y(surface)
        new_east = [
            eastward[c] + GRAVITY_STEP * (CORIOLIS_STEP * northward[c] - along_x(surface[c])) for c in range(3)
        ]
        new_north = [northward[c] + GRAVITY_STEP * (-CORIOLIS_STEP * eastward[c] - slope[c]) for c in range(3)]
        return new_east, new_north

    surface = raise_surface(surface, eastward, northward)
    pushed = push(surface, eastward, northward)
    wave_lane, fine = iota(wide, 0), iota(wide, 1)
    wave_lane = jnp.where(wave_lane < LANES + 64, wave_lane + MARGIN_W, wave_lane - 2 * LANES + MARGIN_W)
    first = 2 * (fine // 3)
    part = fine % 3
    hits = jnp.where(wave_lane == first, 1.0, 0.0) * jnp.where(part == 0, 1.0, jnp.where(part == 1, 0.5, 0.0)) + jnp.where(
        wave_lane == first + 1, 1.0, 0.0
    ) * jnp.where(part == 2, 1.0, jnp.where(part == 1, 0.5, 0.0))
    prolong = hits.astype(jnp.bfloat16)

    for n, (dy, dx) in enumerate(AROUND):

        @pl.when(exists(-dy, -dx))
        def _():
            stress_copy(n).wait_recv()

    side_lane = iota((2 * ROWS, LANES), 1) < 64

    def assemble(s):
        columns = [
            jnp.concatenate([body, across_land[n, 0, s], across_land[n, 1, s]], axis=0)
            for n, body in enumerate((beside_send[s], beside_land[0, s], beside_land[1, s]))
        ]
        return jnp.concatenate([columns[0], jnp.where(side_lane, columns[1], columns[2])], axis=1)

    def edge_row(place):
        rows = [ref[place : place + 1, :] for ref in (beside_send.at[4], beside_land.at[0, 4], beside_land.at[1, 4])]
        return jnp.concatenate([rows[0], jnp.where(side_lane[:1], rows[1], rows[2])], axis=1)

    around_row = iota((2 * ROWS, 2 * LANES), 0)
    around_lane = iota((2 * ROWS, 2 * LANES), 1)
    west_side = west_mask * jnp.where(around_lane % LANES == 0, 1.0, 0.0)
    east_side = east_mask * jnp.where(around_lane % LANES == LANES - 1, 1.0, 0.0)
    side_flux = assemble(3)
    pieces = []
    for s in range(3):
        body = assemble(s)
        from_south = jnp.where(
            around_row == 0, body[24:25], jnp.where(around_row == ROWS, edge_row(s), 0.0)
        )
        from_north = jnp.where(
            around_row == ROWS - 1, body[23:24], jnp.where(around_row == 2 * ROWS - 1, edge_row(8 + s), 0.0)
        )
        body = body + west_side * pltpu.roll(side_flux, s + 1, 1)
        body = body + east_side * pltpu.roll(side_flux, 2 * LANES - 1 - s, 1)
        body = body + south_mask * from_south + north_mask * from_north
        for t in range(2):
            stress[s, t] = body[:, LANES * t : LANES * (t + 1)]
        for c in range(2):
            pieces.append(
                jnp.concatenate([stress[s, t, pl.ds(c, SLOTS, stride=2), :] for t in range(2)], axis=1)
            )
    spread_stress = exact_dot(jnp.concatenate(pieces, axis=0), prolong)
    tensor = []
    for s in range(3):
        low = spread_stress[2 * SLOTS * s : 2 * SLOTS * s + SLOTS]
        high = spread_stress[2 * SLOTS * s + SLOTS : 2 * SLOTS * (s + 1)]
        tensor.append([low, 0.5 * low + 0.5 * high, high])
    cross_y, normal_y = along_y(tensor[1]), along_y(tensor[2])
    force_x = [inverse[c] * (along_x(tensor[0][c]) + cross_y[c]) for c in range(3)]
    force_y = [inverse[c] * (along_x(tensor[1][c]) + normal_y[c]) for c in range(3)]

    for step in range(ITERS):
        if step > 0:
            surface = raise_surface(surface, eastward, northward)
            pushed = push(surface, eastward, northward)
        eastward = [(pushed[0][c] + force_x[c]) * ocean_mask[c] for c in range(3)]
        northward = [(pushed[1][c] + force_y[c]) * ocean_mask[c] for c in range(3)]

    is_even = lax.rem(x, 2) == 0
    for f, values in enumerate((surface, eastward, northward)):
        for c in range(3):
            own = values[c][:8]
            placed = jnp.where(is_even, ocean_shift(own, -MARGIN_O), ocean_shift(own, 64 - MARGIN_O))
            for t in range(2):
                result[t, 8 * (3 * f + c) : 8 * (3 * f + c) + 8, :] = placed[:, LANES * t : LANES * (t + 1)]
    for dest in range(PEERS):
        for t in range(2):
            result_send[dest, t, 0:8, :] = result[t, pl.ds(dest, 8, stride=8), :]
            result_send[dest, t, 8:9, :] = result[t, 64 + dest : 65 + dest, :]

    def result_copy(step):
        dest = peer(step)
        return pltpu.make_async_remote_copy(
            src_ref=result_send.at[dest[2]],
            dst_ref=result_land.at[x],
            send_sem=result_sem.at[0, step],
            recv_sem=result_sem.at[1, step],
            device_id=dest,
            device_id_type=MESH,
        )

    for step in range(1, PEERS):
        result_copy(step).start()
    result_land[x] = result_send[x]
    for step in range(1, PEERS):
        result_copy(step).wait_recv()
    low_half = iota((SLOTS, LANES), 1) < 64
    for q in range(PEERS // 2):
        left, right = 2 * q, 2 * q + 1
        tiles = (
            result_land[left, 0],
            jnp.where(low_half, result_land[left, 1], result_land[right, 0]),
            result_land[right, 1],
        )
        for t in range(3):
            lanes = pl.ds((3 * q + t) * LANES, LANES)
            for f in range(3):
                ocean_out[f, :, lanes] = tiles[t][3 * f : 3 * f + 3]

    for step in range(1, PEERS):
        pack_copy(step).wait_send()
        result_copy(step).wait_send()

    @pl.when(far)
    def _():
        for column in range(PEERS):
            far_copy(column).wait_send()

    for n, (dy, dx) in enumerate(AROUND):

        @pl.when(exists(dy, dx))
        def _():
            stress_copy(n).wait_send()

    for n in range(4):

        @pl.when(sends[n])
        def _():
            halo_copy(n).wait_send()

        @pl.when(receives[n])
        def _():
            halo_copy(n).wait_recv()

        @pl.when(jnp.logical_not(receives[n]))
        def _():
            halo_fill(n).wait()


def wave_kernel(
    spectrum,
    fields,
    rows_in,
    cols_in,
    ocean_in,
    out,
    ocean_out,
    cells,
    updated,
    beside,
    rows,
    cols,
    load_sem,
    store_sem,
    halo_sem,
):
    def load(direction):
        return pltpu.make_async_copy(
            spectrum.at[pl.ds(direction * NFREQ, NFREQ)],
            cells.at[pl.ds(direction * NFREQ, NFREQ), pl.ds(8, ROWS), :],
            load_sem.at[direction],
        )

    def store(direction):
        span = pl.ds(direction * NFREQ, NFREQ)
        return pltpu.make_async_copy(updated.at[span], out.at[span], store_sem.at[direction])

    halos = [pltpu.make_async_copy(rows_in, rows, halo_sem.at[0]), pltpu.make_async_copy(cols_in, cols, halo_sem.at[1])]
    for copy in halos:
        copy.start()
    handed = pltpu.make_async_copy(ocean_in, ocean_out, halo_sem.at[2])
    handed.start()
    for q in range(4):
        load(q * QUARTER + QUARTER - 1).start()
    for q in range(4):
        load(q * QUARTER).start()

    def start_load(i, carry):
        for q in range(4):
            load(q * QUARTER + i).start()
        return carry

    lax.fori_loop(1, QUARTER - 1, start_load, 0)
    flat = cells.reshape((NDIR * NFREQ + 1) * PITCH, LANES)

    def half(n, h):
        return fields[ROWS * n + 8 * h : ROWS * n + 8 * h + 8, :]

    def turn_part(h):
        return half(2, h) * jnp.abs(half(0, h))

    lane = iota((8, LANES), 1)
    for copy in halos:
        copy.wait()

    def place_rows(n, carry):
        span = pl.ds(pl.multiple_of(n * 8, 8), 8)
        flat[pl.ds(n * (8 * PITCH) + 7, 8, stride=PITCH), :] = rows[0, span, :]
        flat[pl.ds(n * (8 * PITCH) + (HALF + 1) * PITCH, 8, stride=PITCH), :] = rows[1, span, :]
        return carry

    lax.fori_loop(0, HALF // 8, place_rows, 0)

    def cell(direction, j, offset):
        return flat[pl.ds(direction * (NFREQ * PITCH) + (j * PITCH + 8 + offset), 8), :]

    odd = lax.rem(lane, 2) == 1

    def rims(i, h):
        columns = []
        for place in (i, QUARTER + i):
            group, part = place // 3, lax.rem(place, 3)
            span = slice(8 * h, 8 * h + 8)
            merged = jnp.where(odd, cols[0, group, span, :], cols[1, group, span, :])
            columns.append(pltpu.roll(merged, lax.rem(LANES - part * (2 * NFREQ), LANES), 1))
        return columns

    def rim_at(columns, j):
        return [pltpu.roll(column, LANES - 1 - 2 * j, 1) for column in columns]

    def prepare(i, h, j, columns, rim):
        following = rim_at(columns, j + 1)
        for q in range(4):
            value = cell(q * QUARTER + i, j, 8 * h)
            if q in (0, 3):
                moved = jnp.where(lane == 0, rim[q // 2], pltpu.roll(value, 1, 1))
            else:
                moved = jnp.where(lane == LANES - 1, following[q // 2], pltpu.roll(value, LANES - 1, 1))
            beside[q * NFREQ + j, 8 * h : 8 * h + 8, :] = moved
        return following

    def update(i, cosine, sine):
        following_step = jnp.minimum(i + 1, QUARTER - 1)
        for h in range(2):
            columns = rims(following_step, h)
            rim = rim_at(columns, 0)
            turn_left = half(0, h) > 0.0
            shift_up = half(1, h) > 0.0
            mask = half(2, h)
            turned = turn_part(h)
            stay = mask - turned
            shifted = mask * half(1, h)
            leave = mask * (cosine + sine)
            factors = []
            for q in range(4):
                speed_x, speed_y = (cosine, sine) if q % 2 == 0 else (sine, cosine)
                factors.append((half(3 if q in (0, 3) else 4, h) * speed_x, half(5 if q in (0, 1) else 6, h) * speed_y))
            values = [cell(q * QUARTER + i, 0, 8 * h) for q in range(4)]
            faces = [None] * 4
            for j in range(NFREQ):
                keep = stay - SPEEDS[j] * leave
                for q in range(4):
                    direction = q * QUARTER + i
                    before, after = direction - 1, direction + 1
                    if q == 0:
                        before = jnp.where(i == 0, NDIR - 1, before)
                    if q == 3:
                        after = jnp.where(i == QUARTER - 1, 0, after)
                    along = cell(direction, j, 8 * h + (-1 if q in (0, 1) else 1))
                    moved = factors[q][0] * beside[q * NFREQ + j, 8 * h : 8 * h + 8, :] + factors[q][1] * along
                    total = keep * values[q] + SPEEDS[j] * moved
                    total = total + turned * jnp.where(turn_left, cell(before, j, 8 * h), cell(after, j, 8 * h))
                    if j > 0:
                        total = total + faces[q]
                    if j < NFREQ - 1:
                        following = cell(direction, j + 1, 8 * h)
                        faces[q] = shifted * jnp.where(shift_up, values[q], following)
                        total = total - faces[q]
                        values[q] = following
                    updated[direction * NFREQ + j, 8 * h : 8 * h + 8, :] = total
                rim = prepare(following_step, h, j, columns, rim)

    for q in range(4):
        load(q * QUARTER + QUARTER - 1).wait()
    for q in range(4):
        load(q * QUARTER).wait()
    for h in range(2):
        first_columns = rims(0, h)
        first_rim = rim_at(first_columns, 0)
        for j in range(NFREQ):
            first_rim = prepare(0, h, j, first_columns, first_rim)

    def one_step(i, angle):
        @pl.when(i < QUARTER - 2)
        def _():
            for q in range(4):
                load(q * QUARTER + i + 1).wait()

        update(i, *angle)
        for q in range(4):
            store(q * QUARTER + i).start()
        return next_angle(*angle)

    lax.fori_loop(0, QUARTER, one_step, first_angle())

    def finish(direction, carry):
        store(direction).wait()
        return carry

    lax.fori_loop(0, NDIR, finish, 0)
    handed.wait()


def shards(mesh_shape, spectrum, sea_mask, ocean_state, depth):
    groups_y = mesh_shape["gy"]
    groups = groups_y * mesh_shape["sec"]
    cells = spectrum.reshape(CELLS, LANES)
    vmem = pl.BlockSpec(memory_space=pltpu.VMEM)
    anywhere = pl.BlockSpec(memory_space=pl.ANY)
    f32 = jnp.float32
    dma = pltpu.SemaphoreType.DMA
    ocean_part, fields, rows, cols = pl.pallas_call(
        functools.partial(coupled_kernel, groups_y, groups),
        out_shape=(
            jax.ShapeDtypeStruct(ocean_state.shape, f32),
            jax.ShapeDtypeStruct((7 * ROWS, LANES), f32),
            jax.ShapeDtypeStruct((2, HALF, LANES), f32),
            jax.ShapeDtypeStruct((2, 6, ROWS, LANES), f32),
        ),
        in_specs=[anywhere] * 4,
        out_specs=(vmem, vmem, anywhere, anywhere),
        scratch_shapes=[
            pltpu.VMEM((CELLS, LANES), f32),
            pltpu.VMEM(ocean_state.shape, f32),
            pltpu.VMEM(depth.shape, f32),
            pltpu.VMEM(sea_mask.shape, jnp.int32),
            pltpu.VMEM((SLOTS, 1792), f32),
            pltpu.VMEM((SLOTS, 1280), f32),
            pltpu.VMEM((PEERS, 2, SLOTS, LANES), f32),
            pltpu.VMEM((2, SLOTS * SLOTS, LANES), f32),
            pltpu.VMEM((2, 2 * ROWS, LANES), f32),
            pltpu.VMEM((5, ROWS, LANES), f32),
            pltpu.VMEM((2, 4, 8, LANES), f32),
            pltpu.VMEM((2, 5, ROWS, LANES), f32),
            pltpu.VMEM((3, 2, 4, 8, LANES), f32),
            pltpu.VMEM((3, 2, 2 * ROWS, LANES), f32),
            pltpu.VMEM((2, 72, LANES), f32),
            pltpu.VMEM((PEERS, 2, SLOTS, LANES), f32),
            pltpu.VMEM((PEERS, 2, SLOTS, LANES), f32),
            pltpu.VMEM((2, HALF, LANES), f32),
            pltpu.VMEM((6, ROWS, LANES), f32),
            dma((3,)),
            dma((NDIR,)),
            dma((2, PEERS)),
            dma((2, PEERS)),
            dma((2, 8)),
            dma((2, PEERS)),
            dma((2, 4)),
            dma((4,)),
        ],
        compiler_params=pltpu.CompilerParams(
            collective_id=0, has_side_effects=True, vmem_limit_bytes=VMEM_LIMIT
        ),
        name="coupled",
    )(cells, sea_mask, ocean_state, depth)
    spectrum_out, ocean_out = pl.pallas_call(
        wave_kernel,
        out_shape=(
            jax.ShapeDtypeStruct((NDIR * NFREQ, ROWS, LANES), f32),
            jax.ShapeDtypeStruct(ocean_state.shape, f32),
        ),
        in_specs=[anywhere, vmem, anywhere, anywhere, anywhere],
        out_specs=(anywhere, anywhere),
        scratch_shapes=[
            pltpu.VMEM((NDIR * NFREQ + 1, PITCH, LANES), f32),
            pltpu.VMEM((NDIR * NFREQ, ROWS, LANES), f32),
            pltpu.VMEM((4 * NFREQ, ROWS, LANES), f32),
            pltpu.VMEM((2, HALF, LANES), f32),
            pltpu.VMEM((2, 6, ROWS, LANES), f32),
            dma((NDIR,)),
            dma((NDIR,)),
            dma((3,)),
        ],
        compiler_params=pltpu.CompilerParams(vmem_limit_bytes=VMEM_LIMIT),
        name="wave",
    )(spectrum.reshape(NDIR * NFREQ, ROWS, LANES), fields, rows, cols, ocean_part)
    return (spectrum_out.reshape(spectrum.shape), ocean_out)


def solution(mesh):
    return jax.shard_map(
        functools.partial(shards, dict(mesh.shape)),
        mesh=mesh,
        in_specs=(
            P(None, None, ("sec", "gy"), "gx"),
            P(("sec", "gy", "gx"), None),
            P(None, ("sec", "gy", "gx"), None),
            P(("sec", "gy", "gx"), None),
        ),
        out_specs=(P(None, None, ("sec", "gy"), "gx"), P(None, ("sec", "gy", "gx"), None)),
        check_vma=False,
    )
```

```python
import functools
import math

import jax
import jax.numpy as jnp
from jax import lax
from jax.experimental import pallas as pl
from jax.experimental.pallas import tpu as pltpu
from jax.sharding import PartitionSpec as P

ITERS = 4
GRAVITY_STEP = 0.3
CORIOLIS_STEP = 0.2
STRESS_GAIN = 2.0
TURN_GAIN = 0.2
SPEED_BASE = 0.35
SPEED_RATIO = 0.9

NDIR = 36
NFREQ = 20
ROWS = 16
LANES = 128
CELLS = NDIR * NFREQ * ROWS
PER_DIR = NFREQ * ROWS
QUARTER = NDIR // 4
PAD = 8
DURING_STRESS = 5
CHUNKS = 8
LOADS = 3
VMEM_LIMIT = 28 * 1024 * 1024
HALF = NDIR // 2 * NFREQ
PEERS = 8
SLOTS = 16
MARGIN_O = 24
MARGIN_W = 16
SPEEDS = [SPEED_BASE * SPEED_RATIO**j for j in range(NFREQ)]
STEP_ANGLE = 2.0 * math.pi / NDIR
MESH = pl.DeviceIdType.MESH
AROUND = [(1, 0), (-1, 0), (0, 1), (0, -1), (1, 1), (1, -1), (-1, 1), (-1, -1)]


def iota(shape, dim):
    return lax.broadcasted_iota(jnp.int32, shape, dim)


def next_angle(cosine, sine):
    turn_c, turn_s = math.cos(STEP_ANGLE), math.sin(STEP_ANGLE)
    return cosine * turn_c - sine * turn_s, sine * turn_c + cosine * turn_s


def angle_at(i):
    return jnp.float32(math.cos((i + 0.5) * STEP_ANGLE)), jnp.float32(math.sin((i + 0.5) * STEP_ANGLE))


def exact_dot(values, weights):
    rows = values.shape[0]
    high = values.astype(jnp.bfloat16)
    rest = values - high.astype(jnp.float32)
    middle = rest.astype(jnp.bfloat16)
    low = (rest - middle.astype(jnp.float32)).astype(jnp.bfloat16)
    stacked = jnp.concatenate([high, middle, low], axis=0)
    product = jnp.dot(stacked, weights, preferred_element_type=jnp.float32)
    return product[:rows] + product[rows : 2 * rows] + product[2 * rows :]


def ocean_shift(values, amount):
    return pltpu.roll(values, amount % values.shape[1], 1)


def along_x(values):
    return (ocean_shift(values, -1) - ocean_shift(values, 1)) * 0.5


def along_y(classes):
    above = [classes[1], classes[2], pltpu.roll(classes[0], SLOTS - 1, 0)]
    below = [pltpu.roll(classes[2], 1, 0), classes[0], classes[1]]
    return [(above[c] - below[c]) * 0.5 for c in range(3)]


def wave_tools(fields, rows, cols, cells, beside, target):
    lane = iota((8, LANES), 1)
    row = iota((8, LANES), 0)

    def half(n, h):
        return fields[ROWS * n + 8 * h : ROWS * n + 8 * h + 8, :]

    def turn_part(h):
        return half(2, h) * jnp.abs(half(0, h))

    def cell(direction, j, offset):
        place = direction * PER_DIR + (PAD + j * ROWS + offset)
        return cells[pl.ds(pl.multiple_of(place, 8) if offset % 8 == 0 else place, 8), :]

    odd = lax.rem(lane, 2) == 1

    def rims(i, h):
        columns = []
        for place in (i, QUARTER + i):
            group, part = place // 3, lax.rem(place, 3)
            span = slice(8 * h, 8 * h + 8)
            merged = jnp.where(odd, cols[0, group, span, :], cols[1, group, span, :])
            columns.append(pltpu.roll(merged, lax.rem(LANES - part * (2 * NFREQ), LANES), 1))
        return columns

    def rim_at(columns, j):
        return [pltpu.roll(column, LANES - 1 - 2 * j, 1) for column in columns]

    def prepare(i, h, j, columns, rim):
        following = rim_at(columns, j + 1)
        for q in range(4):
            value = cell(q * QUARTER + i, j, 8 * h)
            if q in (0, 3):
                moved = jnp.where(lane == 0, rim[q // 2], pltpu.roll(value, 1, 1))
            else:
                moved = jnp.where(lane == LANES - 1, following[q // 2], pltpu.roll(value, LANES - 1, 1))
            beside[q * NFREQ + j, 8 * h : 8 * h + 8, :] = moved
        return following

    def update(i, angle):
        cosine, sine = angle
        following_step = jnp.minimum(i + 1, QUARTER - 1)
        for h in range(2):
            columns = rims(following_step, h)
            rim = rim_at(columns, 0)
            turn_left = half(0, h) > 0.0
            shift_up = half(1, h) > 0.0
            mask = half(2, h)
            turned = turn_part(h)
            stay = mask - turned
            shifted = mask * half(1, h)
            leave = mask * (cosine + sine)
            factors = []
            for q in range(4):
                speed_x, speed_y = (cosine, sine) if q % 2 == 0 else (sine, cosine)
                inner = half(5 if q in (0, 1) else 6, h) * speed_y
                if q in (0, 1) and h == 0:
                    inner = jnp.where(row == 0, 0.0, inner)
                if q in (2, 3) and h == 1:
                    inner = jnp.where(row == 7, 0.0, inner)
                factors.append((half(3 if q in (0, 3) else 4, h) * speed_x, inner))
            values = [cell(q * QUARTER + i, 0, 8 * h) for q in range(4)]
            faces = [None] * 4
            for j in range(NFREQ):
                keep = stay - SPEEDS[j] * leave
                for q in range(4):
                    direction = q * QUARTER + i
                    before, after = direction - 1, direction + 1
                    if q == 0:
                        before = jnp.where(i == 0, NDIR - 1, before)
                    if q == 3:
                        after = jnp.where(i == QUARTER - 1, 0, after)
                    along = cell(direction, j, 8 * h + (-1 if q in (0, 1) else 1))
                    moved = factors[q][0] * beside[q * NFREQ + j, 8 * h : 8 * h + 8, :] + factors[q][1] * along
                    total = keep * values[q] + SPEEDS[j] * moved
                    total = total + turned * jnp.where(turn_left, cell(before, j, 8 * h), cell(after, j, 8 * h))
                    if j > 0:
                        total = total + faces[q]
                    if j < NFREQ - 1:
                        following = cell(direction, j + 1, 8 * h)
                        faces[q] = shifted * jnp.where(shift_up, values[q], following)
                        total = total - faces[q]
                        values[q] = following
                    place = (direction * NFREQ + j) * ROWS + 8 * h
                    target[pl.ds(pl.multiple_of(place, 8), 8), :] = total
                rim = prepare(following_step, h, j, columns, rim)

    def prepare_first():
        for h in range(2):
            columns = rims(0, h)
            rim = rim_at(columns, 0)
            for j in range(NFREQ):
                rim = prepare(0, h, j, columns, rim)

    def finish_rows(i, angle):
        for q in range(4):
            speed_y = angle[1] if q % 2 == 0 else angle[0]
            from_south = q in (0, 1)
            edge = (5 * ROWS) if from_south else (7 * ROWS - 1)
            factor = fields[edge : edge + 1, :] * speed_y
            direction = q * QUARTER + i
            source = (direction if from_south else direction - 2 * QUARTER) * NFREQ
            for first in (0, 8, 16):
                count = min(8, NFREQ - first)
                speeds = jnp.zeros((count, LANES), jnp.float32)
                for r in range(count):
                    speeds = jnp.where(row[:count] == r, SPEEDS[first + r], speeds)
                span = pl.ds((direction * NFREQ + first) * ROWS + (0 if from_south else ROWS - 1), count, stride=ROWS)
                rim = rows[0 if from_south else 1, pl.ds(source + first, count), :]
                target[span, :] = target[span, :] + speeds * (factor * rim)

    return prepare_first, update, finish_rows


def coupled_kernel(
    groups_y,
    groups,
    spectrum,
    sea_mask,
    ocean_state,
    depth,
    ocean_out,
    updated,
    fields_out,
    rows_out,
    cols_out,
    cells,
    beside,
    state_in,
    depth_in,
    mask_in,
    raw,
    raw_mask,
    pack,
    pack_late,
    window,
    window_late,
    brink,
    mask_window,
    beside_send,
    across_send,
    beside_land,
    across_land,
    stress,
    result,
    result_send,
    result_land,
    rows_send,
    cols_send,
    input_sem,
    load_sem,
    pack_sem,
    late_sem,
    far_sem,
    band_sem,
    stress_sem,
    result_sem,
    halo_sem,
    local_sem,
):
    x = lax.axis_index("gx")
    y = lax.axis_index("sec") * groups_y + lax.axis_index("gy")

    def exists(dy, dx):
        checks = []
        if dy > 0:
            checks.append(y < groups - 1)
        if dy < 0:
            checks.append(y > 0)
        if dx > 0:
            checks.append(x < PEERS - 1)
        if dx < 0:
            checks.append(x > 0)
        answer = checks[0]
        for check in checks[1:]:
            answer = jnp.logical_and(answer, check)
        return answer

    def device_at(row, column):
        return (row // groups_y, lax.rem(row, groups_y), column)

    def device(dy, dx):
        return device_at(y + dy, x + dx)

    def peer(step):
        return (lax.axis_index("sec"), lax.axis_index("gy"), lax.rem(x + step, PEERS))

    inputs = [
        pltpu.make_async_copy(ocean_state, state_in, input_sem.at[0]),
        pltpu.make_async_copy(depth, depth_in, input_sem.at[1]),
        pltpu.make_async_copy(sea_mask, mask_in, input_sem.at[2]),
    ]
    for copy in inputs:
        copy.start()

    barrier = pltpu.get_barrier_semaphore()
    for step in range(1, PEERS):
        pl.semaphore_signal(barrier, inc=1, device_id=peer(step), device_id_type=MESH)
    greeted = PEERS - 1
    for dy in (1, -1):
        here = exists(dy, 0)

        @pl.when(here)
        def _():
            for column in range(PEERS):
                pl.semaphore_signal(barrier, inc=1, device_id=device_at(y + dy, column), device_id_type=MESH)

        greeted = greeted + here.astype(jnp.int32) * PEERS

    def load(q, part):
        size = QUARTER // LOADS * PER_DIR
        start = pl.multiple_of(q * (QUARTER * PER_DIR) + part * size, PER_DIR)
        return pltpu.make_async_copy(
            spectrum.at[pl.ds(start, size)],
            cells.at[pl.ds(pl.multiple_of(start + PAD, 8), size)],
            load_sem.at[part * 4 + q],
        )

    for part in range(LOADS):
        for q in range(4):
            load(q, part).start()

    raw[...] = jnp.zeros_like(raw)
    raw_mask[...] = jnp.zeros_like(raw_mask)
    width = state_in.shape[2]
    for copy in inputs:
        copy.wait()
    raw[0:3, :width] = state_in[1]
    raw[3:6, :width] = state_in[2]
    raw[8:11, :width] = state_in[0]
    raw[11:14, :width] = depth_in[...]
    raw_mask[6:8, : mask_in.shape[1]] = mask_in[...].astype(jnp.float32)
    even = ocean_shift(raw[...], MARGIN_O)
    odd = ocean_shift(raw[...], MARGIN_O - 64)
    mask_rows = ocean_shift(raw_mask[...], MARGIN_W)
    is_ocean = iota((8, LANES), 0) < 6
    for dest in range(PEERS):
        source = odd if dest % 2 else even
        origin = 384 * (dest // 2) + (128 if dest % 2 else 0)
        for tile in range(2):
            piece = source[:, origin + LANES * tile : origin + LANES * (tile + 1)]
            pack[dest, tile] = jnp.where(
                is_ocean, piece[:8], mask_rows[:, LANES * (dest + tile) : LANES * (dest + tile + 1)]
            )
            pack_late[dest, tile] = piece[8:]

    slot = pl.ds(pl.multiple_of(x * 8, 8), 8)

    def pack_copy(step, late):
        dest = peer(step)
        return pltpu.make_async_remote_copy(
            src_ref=(pack_late if late else pack).at[dest[2]],
            dst_ref=(window_late if late else window).at[:, slot, :],
            send_sem=(late_sem if late else pack_sem).at[0, step],
            recv_sem=(late_sem if late else pack_sem).at[1, step],
            device_id=dest,
            device_id_type=MESH,
        )

    last, first = x == PEERS - 1, x == 0
    to_north, to_south = jnp.logical_and(last, y < groups - 1), jnp.logical_and(first, y > 0)

    def brink_copy(n, column):
        return pltpu.make_async_remote_copy(
            src_ref=pack.at[column],
            dst_ref=brink.at[n],
            send_sem=far_sem.at[n, column],
            recv_sem=far_sem.at[2, n],
            device_id=device_at(y + (1 if n == 0 else -1), column),
            device_id_type=MESH,
        )

    pl.semaphore_wait(barrier, greeted)
    for n, needed in enumerate((to_north, to_south)):

        @pl.when(needed)
        def _():
            for column in range(PEERS):
                brink_copy(n, column).start()

    for step in range(1, PEERS):
        pack_copy(step, False).start()
    for step in range(1, PEERS):
        pack_copy(step, True).start()
    mask_window[...] = jnp.zeros_like(mask_window)
    cells[:PAD, :] = jnp.zeros((PAD, LANES), jnp.float32)
    cells[PAD + CELLS :, :] = jnp.zeros((PAD, LANES), jnp.float32)
    for ref in (window, window_late):
        ref[:, 11 * 8 : 13 * 8, :] = jnp.zeros((2, 16, LANES), jnp.float32)
    edge = jnp.zeros((2, 24, LANES), jnp.float32)

    @pl.when(y == 0)
    def _():
        window[:, 13 * 8 : 16 * 8, :] = edge
        window_late[:, 13 * 8 : 16 * 8, :] = edge
        brink[0] = jnp.zeros((2, 8, LANES), jnp.float32)
        across_land[:, 1] = jnp.zeros((3, 4, 8, LANES), jnp.float32)

    @pl.when(y == groups - 1)
    def _():
        window[:, 8 * 8 : 11 * 8, :] = edge
        window_late[:, 8 * 8 : 11 * 8, :] = edge
        brink[1] = jnp.zeros((2, 8, LANES), jnp.float32)
        across_land[:, 0] = jnp.zeros((3, 4, 8, LANES), jnp.float32)

    @pl.when(x == 0)
    def _():
        beside_land[1] = jnp.zeros((5, ROWS, LANES), jnp.float32)
        across_land[2] = jnp.zeros((2, 4, 8, LANES), jnp.float32)

    @pl.when(x == PEERS - 1)
    def _():
        beside_land[0] = jnp.zeros((5, ROWS, LANES), jnp.float32)
        across_land[1] = jnp.zeros((2, 4, 8, LANES), jnp.float32)

    window[:, slot, :] = pack[x]
    window_late[:, slot, :] = pack_late[x]

    lane = iota((ROWS, LANES), 1)
    row = iota((ROWS, LANES), 0)
    zero = jnp.zeros((ROWS, LANES), jnp.float32)

    def gather(i, carry):
        (cosine, sine), plain, fluxes = carry
        part = QUARTER // LOADS

        @pl.when(lax.rem(i, part) == 0)
        def _():
            for q in range(4):
                load(q, i // part).wait()

        totals, weighted, rims = [None] * 4, [None] * 4, [zero, zero]
        for j in range(NFREQ):
            values = []
            for q in range(4):
                base = (q * QUARTER + i) * PER_DIR + PAD
                values.append(cells[pl.ds(pl.multiple_of(base + j * ROWS, 8), ROWS), :])
                scaled = values[q] * SPEEDS[j]
                totals[q] = values[q] if j == 0 else totals[q] + values[q]
                weighted[q] = scaled if j == 0 else weighted[q] + scaled
            here = jnp.logical_or(lane == 2 * j + 1, lane == 2 * j + 2)
            for n, (east, west) in enumerate(((0, 1), (3, 2))):
                both = jnp.where(lane == LANES - 1, values[east], values[west])
                rims[n] = jnp.where(here, pltpu.roll(both, 2 * j + 2, 1), rims[n])
        for n in range(2):
            place = i + n * QUARTER
            group, part = place // 3, lax.rem(place, 3)
            earlier = jnp.where(part > 0, cols_send[group], zero)
            cols_send[group] = earlier + pltpu.roll(rims[n], part * (2 * NFREQ), 1)
        scale = 0.5 / (NDIR * NFREQ)
        cc, cs, ss = cosine * cosine * scale, cosine * sine * scale, sine * sine * scale
        pair = (totals[0] + totals[2]) - (totals[1] + totals[3])
        plain = (
            plain[0] + ((totals[0] + totals[2]) + (totals[1] + totals[3])),
            plain[1] + (cc - ss) * pair,
            plain[2] + (2.0 * cs) * pair,
        )
        straight, crossed = (cc, cs, ss), (ss, -cs, cc)
        west, east, south, north = fluxes
        west = tuple(
            west[s] + (cosine * straight[s]) * weighted[0] + (sine * crossed[s]) * weighted[3] for s in range(3)
        )
        east = tuple(
            east[s] + (cosine * straight[s]) * weighted[2] + (sine * crossed[s]) * weighted[1] for s in range(3)
        )
        south = tuple(
            south[s] + (sine * straight[s]) * weighted[0] + (cosine * crossed[s]) * weighted[1] for s in range(3)
        )
        north = tuple(
            north[s] + (sine * straight[s]) * weighted[2] + (cosine * crossed[s]) * weighted[3] for s in range(3)
        )
        return next_angle(cosine, sine), plain, (west, east, south, north)

    cols_send[...] = jnp.zeros_like(cols_send)
    triple = (zero, zero, zero)
    carry = (angle_at(0), triple, (triple, triple, triple, triple))
    _, plain, fluxes = lax.fori_loop(0, QUARTER, gather, carry)

    def pack_rows(n, carry):
        for m in range(5):
            start = n * 40 + m * 8
            span = pl.ds(pl.multiple_of(start, 8), 8)
            rows_send[0, span, :] = cells[pl.ds(start * ROWS + (PAD + ROWS - 1), 8, stride=ROWS), :]
            rows_send[1, span, :] = cells[pl.ds(start * ROWS + (PAD + HALF * ROWS), 8, stride=ROWS), :]
        return carry

    lax.fori_loop(0, HALF // 40, pack_rows, 0)

    sends = (exists(0, 1), exists(0, -1), exists(1, 0), exists(-1, 0))
    receives = (exists(0, -1), exists(0, 1), exists(-1, 0), exists(1, 0))

    def halo_ends(n):
        return (cols_send, cols_out.at[n]) if n < 2 else (rows_send.at[n - 2], rows_out.at[n - 2])

    def halo_copy(n):
        source, target = halo_ends(n)
        return pltpu.make_async_remote_copy(
            src_ref=source,
            dst_ref=target,
            send_sem=halo_sem.at[0, n],
            recv_sem=halo_sem.at[1, n],
            device_id=(device(0, 1), device(0, -1), device(1, 0), device(-1, 0))[n],
            device_id_type=MESH,
        )

    def halo_fill(n):
        source, target = halo_ends(n)
        return pltpu.make_async_copy(source, target, local_sem.at[n])

    def start_halo(n):
        @pl.when(sends[n])
        def _():
            halo_copy(n).start()

        @pl.when(jnp.logical_not(receives[n]))
        def _():
            halo_fill(n).start()

    def wait_halo(n):
        @pl.when(receives[n])
        def _():
            halo_copy(n).wait_recv()

        @pl.when(jnp.logical_not(receives[n]))
        def _():
            halo_fill(n).wait()

    start_halo(0)
    start_halo(1)

    for step in range(1, PEERS):
        pack_copy(step, False).wait_recv()

    def band_copy(n, late):
        source = pl.ds((5 if n == 0 else 0) * 8, 24)
        target = pl.ds((13 if n == 0 else 8) * 8, 24)
        ref = window_late if late else window
        return pltpu.make_async_remote_copy(
            src_ref=ref.at[:, source, :],
            dst_ref=ref.at[:, target, :],
            send_sem=band_sem.at[0, 2 * n + late],
            recv_sem=band_sem.at[1, 2 * n + late],
            device_id=device(1 if n == 0 else -1, 0),
            device_id_type=MESH,
        )

    vertical = (exists(1, 0), exists(-1, 0))
    from_side = (exists(-1, 0), exists(1, 0))
    for n in range(2):

        @pl.when(vertical[n])
        def _():
            band_copy(n, 0).start()

    for n in range(2):

        @pl.when(from_side[n])
        def _():
            brink_copy(n, 0).wait_recv()

    def tiles_of(ref, rows):
        return jnp.concatenate([ref[t, rows, :] for t in range(2)], axis=1)

    def own_rows(first):
        return tiles_of(window, pl.ds(first, 8, stride=8))

    def brink_row(n, place):
        return tiles_of(brink.at[n], pl.ds(place, 1))

    wide = (2 * LANES, 2 * LANES)
    spread = (iota(wide, 0) == (2 * iota(wide, 1)) // 3).astype(jnp.bfloat16)
    wave_masks = [own_rows(6), own_rows(7)]
    brink_masks = [brink_row(0, 7), brink_row(1, 6)]
    top = iota((8, 2 * LANES), 0) == 0
    bottom_row = iota((8, 2 * LANES), 0) == 7
    both = jnp.where(top, brink_masks[0], brink_masks[1])
    masks = jnp.dot(
        jnp.concatenate(wave_masks + [both], axis=0).astype(jnp.bfloat16), spread, preferred_element_type=jnp.float32
    )
    near_mask = [masks[:8], masks[:8], masks[8:16]]
    brink_ocean = [masks[16:17], masks[17:18]]

    def near(base):
        inner = [own_rows(base + c) * near_mask[c] for c in range(3)]
        below = jnp.where(top, brink_row(0, base + 2) * brink_ocean[0], pltpu.roll(inner[2], 1, 0))
        above = jnp.where(bottom_row, brink_row(1, base) * brink_ocean[1], pltpu.roll(inner[0], 7, 0))
        slope = [(inner[1] - below) * 0.5, (inner[2] - inner[0]) * 0.5, (above - inner[1]) * 0.5]
        return inner, slope

    (near_east, east_y), (near_north, north_y) = near(0), near(3)
    vorticity = [along_x(near_north[c]) - east_y[c] for c in range(3)]
    divergence = [along_x(near_east[c]) + north_y[c] for c in range(3)]
    coarse = []
    for field in (vorticity, divergence):
        coarse.append(2.0 * field[0] + field[1])
        coarse.append(field[1] + 2.0 * field[2])
    narrow = (2 * LANES, LANES)
    fine, wave = iota(narrow, 0), iota(narrow, 1) + MARGIN_W
    group = 3 * (wave // 2)
    ends = jnp.where(wave % 2 == 0, group, group + 2)
    weights = jnp.where(fine == ends, 2.0, jnp.where(fine == group + 1, 1.0, 0.0)).astype(jnp.bfloat16)
    coarse = exact_dot(jnp.concatenate(coarse, axis=0), weights) * (1.0 / 9.0)
    for n in range(2):
        for c in range(2):
            place = pl.ds(ROWS * n + c, 8, stride=2)
            fields_out[place, :] = TURN_GAIN * jnp.tanh(coarse[16 * n + 8 * c : 16 * n + 8 * c + 8])

    for c in range(2):
        placed = ocean_shift(wave_masks[c], -MARGIN_W)
        rim_mask = ocean_shift(brink_masks[1 - c], -MARGIN_W)
        for t in range(2):
            span = slice(LANES * t, LANES * (t + 1))
            mask_window[t, pl.ds(c, 8, stride=2), :] = placed[:, span]
            mask_window[t, 16 if c == 0 else 31, :] = rim_mask[0, span]

    def mask_products():
        around = tiles_of(mask_window, slice(None))
        return (
            around,
            around * pltpu.roll(around, 1, 1),
            around * pltpu.roll(around, 2 * LANES - 1, 1),
            around * pltpu.roll(around, 1, 0),
            around * pltpu.roll(around, 2 * ROWS - 1, 0),
        )

    for n, values in enumerate(mask_products()):
        fields_out[(2 + n) * ROWS : (3 + n) * ROWS, :] = values[:ROWS, :LANES]

    def field(n):
        return fields_out[ROWS * n : ROWS * (n + 1), :]

    turning = field(0)
    turn_abs = jnp.abs(turning)
    scale = 0.25 / (NDIR * NFREQ)
    base, along, across = plain[0] * scale, plain[1] * 0.5, plain[2] * 0.5
    turn_c, turn_s = math.cos(2.0 * STEP_ANGLE), math.sin(2.0 * STEP_ANGLE)
    signed = jnp.where(turning > 0.0, turn_s, -turn_s)
    along_turn = along * turn_c - across * signed
    across_turn = across * turn_c + along * signed
    stay = 1.0 - turn_abs
    along = stay * along + turn_abs * along_turn
    across = stay * across + turn_abs * across_turn
    local = [base + along, across, base - along]
    west, east, south, north = fluxes
    rims = zero
    for s in range(3):
        partial = field(2) * (local[s] - ((west[s] + east[s]) + (south[s] + north[s])))
        partial = partial + field(3) * jnp.where(lane == 0, 0.0, pltpu.roll(west[s], 1, 1))
        partial = partial + field(4) * jnp.where(lane == LANES - 1, 0.0, pltpu.roll(east[s], LANES - 1, 1))
        partial = partial + field(5) * jnp.where(row == 0, 0.0, pltpu.roll(south[s], 1, 0))
        partial = partial + field(6) * jnp.where(row == ROWS - 1, 0.0, pltpu.roll(north[s], ROWS - 1, 0))
        beside_send[s] = partial
        across_send[0, s] = partial[8:]
        across_send[0, s, 0:1, :] = south[s][ROWS - 1 :]
        across_send[1, s] = partial[:8]
        across_send[1, s, 7:8, :] = north[s][:1]
        beside_send[4, s : s + 1, :] = south[s][ROWS - 1 :]
        beside_send[4, 8 + s : 9 + s, :] = north[s][:1]
        rims = jnp.where(lane == LANES - 1 - s, pltpu.roll(west[s], (LANES - s) % LANES, 1) if s else west[s], rims)
        rims = jnp.where(lane == s, pltpu.roll(east[s], s, 1) if s else east[s], rims)
    beside_send[3] = rims
    across_send[0, 3] = rims[8:]
    across_send[1, 3] = rims[:8]

    def stress_copy(n):
        dy, dx = AROUND[n]
        if dy == 0:
            source, target = beside_send, beside_land.at[{1: 1, -1: 0}[dx]]
        else:
            source = across_send.at[{1: 0, -1: 1}[dy]]
            target = across_land.at[{0: 0, 1: 2, -1: 1}[dx], {1: 1, -1: 0}[dy]]
        return pltpu.make_async_remote_copy(
            src_ref=source,
            dst_ref=target,
            send_sem=stress_sem.at[0, n],
            recv_sem=stress_sem.at[1, n],
            device_id=device(dy, dx),
            device_id_type=MESH,
        )

    for n, (dy, dx) in enumerate(AROUND):

        @pl.when(exists(dy, dx))
        def _():
            stress_copy(n).start()

    for step in range(1, PEERS):
        pack_copy(step, True).wait_recv()
    for n in range(2):

        @pl.when(vertical[n])
        def _():
            band_copy(n, 1).start()

    start_halo(2)
    start_halo(3)
    prepare_first, update, finish_rows = wave_tools(fields_out, rows_out, cols_out, cells, beside, updated)
    for n in range(2):
        wait_halo(n)
    prepare_first()

    def one_step(i, angle):
        update(i, angle)
        return next_angle(*angle)

    angle = lax.fori_loop(0, DURING_STRESS, one_step, angle_at(0))

    for n in range(2):

        @pl.when(from_side[n])
        def _():
            band_copy(n, 0).wait_recv()
            band_copy(n, 1).wait_recv()

    def all_rows(ref, first):
        return tiles_of(ref, pl.ds(first, SLOTS, stride=8))

    far_masks = [all_rows(window, 6), all_rows(window, 7)]
    masks = jnp.dot(
        jnp.concatenate(far_masks, axis=0).astype(jnp.bfloat16), spread, preferred_element_type=jnp.float32
    )
    ocean_mask = [masks[:SLOTS], masks[:SLOTS], masks[SLOTS:]]
    surface = [all_rows(window_late, c) * ocean_mask[c] for c in range(3)]
    eastward = [all_rows(window, c) * ocean_mask[c] for c in range(3)]
    northward = [all_rows(window, 3 + c) * ocean_mask[c] for c in range(3)]
    bottom = [all_rows(window_late, 3 + c) for c in range(3)]
    for c in range(2):
        placed = ocean_shift(far_masks[c], -MARGIN_W)
        for t in range(2):
            mask_window[t, pl.ds(c, SLOTS, stride=2), :] = placed[:, LANES * t : LANES * (t + 1)]
    _, west_mask, east_mask, south_mask, north_mask = mask_products()

    safe = [jnp.where(bottom[c] > 0.0, bottom[c], 1.0) for c in range(3)]
    inverse = [-STRESS_GAIN / safe[c] for c in range(3)]

    def raise_surface(surface, eastward, northward):
        flow_y = along_y([bottom[c] * northward[c] for c in range(3)])
        return [
            (surface[c] - GRAVITY_STEP * (along_x(bottom[c] * eastward[c]) + flow_y[c])) * ocean_mask[c]
            for c in range(3)
        ]

    def push(surface, eastward, northward):
        slope = along_y(surface)
        new_east = [
            eastward[c] + GRAVITY_STEP * (CORIOLIS_STEP * northward[c] - along_x(surface[c])) for c in range(3)
        ]
        new_north = [northward[c] + GRAVITY_STEP * (-CORIOLIS_STEP * eastward[c] - slope[c]) for c in range(3)]
        return new_east, new_north

    surface = raise_surface(surface, eastward, northward)
    pushed = push(surface, eastward, northward)
    wave_lane, fine = iota(wide, 0), iota(wide, 1)
    wave_lane = jnp.where(wave_lane < LANES + 64, wave_lane + MARGIN_W, wave_lane - 2 * LANES + MARGIN_W)
    first = 2 * (fine // 3)
    part = fine % 3
    hits = jnp.where(wave_lane == first, 1.0, 0.0) * jnp.where(part == 0, 1.0, jnp.where(part == 1, 0.5, 0.0)) + jnp.where(
        wave_lane == first + 1, 1.0, 0.0
    ) * jnp.where(part == 2, 1.0, jnp.where(part == 1, 0.5, 0.0))
    prolong = hits.astype(jnp.bfloat16)

    for n, (dy, dx) in enumerate(AROUND):

        @pl.when(exists(-dy, -dx))
        def _():
            stress_copy(n).wait_recv()

    side_lane = iota((2 * ROWS, LANES), 1) < 64

    def assemble(s):
        columns = [
            jnp.concatenate([body, across_land[n, 0, s], across_land[n, 1, s]], axis=0)
            for n, body in enumerate((beside_send[s], beside_land[0, s], beside_land[1, s]))
        ]
        return jnp.concatenate([columns[0], jnp.where(side_lane, columns[1], columns[2])], axis=1)

    def edge_row(place):
        rows = [ref[place : place + 1, :] for ref in (beside_send.at[4], beside_land.at[0, 4], beside_land.at[1, 4])]
        return jnp.concatenate([rows[0], jnp.where(side_lane[:1], rows[1], rows[2])], axis=1)

    around_row = iota((2 * ROWS, 2 * LANES), 0)
    around_lane = iota((2 * ROWS, 2 * LANES), 1)
    west_side = west_mask * jnp.where(around_lane % LANES == 0, 1.0, 0.0)
    east_side = east_mask * jnp.where(around_lane % LANES == LANES - 1, 1.0, 0.0)
    side_flux = assemble(3)
    pieces = []
    for s in range(3):
        body = assemble(s)
        from_south = jnp.where(
            around_row == 0, body[24:25], jnp.where(around_row == ROWS, edge_row(s), 0.0)
        )
        from_north = jnp.where(
            around_row == ROWS - 1, body[23:24], jnp.where(around_row == 2 * ROWS - 1, edge_row(8 + s), 0.0)
        )
        body = body + west_side * pltpu.roll(side_flux, s + 1, 1)
        body = body + east_side * pltpu.roll(side_flux, 2 * LANES - 1 - s, 1)
        body = body + south_mask * from_south + north_mask * from_north
        for t in range(2):
            stress[s, t] = body[:, LANES * t : LANES * (t + 1)]
        for c in range(2):
            pieces.append(
                jnp.concatenate([stress[s, t, pl.ds(c, SLOTS, stride=2), :] for t in range(2)], axis=1)
            )
    spread_stress = exact_dot(jnp.concatenate(pieces, axis=0), prolong)
    tensor = []
    for s in range(3):
        low = spread_stress[2 * SLOTS * s : 2 * SLOTS * s + SLOTS]
        high = spread_stress[2 * SLOTS * s + SLOTS : 2 * SLOTS * (s + 1)]
        tensor.append([low, 0.5 * low + 0.5 * high, high])
    cross_y, normal_y = along_y(tensor[1]), along_y(tensor[2])
    force_x = [inverse[c] * (along_x(tensor[0][c]) + cross_y[c]) for c in range(3)]
    force_y = [inverse[c] * (along_x(tensor[1][c]) + normal_y[c]) for c in range(3)]

    for step in range(ITERS):
        if step > 0:
            surface = raise_surface(surface, eastward, northward)
            pushed = push(surface, eastward, northward)
        eastward = [(pushed[0][c] + force_x[c]) * ocean_mask[c] for c in range(3)]
        northward = [(pushed[1][c] + force_y[c]) * ocean_mask[c] for c in range(3)]

    is_even = lax.rem(x, 2) == 0
    low_lanes = iota((8, LANES), 1) < 64
    halves = []
    for f, values in enumerate((surface, eastward, northward)):
        for c in range(3):
            own = values[c][:8]
            low, high = ocean_shift(own, -MARGIN_O), ocean_shift(own, 64 - MARGIN_O)
            place = 8 * (3 * f + c)
            result[place : place + 8, :] = jnp.where(is_even, low[:, :LANES], high[:, LANES:])
            halves.append(jnp.where(is_even, low[:, LANES:], pltpu.roll(high[:, :LANES], 64, 1)))
    for m in range(5):
        merged = halves[m] if m == 4 else jnp.where(low_lanes, halves[m], pltpu.roll(halves[5 + m], 64, 1))
        result[72 + 8 * m : 80 + 8 * m, :] = merged
    for dest in range(PEERS):
        result_send[dest, 0:8, :] = result[pl.ds(dest, 8, stride=8), :]
        result_send[dest, 8:14, :] = result[pl.ds(64 + dest, 6, stride=8), :]

    def result_copy(step):
        dest = peer(step)
        return pltpu.make_async_remote_copy(
            src_ref=result_send.at[dest[2]],
            dst_ref=result_land.at[x],
            send_sem=result_sem.at[0, step],
            recv_sem=result_sem.at[1, step],
            device_id=dest,
            device_id_type=MESH,
        )

    for step in range(1, PEERS):
        result_copy(step).start()
    result_land[x] = result_send[x]
    lax.fori_loop(DURING_STRESS, QUARTER, one_step, angle)
    for step in range(1, PEERS):
        result_copy(step).wait_recv()
    for q in range(PEERS // 2):
        left, right = result_land[2 * q], result_land[2 * q + 1]
        left_turned, right_turned = pltpu.roll(left, 64, 1), pltpu.roll(right, 64, 1)
        side = iota((5, LANES), 1) < 64
        middle = jnp.concatenate(
            [
                jnp.where(side, left[9:14], right_turned[9:14]),
                jnp.where(side[:4], left_turned[9:13], right[9:13]),
            ],
            axis=0,
        )
        for t, tile in enumerate((left, middle, right)):
            lanes = pl.ds((3 * q + t) * LANES, LANES)
            for f in range(3):
                ocean_out[f, :, lanes] = tile[3 * f : 3 * f + 3]

    for step in range(1, PEERS):
        pack_copy(step, False).wait_send()
        pack_copy(step, True).wait_send()
        result_copy(step).wait_send()
    for n, needed in enumerate((to_north, to_south)):

        @pl.when(needed)
        def _():
            for column in range(PEERS):
                brink_copy(n, column).wait_send()

        @pl.when(vertical[n])
        def _():
            band_copy(n, 0).wait_send()
            band_copy(n, 1).wait_send()

    for n, (dy, dx) in enumerate(AROUND):

        @pl.when(exists(dy, dx))
        def _():
            stress_copy(n).wait_send()

    for n in range(2, 4):
        wait_halo(n)

    def fix_step(i, angle):
        finish_rows(i, angle)
        return next_angle(*angle)

    lax.fori_loop(0, QUARTER, fix_step, angle_at(0))
    for n in range(4):

        @pl.when(sends[n])
        def _():
            halo_copy(n).wait_send()


def hand_over(ocean_in, updated, out, ocean_out, store_sem, local_sem):
    handed = pltpu.make_async_copy(ocean_in, ocean_out, local_sem)
    handed.start()
    size = CELLS // CHUNKS
    copies = [
        pltpu.make_async_copy(updated.at[pl.ds(n * size, size)], out.at[pl.ds(n * size, size)], store_sem.at[n])
        for n in range(CHUNKS)
    ]
    for copy in copies:
        copy.start()
    for copy in copies:
        copy.wait()
    handed.wait()


def shards(mesh_shape, spectrum, sea_mask, ocean_state, depth):
    groups_y = mesh_shape["gy"]
    groups = groups_y * mesh_shape["sec"]
    cells = spectrum.reshape(CELLS, LANES)
    vmem = pl.BlockSpec(memory_space=pltpu.VMEM)
    anywhere = pl.BlockSpec(memory_space=pl.ANY)
    f32 = jnp.float32
    dma = pltpu.SemaphoreType.DMA
    ocean_part, updated = pl.pallas_call(
        functools.partial(coupled_kernel, groups_y, groups),
        out_shape=(
            jax.ShapeDtypeStruct(ocean_state.shape, f32),
            jax.ShapeDtypeStruct((CELLS, LANES), f32),
        ),
        in_specs=[anywhere] * 4,
        out_specs=(vmem, vmem),
        scratch_shapes=[
            pltpu.VMEM((7 * ROWS, LANES), f32),
            pltpu.VMEM((2, HALF, LANES), f32),
            pltpu.VMEM((2, 6, ROWS, LANES), f32),
            pltpu.VMEM((CELLS + 2 * PAD, LANES), f32),
            pltpu.VMEM((4 * NFREQ, ROWS, LANES), f32),
            pltpu.VMEM(ocean_state.shape, f32),
            pltpu.VMEM(depth.shape, f32),
            pltpu.VMEM(sea_mask.shape, jnp.int32),
            pltpu.VMEM((SLOTS, 1792), f32),
            pltpu.VMEM((8, 1280), f32),
            pltpu.VMEM((PEERS, 2, 8, LANES), f32),
            pltpu.VMEM((PEERS, 2, 8, LANES), f32),
            pltpu.VMEM((2, SLOTS * 8, LANES), f32),
            pltpu.VMEM((2, SLOTS * 8, LANES), f32),
            pltpu.VMEM((2, 2, 8, LANES), f32),
            pltpu.VMEM((2, 2 * ROWS, LANES), f32),
            pltpu.VMEM((5, ROWS, LANES), f32),
            pltpu.VMEM((2, 4, 8, LANES), f32),
            pltpu.VMEM((2, 5, ROWS, LANES), f32),
            pltpu.VMEM((3, 2, 4, 8, LANES), f32),
            pltpu.VMEM((3, 2, 2 * ROWS, LANES), f32),
            pltpu.VMEM((112, LANES), f32),
            pltpu.VMEM((PEERS, SLOTS, LANES), f32),
            pltpu.VMEM((PEERS, SLOTS, LANES), f32),
            pltpu.VMEM((2, HALF, LANES), f32),
            pltpu.VMEM((6, ROWS, LANES), f32),
            dma((3,)),
            dma((4 * LOADS,)),
            dma((2, PEERS)),
            dma((2, PEERS)),
            dma((3, PEERS)),
            dma((2, 4)),
            dma((2, 8)),
            dma((2, PEERS)),
            dma((2, 4)),
            dma((4,)),
        ],
        compiler_params=pltpu.CompilerParams(
            collective_id=0, has_side_effects=True, vmem_limit_bytes=VMEM_LIMIT
        ),
        name="coupled",
    )(*[pltpu.with_memory_space_constraint(a, pltpu.HBM) for a in (cells, sea_mask, ocean_state, depth)])
    spectrum_out, ocean_out = pl.pallas_call(
        hand_over,
        out_shape=(jax.ShapeDtypeStruct((CELLS, LANES), f32), jax.ShapeDtypeStruct(ocean_state.shape, f32)),
        in_specs=[anywhere, anywhere],
        out_specs=(anywhere, anywhere),
        scratch_shapes=[dma((CHUNKS,)), dma],
        compiler_params=pltpu.CompilerParams(vmem_limit_bytes=VMEM_LIMIT),
        name="hand_over",
    )(ocean_part, updated)
    return (spectrum_out.reshape(spectrum.shape), ocean_out)


def solution(mesh):
    return jax.shard_map(
        functools.partial(shards, dict(mesh.shape)),
        mesh=mesh,
        in_specs=(
            P(None, None, ("sec", "gy"), "gx"),
            P(("sec", "gy", "gx"), None),
            P(None, ("sec", "gy", "gx"), None),
            P(("sec", "gy", "gx"), None),
        ),
        out_specs=(P(None, None, ("sec", "gy"), "gx"), P(None, ("sec", "gy", "gx"), None)),
        check_vma=False,
    )
```

```python
import functools
import math

import jax
import jax.numpy as jnp
from jax import lax
from jax.experimental import pallas as pl
from jax.experimental.pallas import tpu as pltpu
from jax.sharding import PartitionSpec as P

ITERS = 4
GRAVITY_STEP = 0.3
CORIOLIS_STEP = 0.2
STRESS_GAIN = 2.0
TURN_GAIN = 0.2
SPEED_BASE = 0.35
SPEED_RATIO = 0.9

NDIR = 36
NFREQ = 20
ROWS = 16
LANES = 128
CELLS = NDIR * NFREQ * ROWS
PER_DIR = NFREQ * ROWS
QUARTER = NDIR // 4
PAD = 8
DURING_STRESS = 5
CHUNKS = 8
LOADS = 3
VMEM_LIMIT = 28 * 1024 * 1024
HALF = NDIR // 2 * NFREQ
PEERS = 8
SLOTS = 16
MARGIN_O = 24
MARGIN_W = 16
SPEEDS = [SPEED_BASE * SPEED_RATIO**j for j in range(NFREQ)]
STEP_ANGLE = 2.0 * math.pi / NDIR
MESH = pl.DeviceIdType.MESH
AROUND = [(1, 0), (-1, 0), (0, 1), (0, -1), (1, 1), (1, -1), (-1, 1), (-1, -1)]


def iota(shape, dim):
    return lax.broadcasted_iota(jnp.int32, shape, dim)


def next_angle(cosine, sine):
    turn_c, turn_s = math.cos(STEP_ANGLE), math.sin(STEP_ANGLE)
    return cosine * turn_c - sine * turn_s, sine * turn_c + cosine * turn_s


def angle_at(i):
    return jnp.float32(math.cos((i + 0.5) * STEP_ANGLE)), jnp.float32(math.sin((i + 0.5) * STEP_ANGLE))


def exact_dot(values, weights):
    rows = values.shape[0]
    high = values.astype(jnp.bfloat16)
    rest = values - high.astype(jnp.float32)
    middle = rest.astype(jnp.bfloat16)
    low = (rest - middle.astype(jnp.float32)).astype(jnp.bfloat16)
    stacked = jnp.concatenate([high, middle, low], axis=0)
    product = jnp.dot(stacked, weights, preferred_element_type=jnp.float32)
    return product[:rows] + product[rows : 2 * rows] + product[2 * rows :]


def ocean_shift(values, amount):
    return pltpu.roll(values, amount % values.shape[1], 1)


def along_x(values):
    return (ocean_shift(values, -1) - ocean_shift(values, 1)) * 0.5


def along_y(classes):
    above = [classes[1], classes[2], pltpu.roll(classes[0], SLOTS - 1, 0)]
    below = [pltpu.roll(classes[2], 1, 0), classes[0], classes[1]]
    return [(above[c] - below[c]) * 0.5 for c in range(3)]


def wave_tools(fields, rows, cols, cells, beside, target):
    lane = iota((8, LANES), 1)
    row = iota((8, LANES), 0)

    def half(n, h):
        return fields[ROWS * n + 8 * h : ROWS * n + 8 * h + 8, :]

    def turn_part(h):
        return half(2, h) * jnp.abs(half(0, h))

    def cell(direction, j, offset):
        place = direction * PER_DIR + (PAD + j * ROWS + offset)
        return cells[pl.ds(pl.multiple_of(place, 8) if offset % 8 == 0 else place, 8), :]

    odd = lax.rem(lane, 2) == 1

    def rims(i, h):
        columns = []
        for place in (i, QUARTER + i):
            group, part = place // 3, lax.rem(place, 3)
            span = slice(8 * h, 8 * h + 8)
            merged = jnp.where(odd, cols[0, group, span, :], cols[1, group, span, :])
            columns.append(pltpu.roll(merged, lax.rem(LANES - part * (2 * NFREQ), LANES), 1))
        return columns

    def rim_at(columns, j):
        return [pltpu.roll(column, LANES - 1 - 2 * j, 1) for column in columns]

    def prepare(i, h, j, columns, rim):
        following = rim_at(columns, j + 1)
        for q in range(4):
            value = cell(q * QUARTER + i, j, 8 * h)
            if q in (0, 3):
                moved = jnp.where(lane == 0, rim[q // 2], pltpu.roll(value, 1, 1))
            else:
                moved = jnp.where(lane == LANES - 1, following[q // 2], pltpu.roll(value, LANES - 1, 1))
            beside[q * NFREQ + j, 8 * h : 8 * h + 8, :] = moved
        return following

    def update(i, angle):
        cosine, sine = angle
        following_step = jnp.minimum(i + 1, QUARTER - 1)
        for h in range(2):
            columns = rims(following_step, h)
            rim = rim_at(columns, 0)
            turn_left = half(0, h) > 0.0
            shift_up = half(1, h) > 0.0
            mask = half(2, h)
            turned = turn_part(h)
            stay = mask - turned
            shifted = mask * half(1, h)
            leave = mask * (cosine + sine)
            factors = []
            for q in range(4):
                speed_x, speed_y = (cosine, sine) if q % 2 == 0 else (sine, cosine)
                inner = half(5 if q in (0, 1) else 6, h) * speed_y
                if q in (0, 1) and h == 0:
                    inner = jnp.where(row == 0, 0.0, inner)
                if q in (2, 3) and h == 1:
                    inner = jnp.where(row == 7, 0.0, inner)
                factors.append((half(3 if q in (0, 3) else 4, h) * speed_x, inner))
            values = [cell(q * QUARTER + i, 0, 8 * h) for q in range(4)]
            faces = [None] * 4
            for j in range(NFREQ):
                keep = stay - SPEEDS[j] * leave
                for q in range(4):
                    direction = q * QUARTER + i
                    before, after = direction - 1, direction + 1
                    if q == 0:
                        before = jnp.where(i == 0, NDIR - 1, before)
                    if q == 3:
                        after = jnp.where(i == QUARTER - 1, 0, after)
                    along = cell(direction, j, 8 * h + (-1 if q in (0, 1) else 1))
                    moved = factors[q][0] * beside[q * NFREQ + j, 8 * h : 8 * h + 8, :] + factors[q][1] * along
                    total = keep * values[q] + SPEEDS[j] * moved
                    total = total + turned * jnp.where(turn_left, cell(before, j, 8 * h), cell(after, j, 8 * h))
                    if j > 0:
                        total = total + faces[q]
                    if j < NFREQ - 1:
                        following = cell(direction, j + 1, 8 * h)
                        faces[q] = shifted * jnp.where(shift_up, values[q], following)
                        total = total - faces[q]
                        values[q] = following
                    place = (direction * NFREQ + j) * ROWS + 8 * h
                    target[pl.ds(pl.multiple_of(place, 8), 8), :] = total
                rim = prepare(following_step, h, j, columns, rim)

    def prepare_first():
        for h in range(2):
            columns = rims(0, h)
            rim = rim_at(columns, 0)
            for j in range(NFREQ):
                rim = prepare(0, h, j, columns, rim)

    def finish_rows(i, angle):
        for q in range(4):
            speed_y = angle[1] if q % 2 == 0 else angle[0]
            from_south = q in (0, 1)
            edge = (5 * ROWS) if from_south else (7 * ROWS - 1)
            factor = fields[edge : edge + 1, :] * speed_y
            direction = q * QUARTER + i
            source = (direction if from_south else direction - 2 * QUARTER) * NFREQ
            for first in (0, 8, 16):
                count = min(8, NFREQ - first)
                speeds = jnp.zeros((count, LANES), jnp.float32)
                for r in range(count):
                    speeds = jnp.where(row[:count] == r, SPEEDS[first + r], speeds)
                span = pl.ds((direction * NFREQ + first) * ROWS + (0 if from_south else ROWS - 1), count, stride=ROWS)
                rim = rows[0 if from_south else 1, pl.ds(source + first, count), :]
                target[span, :] = target[span, :] + speeds * (factor * rim)

    return prepare_first, update, finish_rows


def coupled_kernel(
    groups_y,
    groups,
    spectrum,
    sea_mask,
    ocean_state,
    depth,
    ocean_out,
    updated,
    fields_out,
    rows_out,
    cols_out,
    cells,
    beside,
    state_in,
    depth_in,
    mask_in,
    raw,
    raw_mask,
    pack,
    pack_late,
    window,
    window_late,
    mask_window,
    turn_window,
    beside_send,
    across_send,
    beside_land,
    across_land,
    stress,
    result,
    result_send,
    result_land,
    rows_send,
    cols_send,
    input_sem,
    load_sem,
    pack_sem,
    late_sem,
    band_sem,
    stress_sem,
    result_sem,
    halo_sem,
    local_sem,
):
    x = lax.axis_index("gx")
    y = lax.axis_index("sec") * groups_y + lax.axis_index("gy")

    def exists(dy, dx):
        checks = []
        if dy > 0:
            checks.append(y < groups - 1)
        if dy < 0:
            checks.append(y > 0)
        if dx > 0:
            checks.append(x < PEERS - 1)
        if dx < 0:
            checks.append(x > 0)
        answer = checks[0]
        for check in checks[1:]:
            answer = jnp.logical_and(answer, check)
        return answer

    def device_at(row, column):
        return (row // groups_y, lax.rem(row, groups_y), column)

    def device(dy, dx):
        return device_at(y + dy, x + dx)

    def peer(step):
        return (lax.axis_index("sec"), lax.axis_index("gy"), lax.rem(x + step, PEERS))

    inputs = [
        pltpu.make_async_copy(ocean_state, state_in, input_sem.at[0]),
        pltpu.make_async_copy(depth, depth_in, input_sem.at[1]),
        pltpu.make_async_copy(sea_mask, mask_in, input_sem.at[2]),
    ]
    for copy in inputs:
        copy.start()

    barrier = pltpu.get_barrier_semaphore()
    for step in range(1, PEERS):
        pl.semaphore_signal(barrier, inc=1, device_id=peer(step), device_id_type=MESH)
    greeted = PEERS - 1
    for dy, dx in AROUND:
        if dy != 0:
            here = exists(dy, dx)

            @pl.when(here)
            def _():
                pl.semaphore_signal(barrier, inc=1, device_id=device(dy, dx), device_id_type=MESH)

            greeted = greeted + here.astype(jnp.int32)

    def load(q, part):
        size = QUARTER // LOADS * PER_DIR
        start = pl.multiple_of(q * (QUARTER * PER_DIR) + part * size, PER_DIR)
        return pltpu.make_async_copy(
            spectrum.at[pl.ds(start, size)],
            cells.at[pl.ds(pl.multiple_of(start + PAD, 8), size)],
            load_sem.at[part * 4 + q],
        )

    for part in range(LOADS):
        for q in range(4):
            load(q, part).start()

    raw[...] = jnp.zeros_like(raw)
    raw_mask[...] = jnp.zeros_like(raw_mask)
    width = state_in.shape[2]
    for copy in inputs:
        copy.wait()
    raw[0:3, :width] = state_in[1]
    raw[3:6, :width] = state_in[2]
    raw[8:11, :width] = state_in[0]
    raw[11:14, :width] = depth_in[...]
    raw_mask[6:8, : mask_in.shape[1]] = mask_in[...].astype(jnp.float32)
    even = ocean_shift(raw[...], MARGIN_O)
    odd = ocean_shift(raw[...], MARGIN_O - 64)
    mask_rows = ocean_shift(raw_mask[...], MARGIN_W)
    is_ocean = iota((8, LANES), 0) < 6
    for dest in range(PEERS):
        source = odd if dest % 2 else even
        origin = 384 * (dest // 2) + (128 if dest % 2 else 0)
        for tile in range(2):
            piece = source[:, origin + LANES * tile : origin + LANES * (tile + 1)]
            pack[dest, tile] = jnp.where(
                is_ocean, piece[:8], mask_rows[:, LANES * (dest + tile) : LANES * (dest + tile + 1)]
            )
            pack_late[dest, tile] = piece[8:]

    slot = pl.ds(pl.multiple_of(x * 8, 8), 8)

    def pack_copy(step, late):
        dest = peer(step)
        return pltpu.make_async_remote_copy(
            src_ref=(pack_late if late else pack).at[dest[2]],
            dst_ref=(window_late if late else window).at[:, slot, :],
            send_sem=(late_sem if late else pack_sem).at[0, step],
            recv_sem=(late_sem if late else pack_sem).at[1, step],
            device_id=dest,
            device_id_type=MESH,
        )

    pl.semaphore_wait(barrier, greeted)
    for step in range(1, PEERS):
        pack_copy(step, False).start()
    for step in range(1, PEERS):
        pack_copy(step, True).start()
    mask_window[...] = jnp.zeros_like(mask_window)
    cells[:PAD, :] = jnp.zeros((PAD, LANES), jnp.float32)
    cells[PAD + CELLS :, :] = jnp.zeros((PAD, LANES), jnp.float32)
    for ref in (window, window_late):
        ref[:, 11 * 8 : 13 * 8, :] = jnp.zeros((2, 16, LANES), jnp.float32)
    edge = jnp.zeros((2, 24, LANES), jnp.float32)

    @pl.when(y == 0)
    def _():
        window[:, 13 * 8 : 16 * 8, :] = edge
        window_late[:, 13 * 8 : 16 * 8, :] = edge
        across_land[:, 1] = jnp.zeros((3, 4, 8, LANES), jnp.float32)

    @pl.when(y == groups - 1)
    def _():
        window[:, 8 * 8 : 11 * 8, :] = edge
        window_late[:, 8 * 8 : 11 * 8, :] = edge
        across_land[:, 0] = jnp.zeros((3, 4, 8, LANES), jnp.float32)

    @pl.when(x == 0)
    def _():
        beside_land[1] = jnp.zeros((5, ROWS, LANES), jnp.float32)
        across_land[2] = jnp.zeros((2, 4, 8, LANES), jnp.float32)

    @pl.when(x == PEERS - 1)
    def _():
        beside_land[0] = jnp.zeros((5, ROWS, LANES), jnp.float32)
        across_land[1] = jnp.zeros((2, 4, 8, LANES), jnp.float32)

    window[:, slot, :] = pack[x]
    window_late[:, slot, :] = pack_late[x]

    lane = iota((ROWS, LANES), 1)
    row = iota((ROWS, LANES), 0)
    zero = jnp.zeros((ROWS, LANES), jnp.float32)

    def gather(i, carry):
        (cosine, sine), plain, fluxes = carry
        part = QUARTER // LOADS

        @pl.when(lax.rem(i, part) == 0)
        def _():
            for q in range(4):
                load(q, i // part).wait()

        totals, weighted, rims = [None] * 4, [None] * 4, [zero, zero]
        for j in range(NFREQ):
            values = []
            for q in range(4):
                base = (q * QUARTER + i) * PER_DIR + PAD
                values.append(cells[pl.ds(pl.multiple_of(base + j * ROWS, 8), ROWS), :])
                scaled = values[q] * SPEEDS[j]
                totals[q] = values[q] if j == 0 else totals[q] + values[q]
                weighted[q] = scaled if j == 0 else weighted[q] + scaled
            here = jnp.logical_or(lane == 2 * j + 1, lane == 2 * j + 2)
            for n, (east, west) in enumerate(((0, 1), (3, 2))):
                both = jnp.where(lane == LANES - 1, values[east], values[west])
                rims[n] = jnp.where(here, pltpu.roll(both, 2 * j + 2, 1), rims[n])
        for n in range(2):
            place = i + n * QUARTER
            group, part = place // 3, lax.rem(place, 3)
            earlier = jnp.where(part > 0, cols_send[group], zero)
            cols_send[group] = earlier + pltpu.roll(rims[n], part * (2 * NFREQ), 1)
        scale = 0.5 / (NDIR * NFREQ)
        cc, cs, ss = cosine * cosine * scale, cosine * sine * scale, sine * sine * scale
        pair = (totals[0] + totals[2]) - (totals[1] + totals[3])
        plain = (
            plain[0] + ((totals[0] + totals[2]) + (totals[1] + totals[3])),
            plain[1] + (cc - ss) * pair,
            plain[2] + (2.0 * cs) * pair,
        )
        straight, crossed = (cc, cs, ss), (ss, -cs, cc)
        west, east, south, north = fluxes
        west = tuple(
            west[s] + (cosine * straight[s]) * weighted[0] + (sine * crossed[s]) * weighted[3] for s in range(3)
        )
        east = tuple(
            east[s] + (cosine * straight[s]) * weighted[2] + (sine * crossed[s]) * weighted[1] for s in range(3)
        )
        south = tuple(
            south[s] + (sine * straight[s]) * weighted[0] + (cosine * crossed[s]) * weighted[1] for s in range(3)
        )
        north = tuple(
            north[s] + (sine * straight[s]) * weighted[2] + (cosine * crossed[s]) * weighted[3] for s in range(3)
        )
        return next_angle(cosine, sine), plain, (west, east, south, north)

    cols_send[...] = jnp.zeros_like(cols_send)
    triple = (zero, zero, zero)
    carry = (angle_at(0), triple, (triple, triple, triple, triple))
    _, plain, fluxes = lax.fori_loop(0, QUARTER, gather, carry)

    def pack_rows(n, carry):
        for m in range(5):
            start = n * 40 + m * 8
            span = pl.ds(pl.multiple_of(start, 8), 8)
            rows_send[0, span, :] = cells[pl.ds(start * ROWS + (PAD + ROWS - 1), 8, stride=ROWS), :]
            rows_send[1, span, :] = cells[pl.ds(start * ROWS + (PAD + HALF * ROWS), 8, stride=ROWS), :]
        return carry

    lax.fori_loop(0, HALF // 40, pack_rows, 0)

    sends = (exists(0, 1), exists(0, -1), exists(1, 0), exists(-1, 0))
    receives = (exists(0, -1), exists(0, 1), exists(-1, 0), exists(1, 0))

    def halo_ends(n):
        return (cols_send, cols_out.at[n]) if n < 2 else (rows_send.at[n - 2], rows_out.at[n - 2])

    def halo_copy(n):
        source, target = halo_ends(n)
        return pltpu.make_async_remote_copy(
            src_ref=source,
            dst_ref=target,
            send_sem=halo_sem.at[0, n],
            recv_sem=halo_sem.at[1, n],
            device_id=(device(0, 1), device(0, -1), device(1, 0), device(-1, 0))[n],
            device_id_type=MESH,
        )

    def halo_fill(n):
        source, target = halo_ends(n)
        return pltpu.make_async_copy(source, target, local_sem.at[n])

    def start_halo(n):
        @pl.when(sends[n])
        def _():
            halo_copy(n).start()

        @pl.when(jnp.logical_not(receives[n]))
        def _():
            halo_fill(n).start()

    def wait_halo(n):
        @pl.when(receives[n])
        def _():
            halo_copy(n).wait_recv()

        @pl.when(jnp.logical_not(receives[n]))
        def _():
            halo_fill(n).wait()

    start_halo(0)
    start_halo(1)

    for step in range(1, PEERS):
        pack_copy(step, False).wait_recv()

    def band_copy(n, late):
        source = pl.ds((5 if n == 0 else 0) * 8, 24)
        target = pl.ds((13 if n == 0 else 8) * 8, 24)
        ref = window_late if late else window
        return pltpu.make_async_remote_copy(
            src_ref=ref.at[:, source, :],
            dst_ref=ref.at[:, target, :],
            send_sem=band_sem.at[0, 2 * n + late],
            recv_sem=band_sem.at[1, 2 * n + late],
            device_id=device(1 if n == 0 else -1, 0),
            device_id_type=MESH,
        )

    vertical = (exists(1, 0), exists(-1, 0))
    from_side = (exists(-1, 0), exists(1, 0))
    for n in range(2):

        @pl.when(vertical[n])
        def _():
            band_copy(n, 0).start()

    def tiles_of(ref, rows):
        return jnp.concatenate([ref[t, rows, :] for t in range(2)], axis=1)

    def own_rows(first):
        return tiles_of(window, pl.ds(first, 8, stride=8))

    wide = (2 * LANES, 2 * LANES)
    spread = (iota(wide, 0) == (2 * iota(wide, 1)) // 3).astype(jnp.bfloat16)
    wave_masks = [own_rows(6), own_rows(7)]
    masks = jnp.dot(
        jnp.concatenate(wave_masks, axis=0).astype(jnp.bfloat16), spread, preferred_element_type=jnp.float32
    )
    near_mask = [masks[:8], masks[:8], masks[8:]]

    def restriction(width):
        fine, wave = iota((2 * LANES, width), 0), iota((2 * LANES, width), 1)
        wave = jnp.where(wave < 3 * LANES // 2, wave, wave - 2 * LANES) + MARGIN_W
        group = 3 * (wave // 2)
        ends = jnp.where(wave % 2 == 0, group, group + 2)
        return jnp.where(fine == ends, 2.0, jnp.where(fine == group + 1, 1.0, 0.0)).astype(jnp.bfloat16)

    near_east = [own_rows(c) * near_mask[c] for c in range(3)]
    near_north = [own_rows(3 + c) * near_mask[c] for c in range(3)]
    near_slope = [
        (near_east[1] - pltpu.roll(near_east[2], 1, 0)) * 0.5,
        (near_east[2] - near_east[0]) * 0.5,
        (pltpu.roll(near_east[0], 7, 0) - near_east[1]) * 0.5,
    ]
    vorticity = [along_x(near_north[c]) - near_slope[c] for c in range(3)]
    coarse = jnp.concatenate([2.0 * vorticity[0] + vorticity[1], vorticity[1] + 2.0 * vorticity[2]], axis=0)
    coarse = TURN_GAIN * jnp.tanh(exact_dot(coarse, restriction(LANES)) * (1.0 / 9.0))
    for c in range(2):
        turn_window[0, pl.ds(c, 8, stride=2), :] = coarse[8 * c : 8 * c + 8]
        placed = ocean_shift(wave_masks[c], -MARGIN_W)
        for t in range(2):
            mask_window[t, pl.ds(c, 8, stride=2), :] = placed[:, LANES * t : LANES * (t + 1)]

    def mask_products():
        around = tiles_of(mask_window, slice(None))
        return (
            around,
            around * pltpu.roll(around, 1, 1),
            around * pltpu.roll(around, 2 * LANES - 1, 1),
            around * pltpu.roll(around, 1, 0),
            around * pltpu.roll(around, 2 * ROWS - 1, 0),
        )

    near_products = [values[:ROWS, :LANES] for values in mask_products()]

    inside = jnp.logical_and(row > 0, row < ROWS - 1)
    turning = jnp.where(inside, turn_window[0, :ROWS, :], 0.0)
    turn_abs = jnp.abs(turning)
    scale = 0.25 / (NDIR * NFREQ)
    base, along, across = plain[0] * scale, plain[1] * 0.5, plain[2] * 0.5
    turn_c, turn_s = math.cos(2.0 * STEP_ANGLE), math.sin(2.0 * STEP_ANGLE)
    plain_along, plain_across = along, across
    signed = jnp.where(turning > 0.0, turn_s, -turn_s)
    along_turn = along * turn_c - across * signed
    across_turn = across * turn_c + along * signed
    stay = 1.0 - turn_abs
    along = stay * along + turn_abs * along_turn
    across = stay * across + turn_abs * across_turn
    local = [base + along, across, base - along]
    west, east, south, north = fluxes
    rims = zero
    for s in range(3):
        partial = near_products[0] * (local[s] - ((west[s] + east[s]) + (south[s] + north[s])))
        partial = partial + near_products[1] * jnp.where(lane == 0, 0.0, pltpu.roll(west[s], 1, 1))
        partial = partial + near_products[2] * jnp.where(lane == LANES - 1, 0.0, pltpu.roll(east[s], LANES - 1, 1))
        partial = partial + near_products[3] * jnp.where(row == 0, 0.0, pltpu.roll(south[s], 1, 0))
        partial = partial + near_products[4] * jnp.where(row == ROWS - 1, 0.0, pltpu.roll(north[s], ROWS - 1, 0))
        beside_send[s] = partial
        across_send[0, s] = partial[8:]
        across_send[0, s, 0:1, :] = south[s][ROWS - 1 :]
        across_send[1, s] = partial[:8]
        across_send[1, s, 7:8, :] = north[s][:1]
        beside_send[4, s : s + 1, :] = south[s][ROWS - 1 :]
        beside_send[4, 8 + s : 9 + s, :] = north[s][:1]
        rims = jnp.where(lane == LANES - 1 - s, pltpu.roll(west[s], (LANES - s) % LANES, 1) if s else west[s], rims)
        rims = jnp.where(lane == s, pltpu.roll(east[s], s, 1) if s else east[s], rims)
    for n, values in enumerate((plain_along, plain_across)):
        across_send[0, n, 1:2, :] = values[ROWS - 1 :]
        across_send[1, n, 6:7, :] = values[:1]
        beside_send[4, 3 + n : 4 + n, :] = values[ROWS - 1 :]
        beside_send[4, 11 + n : 12 + n, :] = values[:1]
    beside_send[3] = rims
    across_send[0, 3] = rims[8:]
    across_send[1, 3] = rims[:8]

    def stress_copy(n):
        dy, dx = AROUND[n]
        if dy == 0:
            source, target = beside_send, beside_land.at[{1: 1, -1: 0}[dx]]
        else:
            source = across_send.at[{1: 0, -1: 1}[dy]]
            target = across_land.at[{0: 0, 1: 2, -1: 1}[dx], {1: 1, -1: 0}[dy]]
        return pltpu.make_async_remote_copy(
            src_ref=source,
            dst_ref=target,
            send_sem=stress_sem.at[0, n],
            recv_sem=stress_sem.at[1, n],
            device_id=device(dy, dx),
            device_id_type=MESH,
        )

    for n, (dy, dx) in enumerate(AROUND):

        @pl.when(exists(dy, dx))
        def _():
            stress_copy(n).start()

    for step in range(1, PEERS):
        pack_copy(step, True).wait_recv()
    for n in range(2):

        @pl.when(vertical[n])
        def _():
            band_copy(n, 1).start()

    start_halo(2)
    start_halo(3)
    for n in range(2):

        @pl.when(from_side[n])
        def _():
            band_copy(n, 0).wait_recv()

    def all_rows(ref, first):
        return tiles_of(ref, pl.ds(first, SLOTS, stride=8))

    far_masks = [all_rows(window, 6), all_rows(window, 7)]
    masks = jnp.dot(
        jnp.concatenate(far_masks, axis=0).astype(jnp.bfloat16), spread, preferred_element_type=jnp.float32
    )
    ocean_mask = [masks[:SLOTS], masks[:SLOTS], masks[SLOTS:]]
    eastward = [all_rows(window, c) * ocean_mask[c] for c in range(3)]
    northward = [all_rows(window, 3 + c) * ocean_mask[c] for c in range(3)]
    east_y, north_y = along_y(eastward), along_y(northward)
    vorticity = [along_x(northward[c]) - east_y[c] for c in range(3)]
    divergence = [along_x(eastward[c]) + north_y[c] for c in range(3)]
    coarse = []
    for values in (vorticity, divergence):
        coarse.append(2.0 * values[0] + values[1])
        coarse.append(values[1] + 2.0 * values[2])
    coarse = exact_dot(jnp.concatenate(coarse, axis=0), restriction(2 * LANES)) * (1.0 / 9.0)
    coarse = TURN_GAIN * jnp.tanh(coarse)
    for c in range(2):
        placed = ocean_shift(far_masks[c], -MARGIN_W)
        for t in range(2):
            span = slice(LANES * t, LANES * (t + 1))
            mask_window[t, pl.ds(c, SLOTS, stride=2), :] = placed[:, span]
            turn_window[t, pl.ds(c, SLOTS, stride=2), :] = coarse[SLOTS * c : SLOTS * (c + 1), span]
        fields_out[pl.ds(ROWS + c, 8, stride=2), :] = coarse[SLOTS * (2 + c) : SLOTS * (2 + c) + 8, :LANES]
    fields_out[:ROWS, :] = turn_window[0, :ROWS, :]
    products = mask_products()
    for n, values in enumerate(products):
        fields_out[(2 + n) * ROWS : (3 + n) * ROWS, :] = values[:ROWS, :LANES]
    around, west_mask, east_mask, south_mask, north_mask = products

    prepare_first, update, finish_rows = wave_tools(fields_out, rows_out, cols_out, cells, beside, updated)
    for n in range(2):
        wait_halo(n)
    prepare_first()

    def one_step(i, angle):
        update(i, angle)
        return next_angle(*angle)

    angle = lax.fori_loop(0, DURING_STRESS, one_step, angle_at(0))

    for n in range(2):

        @pl.when(from_side[n])
        def _():
            band_copy(n, 1).wait_recv()

    surface = [all_rows(window_late, c) * ocean_mask[c] for c in range(3)]
    bottom = [all_rows(window_late, 3 + c) for c in range(3)]
    safe = [jnp.where(bottom[c] > 0.0, bottom[c], 1.0) for c in range(3)]
    inverse = [-STRESS_GAIN / safe[c] for c in range(3)]

    def raise_surface(surface, eastward, northward):
        flow_y = along_y([bottom[c] * northward[c] for c in range(3)])
        return [
            (surface[c] - GRAVITY_STEP * (along_x(bottom[c] * eastward[c]) + flow_y[c])) * ocean_mask[c]
            for c in range(3)
        ]

    def push(surface, eastward, northward):
        slope = along_y(surface)
        new_east = [
            eastward[c] + GRAVITY_STEP * (CORIOLIS_STEP * northward[c] - along_x(surface[c])) for c in range(3)
        ]
        new_north = [northward[c] + GRAVITY_STEP * (-CORIOLIS_STEP * eastward[c] - slope[c]) for c in range(3)]
        return new_east, new_north

    surface = raise_surface(surface, eastward, northward)
    pushed = push(surface, eastward, northward)
    wave_lane, fine = iota(wide, 0), iota(wide, 1)
    wave_lane = jnp.where(wave_lane < LANES + 64, wave_lane + MARGIN_W, wave_lane - 2 * LANES + MARGIN_W)
    first = 2 * (fine // 3)
    part = fine % 3
    hits = jnp.where(wave_lane == first, 1.0, 0.0) * jnp.where(part == 0, 1.0, jnp.where(part == 1, 0.5, 0.0)) + jnp.where(
        wave_lane == first + 1, 1.0, 0.0
    ) * jnp.where(part == 2, 1.0, jnp.where(part == 1, 0.5, 0.0))
    prolong = hits.astype(jnp.bfloat16)

    for n, (dy, dx) in enumerate(AROUND):

        @pl.when(exists(-dy, -dx))
        def _():
            stress_copy(n).wait_recv()

    side_lane = iota((2 * ROWS, LANES), 1) < 64

    def assemble(s):
        columns = [
            jnp.concatenate([body, across_land[n, 0, s], across_land[n, 1, s]], axis=0)
            for n, body in enumerate((beside_send[s], beside_land[0, s], beside_land[1, s]))
        ]
        return jnp.concatenate([columns[0], jnp.where(side_lane, columns[1], columns[2])], axis=1)

    def edge_row(place):
        rows = [ref[place : place + 1, :] for ref in (beside_send.at[4], beside_land.at[0, 4], beside_land.at[1, 4])]
        return jnp.concatenate([rows[0], jnp.where(side_lane[:1], rows[1], rows[2])], axis=1)

    around_row = iota((2 * ROWS, 2 * LANES), 0)
    around_lane = iota((2 * ROWS, 2 * LANES), 1)
    west_side = west_mask * jnp.where(around_lane % LANES == 0, 1.0, 0.0)
    east_side = east_mask * jnp.where(around_lane % LANES == LANES - 1, 1.0, 0.0)
    side_flux = assemble(3)
    pieces = []
    bodies = [assemble(s) for s in range(3)]

    def edge_rows(n):
        low, high = edge_row(11 + n), edge_row(3 + n)
        values = jnp.where(around_row == 0, low, jnp.where(around_row == ROWS - 1, high, 0.0))
        values = jnp.where(around_row == ROWS, bodies[n][22:23], values)
        return jnp.where(around_row == 2 * ROWS - 1, bodies[n][25:26], values)

    edge_along, edge_across = edge_rows(0), edge_rows(1)
    edge_turn = tiles_of(turn_window, slice(None))
    edge_signed = jnp.where(edge_turn > 0.0, turn_s, -turn_s)
    edge_scale = around * jnp.abs(edge_turn)
    along_change = edge_scale * (edge_along * (turn_c - 1.0) - edge_across * edge_signed)
    across_change = edge_scale * (edge_across * (turn_c - 1.0) + edge_along * edge_signed)
    changes = (along_change, across_change, -along_change)
    for s in range(3):
        body = bodies[s] + changes[s]
        from_south = jnp.where(
            around_row == 0, bodies[s][24:25], jnp.where(around_row == ROWS, edge_row(s), 0.0)
        )
        from_north = jnp.where(
            around_row == ROWS - 1, bodies[s][23:24], jnp.where(around_row == 2 * ROWS - 1, edge_row(8 + s), 0.0)
        )
        body = body + west_side * pltpu.roll(side_flux, s + 1, 1)
        body = body + east_side * pltpu.roll(side_flux, 2 * LANES - 1 - s, 1)
        body = body + south_mask * from_south + north_mask * from_north
        for t in range(2):
            stress[s, t] = body[:, LANES * t : LANES * (t + 1)]
        for c in range(2):
            pieces.append(
                jnp.concatenate([stress[s, t, pl.ds(c, SLOTS, stride=2), :] for t in range(2)], axis=1)
            )
    spread_stress = exact_dot(jnp.concatenate(pieces, axis=0), prolong)
    tensor = []
    for s in range(3):
        low = spread_stress[2 * SLOTS * s : 2 * SLOTS * s + SLOTS]
        high = spread_stress[2 * SLOTS * s + SLOTS : 2 * SLOTS * (s + 1)]
        tensor.append([low, 0.5 * low + 0.5 * high, high])
    cross_y, normal_y = along_y(tensor[1]), along_y(tensor[2])
    force_x = [inverse[c] * (along_x(tensor[0][c]) + cross_y[c]) for c in range(3)]
    force_y = [inverse[c] * (along_x(tensor[1][c]) + normal_y[c]) for c in range(3)]

    for step in range(ITERS):
        if step > 0:
            surface = raise_surface(surface, eastward, northward)
            pushed = push(surface, eastward, northward)
        eastward = [(pushed[0][c] + force_x[c]) * ocean_mask[c] for c in range(3)]
        northward = [(pushed[1][c] + force_y[c]) * ocean_mask[c] for c in range(3)]

    is_even = lax.rem(x, 2) == 0
    low_lanes = iota((8, LANES), 1) < 64
    halves = []
    for f, values in enumerate((surface, eastward, northward)):
        for c in range(3):
            own = values[c][:8]
            low, high = ocean_shift(own, -MARGIN_O), ocean_shift(own, 64 - MARGIN_O)
            place = 8 * (3 * f + c)
            result[place : place + 8, :] = jnp.where(is_even, low[:, :LANES], high[:, LANES:])
            halves.append(jnp.where(is_even, low[:, LANES:], pltpu.roll(high[:, :LANES], 64, 1)))
    for m in range(5):
        merged = halves[m] if m == 4 else jnp.where(low_lanes, halves[m], pltpu.roll(halves[5 + m], 64, 1))
        result[72 + 8 * m : 80 + 8 * m, :] = merged
    for dest in range(PEERS):
        result_send[dest, 0:8, :] = result[pl.ds(dest, 8, stride=8), :]
        result_send[dest, 8:14, :] = result[pl.ds(64 + dest, 6, stride=8), :]

    def result_copy(step):
        dest = peer(step)
        return pltpu.make_async_remote_copy(
            src_ref=result_send.at[dest[2]],
            dst_ref=result_land.at[x],
            send_sem=result_sem.at[0, step],
            recv_sem=result_sem.at[1, step],
            device_id=dest,
            device_id_type=MESH,
        )

    for step in range(1, PEERS):
        result_copy(step).start()
    result_land[x] = result_send[x]
    lax.fori_loop(DURING_STRESS, QUARTER, one_step, angle)
    for step in range(1, PEERS):
        result_copy(step).wait_recv()
    for q in range(PEERS // 2):
        left, right = result_land[2 * q], result_land[2 * q + 1]
        left_turned, right_turned = pltpu.roll(left, 64, 1), pltpu.roll(right, 64, 1)
        side = iota((5, LANES), 1) < 64
        middle = jnp.concatenate(
            [
                jnp.where(side, left[9:14], right_turned[9:14]),
                jnp.where(side[:4], left_turned[9:13], right[9:13]),
            ],
            axis=0,
        )
        for t, tile in enumerate((left, middle, right)):
            lanes = pl.ds((3 * q + t) * LANES, LANES)
            for f in range(3):
                ocean_out[f, :, lanes] = tile[3 * f : 3 * f + 3]

    for step in range(1, PEERS):
        pack_copy(step, False).wait_send()
        pack_copy(step, True).wait_send()
        result_copy(step).wait_send()
    for n in range(2):

        @pl.when(vertical[n])
        def _():
            band_copy(n, 0).wait_send()
            band_copy(n, 1).wait_send()

    for n, (dy, dx) in enumerate(AROUND):

        @pl.when(exists(dy, dx))
        def _():
            stress_copy(n).wait_send()

    for n in range(2, 4):
        wait_halo(n)

    def fix_step(i, angle):
        finish_rows(i, angle)
        return next_angle(*angle)

    lax.fori_loop(0, QUARTER, fix_step, angle_at(0))
    for n in range(4):

        @pl.when(sends[n])
        def _():
            halo_copy(n).wait_send()


def hand_over(ocean_in, updated, out, ocean_out, store_sem, local_sem):
    handed = pltpu.make_async_copy(ocean_in, ocean_out, local_sem)
    handed.start()
    size = CELLS // CHUNKS
    copies = [
        pltpu.make_async_copy(updated.at[pl.ds(n * size, size)], out.at[pl.ds(n * size, size)], store_sem.at[n])
        for n in range(CHUNKS)
    ]
    for copy in copies:
        copy.start()
    for copy in copies:
        copy.wait()
    handed.wait()


def shards(mesh_shape, spectrum, sea_mask, ocean_state, depth):
    groups_y = mesh_shape["gy"]
    groups = groups_y * mesh_shape["sec"]
    cells = spectrum.reshape(CELLS, LANES)
    vmem = pl.BlockSpec(memory_space=pltpu.VMEM)
    anywhere = pl.BlockSpec(memory_space=pl.ANY)
    f32 = jnp.float32
    dma = pltpu.SemaphoreType.DMA
    ocean_part, updated = pl.pallas_call(
        functools.partial(coupled_kernel, groups_y, groups),
        out_shape=(
            jax.ShapeDtypeStruct(ocean_state.shape, f32),
            jax.ShapeDtypeStruct((CELLS, LANES), f32),
        ),
        in_specs=[anywhere] * 4,
        out_specs=(vmem, vmem),
        scratch_shapes=[
            pltpu.VMEM((7 * ROWS, LANES), f32),
            pltpu.VMEM((2, HALF, LANES), f32),
            pltpu.VMEM((2, 6, ROWS, LANES), f32),
            pltpu.VMEM((CELLS + 2 * PAD, LANES), f32),
            pltpu.VMEM((4 * NFREQ, ROWS, LANES), f32),
            pltpu.VMEM(ocean_state.shape, f32),
            pltpu.VMEM(depth.shape, f32),
            pltpu.VMEM(sea_mask.shape, jnp.int32),
            pltpu.VMEM((SLOTS, 1792), f32),
            pltpu.VMEM((8, 1280), f32),
            pltpu.VMEM((PEERS, 2, 8, LANES), f32),
            pltpu.VMEM((PEERS, 2, 8, LANES), f32),
            pltpu.VMEM((2, SLOTS * 8, LANES), f32),
            pltpu.VMEM((2, SLOTS * 8, LANES), f32),
            pltpu.VMEM((2, 2 * ROWS, LANES), f32),
            pltpu.VMEM((2, 2 * ROWS, LANES), f32),
            pltpu.VMEM((5, ROWS, LANES), f32),
            pltpu.VMEM((2, 4, 8, LANES), f32),
            pltpu.VMEM((2, 5, ROWS, LANES), f32),
            pltpu.VMEM((3, 2, 4, 8, LANES), f32),
            pltpu.VMEM((3, 2, 2 * ROWS, LANES), f32),
            pltpu.VMEM((112, LANES), f32),
            pltpu.VMEM((PEERS, SLOTS, LANES), f32),
            pltpu.VMEM((PEERS, SLOTS, LANES), f32),
            pltpu.VMEM((2, HALF, LANES), f32),
            pltpu.VMEM((6, ROWS, LANES), f32),
            dma((3,)),
            dma((4 * LOADS,)),
            dma((2, PEERS)),
            dma((2, PEERS)),
            dma((2, 4)),
            dma((2, 8)),
            dma((2, PEERS)),
            dma((2, 4)),
            dma((4,)),
        ],
        compiler_params=pltpu.CompilerParams(
            collective_id=0, has_side_effects=True, vmem_limit_bytes=VMEM_LIMIT
        ),
        name="coupled",
    )(*[pltpu.with_memory_space_constraint(a, pltpu.HBM) for a in (cells, sea_mask, ocean_state, depth)])
    spectrum_out, ocean_out = pl.pallas_call(
        hand_over,
        out_shape=(jax.ShapeDtypeStruct((CELLS, LANES), f32), jax.ShapeDtypeStruct(ocean_state.shape, f32)),
        in_specs=[anywhere, anywhere],
        out_specs=(anywhere, anywhere),
        scratch_shapes=[dma((CHUNKS,)), dma],
        compiler_params=pltpu.CompilerParams(vmem_limit_bytes=VMEM_LIMIT),
        name="hand_over",
    )(ocean_part, updated)
    return (spectrum_out.reshape(spectrum.shape), ocean_out)


def solution(mesh):
    return jax.shard_map(
        functools.partial(shards, dict(mesh.shape)),
        mesh=mesh,
        in_specs=(
            P(None, None, ("sec", "gy"), "gx"),
            P(("sec", "gy", "gx"), None),
            P(None, ("sec", "gy", "gx"), None),
            P(("sec", "gy", "gx"), None),
        ),
        out_specs=(P(None, None, ("sec", "gy"), "gx"), P(None, ("sec", "gy", "gx"), None)),
        check_vma=False,
    )
```

```python
import functools
import math

import jax
import jax.numpy as jnp
from jax import lax
from jax.experimental import pallas as pl
from jax.experimental.pallas import tpu as pltpu
from jax.sharding import PartitionSpec as P

ITERS = 4
GRAVITY_STEP = 0.3
CORIOLIS_STEP = 0.2
STRESS_GAIN = 2.0
TURN_GAIN = 0.2
SPEED_BASE = 0.35
SPEED_RATIO = 0.9

NDIR = 36
NFREQ = 20
ROWS = 16
LANES = 128
CELLS = NDIR * NFREQ * ROWS
PER_DIR = NFREQ * ROWS
QUARTER = NDIR // 4
PAD = 8
DURING_STRESS = 2
CHUNKS = 8
LOADS = 3
VMEM_LIMIT = 28 * 1024 * 1024
HALF = NDIR // 2 * NFREQ
PEERS = 8
SLOTS = 16
MARGIN_O = 24
MARGIN_W = 16
SPEEDS = [SPEED_BASE * SPEED_RATIO**j for j in range(NFREQ)]
STEP_ANGLE = 2.0 * math.pi / NDIR
MESH = pl.DeviceIdType.MESH
AROUND = [(1, 0), (-1, 0), (0, 1), (0, -1), (1, 1), (1, -1), (-1, 1), (-1, -1)]


def iota(shape, dim):
    return lax.broadcasted_iota(jnp.int32, shape, dim)


def next_angle(cosine, sine):
    turn_c, turn_s = math.cos(STEP_ANGLE), math.sin(STEP_ANGLE)
    return cosine * turn_c - sine * turn_s, sine * turn_c + cosine * turn_s


def angle_at(i):
    return jnp.float32(math.cos((i + 0.5) * STEP_ANGLE)), jnp.float32(math.sin((i + 0.5) * STEP_ANGLE))


def exact_dot(values, weights):
    rows = values.shape[0]
    high = values.astype(jnp.bfloat16)
    rest = values - high.astype(jnp.float32)
    middle = rest.astype(jnp.bfloat16)
    low = (rest - middle.astype(jnp.float32)).astype(jnp.bfloat16)
    stacked = jnp.concatenate([high, middle, low], axis=0)
    product = jnp.dot(stacked, weights, preferred_element_type=jnp.float32)
    return product[:rows] + product[rows : 2 * rows] + product[2 * rows :]


def ocean_shift(values, amount):
    return pltpu.roll(values, amount % values.shape[1], 1)


def along_x(values):
    return (ocean_shift(values, -1) - ocean_shift(values, 1)) * 0.5


def along_y(classes):
    above = [classes[1], classes[2], pltpu.roll(classes[0], SLOTS - 1, 0)]
    below = [pltpu.roll(classes[2], 1, 0), classes[0], classes[1]]
    return [(above[c] - below[c]) * 0.5 for c in range(3)]


def wave_tools(fields, rows, cols, cells, beside, target):
    lane = iota((8, LANES), 1)
    row = iota((8, LANES), 0)

    def half(n, h):
        return fields[ROWS * n + 8 * h : ROWS * n + 8 * h + 8, :]

    def turn_part(h):
        return half(2, h) * jnp.abs(half(0, h))

    def cell(direction, j, offset):
        place = direction * PER_DIR + (PAD + j * ROWS + offset)
        return cells[pl.ds(pl.multiple_of(place, 8) if offset % 8 == 0 else place, 8), :]

    odd = lax.rem(lane, 2) == 1

    def rims(i, h):
        columns = []
        for place in (i, QUARTER + i):
            group, part = place // 3, lax.rem(place, 3)
            span = slice(8 * h, 8 * h + 8)
            merged = jnp.where(odd, cols[0, group, span, :], cols[1, group, span, :])
            columns.append(pltpu.roll(merged, lax.rem(LANES - part * (2 * NFREQ), LANES), 1))
        return columns

    def rim_at(columns, j):
        return [pltpu.roll(column, LANES - 1 - 2 * j, 1) for column in columns]

    def prepare(i, h, j, columns, rim):
        following = rim_at(columns, j + 1)
        for q in range(4):
            value = cell(q * QUARTER + i, j, 8 * h)
            if q in (0, 3):
                moved = jnp.where(lane == 0, rim[q // 2], pltpu.roll(value, 1, 1))
            else:
                moved = jnp.where(lane == LANES - 1, following[q // 2], pltpu.roll(value, LANES - 1, 1))
            beside[q * NFREQ + j, 8 * h : 8 * h + 8, :] = moved
        return following

    def update(i, angle):
        cosine, sine = angle
        following_step = jnp.minimum(i + 1, QUARTER - 1)
        for h in range(2):
            columns = rims(following_step, h)
            rim = rim_at(columns, 0)
            turn_left = half(0, h) > 0.0
            shift_up = half(1, h) > 0.0
            mask = half(2, h)
            turned = turn_part(h)
            stay = mask - turned
            shifted = mask * half(1, h)
            leave = mask * (cosine + sine)
            factors = []
            for q in range(4):
                speed_x, speed_y = (cosine, sine) if q % 2 == 0 else (sine, cosine)
                inner = half(5 if q in (0, 1) else 6, h) * speed_y
                if q in (0, 1) and h == 0:
                    inner = jnp.where(row == 0, 0.0, inner)
                if q in (2, 3) and h == 1:
                    inner = jnp.where(row == 7, 0.0, inner)
                factors.append((half(3 if q in (0, 3) else 4, h) * speed_x, inner))
            values = [cell(q * QUARTER + i, 0, 8 * h) for q in range(4)]
            faces = [None] * 4
            for j in range(NFREQ):
                keep = stay - SPEEDS[j] * leave
                for q in range(4):
                    direction = q * QUARTER + i
                    before, after = direction - 1, direction + 1
                    if q == 0:
                        before = jnp.where(i == 0, NDIR - 1, before)
                    if q == 3:
                        after = jnp.where(i == QUARTER - 1, 0, after)
                    along = cell(direction, j, 8 * h + (-1 if q in (0, 1) else 1))
                    moved = factors[q][0] * beside[q * NFREQ + j, 8 * h : 8 * h + 8, :] + factors[q][1] * along
                    total = keep * values[q] + SPEEDS[j] * moved
                    total = total + turned * jnp.where(turn_left, cell(before, j, 8 * h), cell(after, j, 8 * h))
                    if j > 0:
                        total = total + faces[q]
                    if j < NFREQ - 1:
                        following = cell(direction, j + 1, 8 * h)
                        faces[q] = shifted * jnp.where(shift_up, values[q], following)
                        total = total - faces[q]
                        values[q] = following
                    place = (direction * NFREQ + j) * ROWS + 8 * h
                    target[pl.ds(pl.multiple_of(place, 8), 8), :] = total
                rim = prepare(following_step, h, j, columns, rim)

    def prepare_first():
        for h in range(2):
            columns = rims(0, h)
            rim = rim_at(columns, 0)
            for j in range(NFREQ):
                rim = prepare(0, h, j, columns, rim)

    def finish_rows(i, angle):
        for q in range(4):
            speed_y = angle[1] if q % 2 == 0 else angle[0]
            from_south = q in (0, 1)
            edge = (5 * ROWS) if from_south else (7 * ROWS - 1)
            factor = fields[edge : edge + 1, :] * speed_y
            direction = q * QUARTER + i
            source = (direction if from_south else direction - 2 * QUARTER) * NFREQ
            for first in (0, 8, 16):
                count = min(8, NFREQ - first)
                speeds = jnp.zeros((count, LANES), jnp.float32)
                for r in range(count):
                    speeds = jnp.where(row[:count] == r, SPEEDS[first + r], speeds)
                span = pl.ds((direction * NFREQ + first) * ROWS + (0 if from_south else ROWS - 1), count, stride=ROWS)
                rim = rows[0 if from_south else 1, pl.ds(source + first, count), :]
                target[span, :] = target[span, :] + speeds * (factor * rim)

    return prepare_first, update, finish_rows


def coupled_kernel(
    groups_y,
    groups,
    spectrum,
    sea_mask,
    ocean_state,
    depth,
    ocean_out,
    updated,
    fields_out,
    rows_out,
    cols_out,
    cells,
    beside,
    state_in,
    depth_in,
    mask_in,
    raw,
    raw_mask,
    pack,
    pack_late,
    window,
    window_late,
    mask_window,
    turn_window,
    beside_send,
    across_send,
    beside_land,
    across_land,
    stress,
    result,
    result_send,
    result_land,
    rows_send,
    cols_send,
    input_sem,
    load_sem,
    pack_sem,
    late_sem,
    band_sem,
    stress_sem,
    result_sem,
    halo_sem,
    local_sem,
):
    x = lax.axis_index("gx")
    y = lax.axis_index("sec") * groups_y + lax.axis_index("gy")

    def exists(dy, dx):
        checks = []
        if dy > 0:
            checks.append(y < groups - 1)
        if dy < 0:
            checks.append(y > 0)
        if dx > 0:
            checks.append(x < PEERS - 1)
        if dx < 0:
            checks.append(x > 0)
        answer = checks[0]
        for check in checks[1:]:
            answer = jnp.logical_and(answer, check)
        return answer

    def device_at(row, column):
        return (row // groups_y, lax.rem(row, groups_y), column)

    def device(dy, dx):
        return device_at(y + dy, x + dx)

    def peer(step):
        return (lax.axis_index("sec"), lax.axis_index("gy"), lax.rem(x + step, PEERS))

    inputs = [
        pltpu.make_async_copy(ocean_state, state_in, input_sem.at[0]),
        pltpu.make_async_copy(depth, depth_in, input_sem.at[1]),
        pltpu.make_async_copy(sea_mask, mask_in, input_sem.at[2]),
    ]
    for copy in inputs:
        copy.start()

    barrier = pltpu.get_barrier_semaphore()
    for step in range(1, PEERS):
        pl.semaphore_signal(barrier, inc=1, device_id=peer(step), device_id_type=MESH)
    greeted = PEERS - 1
    for dy, dx in AROUND:
        if dy != 0:
            here = exists(dy, dx)

            @pl.when(here)
            def _():
                pl.semaphore_signal(barrier, inc=1, device_id=device(dy, dx), device_id_type=MESH)

            greeted = greeted + here.astype(jnp.int32)

    def load(q, part):
        size = QUARTER // LOADS * PER_DIR
        start = pl.multiple_of(q * (QUARTER * PER_DIR) + part * size, PER_DIR)
        return pltpu.make_async_copy(
            spectrum.at[pl.ds(start, size)],
            cells.at[pl.ds(pl.multiple_of(start + PAD, 8), size)],
            load_sem.at[part * 4 + q],
        )

    for part in range(LOADS):
        for q in range(4):
            load(q, part).start()

    raw[...] = jnp.zeros_like(raw)
    raw_mask[...] = jnp.zeros_like(raw_mask)
    width = state_in.shape[2]
    for copy in inputs:
        copy.wait()
    raw[0:3, :width] = state_in[1]
    raw[3:6, :width] = state_in[2]
    raw[8:11, :width] = state_in[0]
    raw[11:14, :width] = depth_in[...]
    raw_mask[6:8, : mask_in.shape[1]] = mask_in[...].astype(jnp.float32)
    even = ocean_shift(raw[...], MARGIN_O)
    odd = ocean_shift(raw[...], MARGIN_O - 64)
    mask_rows = ocean_shift(raw_mask[...], MARGIN_W)
    is_ocean = iota((8, LANES), 0) < 6
    for dest in range(PEERS):
        source = odd if dest % 2 else even
        origin = 384 * (dest // 2) + (128 if dest % 2 else 0)
        for tile in range(2):
            piece = source[:, origin + LANES * tile : origin + LANES * (tile + 1)]
            pack[dest, tile] = jnp.where(
                is_ocean, piece[:8], mask_rows[:, LANES * (dest + tile) : LANES * (dest + tile + 1)]
            )
            pack_late[dest, tile] = piece[8:]

    slot = pl.ds(pl.multiple_of(x * 8, 8), 8)

    def pack_copy(step, late):
        dest = peer(step)
        return pltpu.make_async_remote_copy(
            src_ref=(pack_late if late else pack).at[dest[2]],
            dst_ref=(window_late if late else window).at[:, slot, :],
            send_sem=(late_sem if late else pack_sem).at[0, step],
            recv_sem=(late_sem if late else pack_sem).at[1, step],
            device_id=dest,
            device_id_type=MESH,
        )

    pl.semaphore_wait(barrier, greeted)
    for step in range(1, PEERS):
        pack_copy(step, False).start()
    for step in range(1, PEERS):
        pack_copy(step, True).start()
    mask_window[...] = jnp.zeros_like(mask_window)
    cells[:PAD, :] = jnp.zeros((PAD, LANES), jnp.float32)
    cells[PAD + CELLS :, :] = jnp.zeros((PAD, LANES), jnp.float32)
    for ref in (window, window_late):
        ref[:, 11 * 8 : 13 * 8, :] = jnp.zeros((2, 16, LANES), jnp.float32)
    edge = jnp.zeros((2, 24, LANES), jnp.float32)

    @pl.when(y == 0)
    def _():
        window[:, 13 * 8 : 16 * 8, :] = edge
        window_late[:, 13 * 8 : 16 * 8, :] = edge
        across_land[:, 1] = jnp.zeros((3, 4, 8, LANES), jnp.float32)

    @pl.when(y == groups - 1)
    def _():
        window[:, 8 * 8 : 11 * 8, :] = edge
        window_late[:, 8 * 8 : 11 * 8, :] = edge
        across_land[:, 0] = jnp.zeros((3, 4, 8, LANES), jnp.float32)

    @pl.when(x == 0)
    def _():
        beside_land[1] = jnp.zeros((5, ROWS, LANES), jnp.float32)
        across_land[2] = jnp.zeros((2, 4, 8, LANES), jnp.float32)

    @pl.when(x == PEERS - 1)
    def _():
        beside_land[0] = jnp.zeros((5, ROWS, LANES), jnp.float32)
        across_land[1] = jnp.zeros((2, 4, 8, LANES), jnp.float32)

    window[:, slot, :] = pack[x]
    window_late[:, slot, :] = pack_late[x]

    lane = iota((ROWS, LANES), 1)
    row = iota((ROWS, LANES), 0)
    zero = jnp.zeros((ROWS, LANES), jnp.float32)

    def gather(i, carry):
        (cosine, sine), plain, fluxes = carry
        part = QUARTER // LOADS

        @pl.when(lax.rem(i, part) == 0)
        def _():
            for q in range(4):
                load(q, i // part).wait()

        totals, weighted, rims = [None] * 4, [None] * 4, [zero, zero]
        for j in range(NFREQ):
            values = []
            for q in range(4):
                base = (q * QUARTER + i) * PER_DIR + PAD
                values.append(cells[pl.ds(pl.multiple_of(base + j * ROWS, 8), ROWS), :])
                scaled = values[q] * SPEEDS[j]
                totals[q] = values[q] if j == 0 else totals[q] + values[q]
                weighted[q] = scaled if j == 0 else weighted[q] + scaled
            here = jnp.logical_or(lane == 2 * j + 1, lane == 2 * j + 2)
            for n, (east, west) in enumerate(((0, 1), (3, 2))):
                both = jnp.where(lane == LANES - 1, values[east], values[west])
                rims[n] = jnp.where(here, pltpu.roll(both, 2 * j + 2, 1), rims[n])
        for n in range(2):
            place = i + n * QUARTER
            group, part = place // 3, lax.rem(place, 3)
            earlier = jnp.where(part > 0, cols_send[group], zero)
            cols_send[group] = earlier + pltpu.roll(rims[n], part * (2 * NFREQ), 1)
        scale = 0.5 / (NDIR * NFREQ)
        cc, cs, ss = cosine * cosine * scale, cosine * sine * scale, sine * sine * scale
        pair = (totals[0] + totals[2]) - (totals[1] + totals[3])
        plain = (
            plain[0] + ((totals[0] + totals[2]) + (totals[1] + totals[3])),
            plain[1] + (cc - ss) * pair,
            plain[2] + (2.0 * cs) * pair,
        )
        straight, crossed = (cc, cs, ss), (ss, -cs, cc)
        west, east, south, north = fluxes
        west = tuple(
            west[s] + (cosine * straight[s]) * weighted[0] + (sine * crossed[s]) * weighted[3] for s in range(3)
        )
        east = tuple(
            east[s] + (cosine * straight[s]) * weighted[2] + (sine * crossed[s]) * weighted[1] for s in range(3)
        )
        south = tuple(
            south[s] + (sine * straight[s]) * weighted[0] + (cosine * crossed[s]) * weighted[1] for s in range(3)
        )
        north = tuple(
            north[s] + (sine * straight[s]) * weighted[2] + (cosine * crossed[s]) * weighted[3] for s in range(3)
        )
        return next_angle(cosine, sine), plain, (west, east, south, north)

    cols_send[...] = jnp.zeros_like(cols_send)
    triple = (zero, zero, zero)
    carry = (angle_at(0), triple, (triple, triple, triple, triple))
    _, plain, fluxes = lax.fori_loop(0, QUARTER, gather, carry)

    def pack_rows(n, carry):
        for m in range(5):
            start = n * 40 + m * 8
            span = pl.ds(pl.multiple_of(start, 8), 8)
            rows_send[0, span, :] = cells[pl.ds(start * ROWS + (PAD + ROWS - 1), 8, stride=ROWS), :]
            rows_send[1, span, :] = cells[pl.ds(start * ROWS + (PAD + HALF * ROWS), 8, stride=ROWS), :]
        return carry

    lax.fori_loop(0, HALF // 40, pack_rows, 0)

    sends = (exists(0, 1), exists(0, -1), exists(1, 0), exists(-1, 0))
    receives = (exists(0, -1), exists(0, 1), exists(-1, 0), exists(1, 0))

    def halo_ends(n):
        return (cols_send, cols_out.at[n]) if n < 2 else (rows_send.at[n - 2], rows_out.at[n - 2])

    def halo_copy(n):
        source, target = halo_ends(n)
        return pltpu.make_async_remote_copy(
            src_ref=source,
            dst_ref=target,
            send_sem=halo_sem.at[0, n],
            recv_sem=halo_sem.at[1, n],
            device_id=(device(0, 1), device(0, -1), device(1, 0), device(-1, 0))[n],
            device_id_type=MESH,
        )

    def halo_fill(n):
        source, target = halo_ends(n)
        return pltpu.make_async_copy(source, target, local_sem.at[n])

    def start_halo(n):
        @pl.when(sends[n])
        def _():
            halo_copy(n).start()

        @pl.when(jnp.logical_not(receives[n]))
        def _():
            halo_fill(n).start()

    def wait_halo(n):
        @pl.when(receives[n])
        def _():
            halo_copy(n).wait_recv()

        @pl.when(jnp.logical_not(receives[n]))
        def _():
            halo_fill(n).wait()

    start_halo(0)
    start_halo(1)

    for step in range(1, PEERS):
        pack_copy(step, False).wait_recv()

    def band_copy(n, late):
        source = pl.ds((5 if n == 0 else 0) * 8, 24)
        target = pl.ds((13 if n == 0 else 8) * 8, 24)
        ref = window_late if late else window
        return pltpu.make_async_remote_copy(
            src_ref=ref.at[:, source, :],
            dst_ref=ref.at[:, target, :],
            send_sem=band_sem.at[0, 2 * n + late],
            recv_sem=band_sem.at[1, 2 * n + late],
            device_id=device(1 if n == 0 else -1, 0),
            device_id_type=MESH,
        )

    vertical = (exists(1, 0), exists(-1, 0))
    from_side = (exists(-1, 0), exists(1, 0))
    for n in range(2):

        @pl.when(vertical[n])
        def _():
            band_copy(n, 0).start()

    def tiles_of(ref, rows):
        return jnp.concatenate([ref[t, rows, :] for t in range(2)], axis=1)

    def own_rows(first):
        return tiles_of(window, pl.ds(first, 8, stride=8))

    wide = (2 * LANES, 2 * LANES)
    spread = (iota(wide, 0) == (2 * iota(wide, 1)) // 3).astype(jnp.bfloat16)
    wave_masks = [own_rows(6), own_rows(7)]
    masks = jnp.dot(
        jnp.concatenate(wave_masks, axis=0).astype(jnp.bfloat16), spread, preferred_element_type=jnp.float32
    )
    near_mask = [masks[:8], masks[:8], masks[8:]]

    def restriction(width):
        fine, wave = iota((2 * LANES, width), 0), iota((2 * LANES, width), 1)
        wave = jnp.where(wave < 3 * LANES // 2, wave, wave - 2 * LANES) + MARGIN_W
        group = 3 * (wave // 2)
        ends = jnp.where(wave % 2 == 0, group, group + 2)
        return jnp.where(fine == ends, 2.0, jnp.where(fine == group + 1, 1.0, 0.0)).astype(jnp.bfloat16)

    near_east = [own_rows(c) * near_mask[c] for c in range(3)]
    near_north = [own_rows(3 + c) * near_mask[c] for c in range(3)]
    near_slope = [
        (near_east[1] - pltpu.roll(near_east[2], 1, 0)) * 0.5,
        (near_east[2] - near_east[0]) * 0.5,
        (pltpu.roll(near_east[0], 7, 0) - near_east[1]) * 0.5,
    ]
    vorticity = [along_x(near_north[c]) - near_slope[c] for c in range(3)]
    coarse = jnp.concatenate([2.0 * vorticity[0] + vorticity[1], vorticity[1] + 2.0 * vorticity[2]], axis=0)
    coarse = TURN_GAIN * jnp.tanh(exact_dot(coarse, restriction(LANES)) * (1.0 / 9.0))
    for c in range(2):
        turn_window[0, pl.ds(c, 8, stride=2), :] = coarse[8 * c : 8 * c + 8]
        placed = ocean_shift(wave_masks[c], -MARGIN_W)
        for t in range(2):
            mask_window[t, pl.ds(c, 8, stride=2), :] = placed[:, LANES * t : LANES * (t + 1)]

    def mask_products():
        around = tiles_of(mask_window, slice(None))
        return (
            around,
            around * pltpu.roll(around, 1, 1),
            around * pltpu.roll(around, 2 * LANES - 1, 1),
            around * pltpu.roll(around, 1, 0),
            around * pltpu.roll(around, 2 * ROWS - 1, 0),
        )

    near_products = [values[:ROWS, :LANES] for values in mask_products()]

    inside = jnp.logical_and(row > 0, row < ROWS - 1)
    turning = jnp.where(inside, turn_window[0, :ROWS, :], 0.0)
    turn_abs = jnp.abs(turning)
    scale = 0.25 / (NDIR * NFREQ)
    base, along, across = plain[0] * scale, plain[1] * 0.5, plain[2] * 0.5
    turn_c, turn_s = math.cos(2.0 * STEP_ANGLE), math.sin(2.0 * STEP_ANGLE)
    plain_along, plain_across = along, across
    signed = jnp.where(turning > 0.0, turn_s, -turn_s)
    along_turn = along * turn_c - across * signed
    across_turn = across * turn_c + along * signed
    stay = 1.0 - turn_abs
    along = stay * along + turn_abs * along_turn
    across = stay * across + turn_abs * across_turn
    local = [base + along, across, base - along]
    west, east, south, north = fluxes
    rims = zero
    for s in range(3):
        partial = near_products[0] * (local[s] - ((west[s] + east[s]) + (south[s] + north[s])))
        partial = partial + near_products[1] * jnp.where(lane == 0, 0.0, pltpu.roll(west[s], 1, 1))
        partial = partial + near_products[2] * jnp.where(lane == LANES - 1, 0.0, pltpu.roll(east[s], LANES - 1, 1))
        partial = partial + near_products[3] * jnp.where(row == 0, 0.0, pltpu.roll(south[s], 1, 0))
        partial = partial + near_products[4] * jnp.where(row == ROWS - 1, 0.0, pltpu.roll(north[s], ROWS - 1, 0))
        beside_send[s] = partial
        across_send[0, s] = partial[8:]
        across_send[0, s, 0:1, :] = south[s][ROWS - 1 :]
        across_send[1, s] = partial[:8]
        across_send[1, s, 7:8, :] = north[s][:1]
        beside_send[4, s : s + 1, :] = south[s][ROWS - 1 :]
        beside_send[4, 8 + s : 9 + s, :] = north[s][:1]
        rims = jnp.where(lane == LANES - 1 - s, pltpu.roll(west[s], (LANES - s) % LANES, 1) if s else west[s], rims)
        rims = jnp.where(lane == s, pltpu.roll(east[s], s, 1) if s else east[s], rims)
    for n, values in enumerate((plain_along, plain_across)):
        across_send[0, n, 1:2, :] = values[ROWS - 1 :]
        across_send[1, n, 6:7, :] = values[:1]
        beside_send[4, 3 + n : 4 + n, :] = values[ROWS - 1 :]
        beside_send[4, 11 + n : 12 + n, :] = values[:1]
    beside_send[3] = rims
    across_send[0, 3] = rims[8:]
    across_send[1, 3] = rims[:8]

    def stress_copy(n):
        dy, dx = AROUND[n]
        if dy == 0:
            source, target = beside_send, beside_land.at[{1: 1, -1: 0}[dx]]
        else:
            source = across_send.at[{1: 0, -1: 1}[dy]]
            target = across_land.at[{0: 0, 1: 2, -1: 1}[dx], {1: 1, -1: 0}[dy]]
        return pltpu.make_async_remote_copy(
            src_ref=source,
            dst_ref=target,
            send_sem=stress_sem.at[0, n],
            recv_sem=stress_sem.at[1, n],
            device_id=device(dy, dx),
            device_id_type=MESH,
        )

    for n, (dy, dx) in enumerate(AROUND):

        @pl.when(exists(dy, dx))
        def _():
            stress_copy(n).start()

    for step in range(1, PEERS):
        pack_copy(step, True).wait_recv()
    for n in range(2):

        @pl.when(vertical[n])
        def _():
            band_copy(n, 1).start()

    start_halo(2)
    start_halo(3)
    for n in range(2):

        @pl.when(from_side[n])
        def _():
            band_copy(n, 0).wait_recv()

    def all_rows(ref, first):
        return tiles_of(ref, pl.ds(first, SLOTS, stride=8))

    far_masks = [all_rows(window, 6), all_rows(window, 7)]
    masks = jnp.dot(
        jnp.concatenate(far_masks, axis=0).astype(jnp.bfloat16), spread, preferred_element_type=jnp.float32
    )
    ocean_mask = [masks[:SLOTS], masks[:SLOTS], masks[SLOTS:]]
    eastward = [all_rows(window, c) * ocean_mask[c] for c in range(3)]
    northward = [all_rows(window, 3 + c) * ocean_mask[c] for c in range(3)]
    east_y, north_y = along_y(eastward), along_y(northward)
    vorticity = [along_x(northward[c]) - east_y[c] for c in range(3)]
    divergence = [along_x(eastward[c]) + north_y[c] for c in range(3)]
    coarse = []
    for values in (vorticity, divergence):
        coarse.append(2.0 * values[0] + values[1])
        coarse.append(values[1] + 2.0 * values[2])
    coarse = exact_dot(jnp.concatenate(coarse, axis=0), restriction(2 * LANES)) * (1.0 / 9.0)
    coarse = TURN_GAIN * jnp.tanh(coarse)
    for c in range(2):
        placed = ocean_shift(far_masks[c], -MARGIN_W)
        for t in range(2):
            span = slice(LANES * t, LANES * (t + 1))
            mask_window[t, pl.ds(c, SLOTS, stride=2), :] = placed[:, span]
            turn_window[t, pl.ds(c, SLOTS, stride=2), :] = coarse[SLOTS * c : SLOTS * (c + 1), span]
        fields_out[pl.ds(ROWS + c, 8, stride=2), :] = coarse[SLOTS * (2 + c) : SLOTS * (2 + c) + 8, :LANES]
    fields_out[:ROWS, :] = turn_window[0, :ROWS, :]
    products = mask_products()
    for n, values in enumerate(products):
        fields_out[(2 + n) * ROWS : (3 + n) * ROWS, :] = values[:ROWS, :LANES]
    around, west_mask, east_mask, south_mask, north_mask = products

    prepare_first, update, finish_rows = wave_tools(fields_out, rows_out, cols_out, cells, beside, updated)
    for n in range(2):
        wait_halo(n)
    prepare_first()

    def one_step(i, angle):
        update(i, angle)
        return next_angle(*angle)

    angle = lax.fori_loop(0, DURING_STRESS, one_step, angle_at(0))

    for n in range(2):

        @pl.when(from_side[n])
        def _():
            band_copy(n, 1).wait_recv()

    surface = [all_rows(window_late, c) * ocean_mask[c] for c in range(3)]
    bottom = [all_rows(window_late, 3 + c) for c in range(3)]
    safe = [jnp.where(bottom[c] > 0.0, bottom[c], 1.0) for c in range(3)]
    inverse = [-STRESS_GAIN / safe[c] for c in range(3)]

    def raise_surface(surface, eastward, northward):
        flow_y = along_y([bottom[c] * northward[c] for c in range(3)])
        return [
            (surface[c] - GRAVITY_STEP * (along_x(bottom[c] * eastward[c]) + flow_y[c])) * ocean_mask[c]
            for c in range(3)
        ]

    def push(surface, eastward, northward):
        slope = along_y(surface)
        new_east = [
            eastward[c] + GRAVITY_STEP * (CORIOLIS_STEP * northward[c] - along_x(surface[c])) for c in range(3)
        ]
        new_north = [northward[c] + GRAVITY_STEP * (-CORIOLIS_STEP * eastward[c] - slope[c]) for c in range(3)]
        return new_east, new_north

    surface = raise_surface(surface, eastward, northward)
    pushed = push(surface, eastward, northward)
    wave_lane, fine = iota(wide, 0), iota(wide, 1)
    wave_lane = jnp.where(wave_lane < LANES + 64, wave_lane + MARGIN_W, wave_lane - 2 * LANES + MARGIN_W)
    first = 2 * (fine // 3)
    part = fine % 3
    hits = jnp.where(wave_lane == first, 1.0, 0.0) * jnp.where(part == 0, 1.0, jnp.where(part == 1, 0.5, 0.0)) + jnp.where(
        wave_lane == first + 1, 1.0, 0.0
    ) * jnp.where(part == 2, 1.0, jnp.where(part == 1, 0.5, 0.0))
    prolong = hits.astype(jnp.bfloat16)

    for n, (dy, dx) in enumerate(AROUND):

        @pl.when(exists(-dy, -dx))
        def _():
            stress_copy(n).wait_recv()

    side_lane = iota((2 * ROWS, LANES), 1) < 64

    def assemble(s):
        columns = [
            jnp.concatenate([body, across_land[n, 0, s], across_land[n, 1, s]], axis=0)
            for n, body in enumerate((beside_send[s], beside_land[0, s], beside_land[1, s]))
        ]
        return jnp.concatenate([columns[0], jnp.where(side_lane, columns[1], columns[2])], axis=1)

    def edge_row(place):
        rows = [ref[place : place + 1, :] for ref in (beside_send.at[4], beside_land.at[0, 4], beside_land.at[1, 4])]
        return jnp.concatenate([rows[0], jnp.where(side_lane[:1], rows[1], rows[2])], axis=1)

    around_row = iota((2 * ROWS, 2 * LANES), 0)
    around_lane = iota((2 * ROWS, 2 * LANES), 1)
    west_side = west_mask * jnp.where(around_lane % LANES == 0, 1.0, 0.0)
    east_side = east_mask * jnp.where(around_lane % LANES == LANES - 1, 1.0, 0.0)
    side_flux = assemble(3)
    pieces = []
    bodies = [assemble(s) for s in range(3)]

    def edge_rows(n):
        low, high = edge_row(11 + n), edge_row(3 + n)
        values = jnp.where(around_row == 0, low, jnp.where(around_row == ROWS - 1, high, 0.0))
        values = jnp.where(around_row == ROWS, bodies[n][22:23], values)
        return jnp.where(around_row == 2 * ROWS - 1, bodies[n][25:26], values)

    edge_along, edge_across = edge_rows(0), edge_rows(1)
    edge_turn = tiles_of(turn_window, slice(None))
    edge_signed = jnp.where(edge_turn > 0.0, turn_s, -turn_s)
    edge_scale = around * jnp.abs(edge_turn)
    along_change = edge_scale * (edge_along * (turn_c - 1.0) - edge_across * edge_signed)
    across_change = edge_scale * (edge_across * (turn_c - 1.0) + edge_along * edge_signed)
    changes = (along_change, across_change, -along_change)
    for s in range(3):
        body = bodies[s] + changes[s]
        from_south = jnp.where(
            around_row == 0, bodies[s][24:25], jnp.where(around_row == ROWS, edge_row(s), 0.0)
        )
        from_north = jnp.where(
            around_row == ROWS - 1, bodies[s][23:24], jnp.where(around_row == 2 * ROWS - 1, edge_row(8 + s), 0.0)
        )
        body = body + west_side * pltpu.roll(side_flux, s + 1, 1)
        body = body + east_side * pltpu.roll(side_flux, 2 * LANES - 1 - s, 1)
        body = body + south_mask * from_south + north_mask * from_north
        for t in range(2):
            stress[s, t] = body[:, LANES * t : LANES * (t + 1)]
        for c in range(2):
            pieces.append(
                jnp.concatenate([stress[s, t, pl.ds(c, SLOTS, stride=2), :] for t in range(2)], axis=1)
            )
    spread_stress = exact_dot(jnp.concatenate(pieces, axis=0), prolong)
    tensor = []
    for s in range(3):
        low = spread_stress[2 * SLOTS * s : 2 * SLOTS * s + SLOTS]
        high = spread_stress[2 * SLOTS * s + SLOTS : 2 * SLOTS * (s + 1)]
        tensor.append([low, 0.5 * low + 0.5 * high, high])
    cross_y, normal_y = along_y(tensor[1]), along_y(tensor[2])
    force_x = [inverse[c] * (along_x(tensor[0][c]) + cross_y[c]) for c in range(3)]
    force_y = [inverse[c] * (along_x(tensor[1][c]) + normal_y[c]) for c in range(3)]

    for step in range(ITERS):
        if step > 0:
            surface = raise_surface(surface, eastward, northward)
            pushed = push(surface, eastward, northward)
        eastward = [(pushed[0][c] + force_x[c]) * ocean_mask[c] for c in range(3)]
        northward = [(pushed[1][c] + force_y[c]) * ocean_mask[c] for c in range(3)]

    is_even = lax.rem(x, 2) == 0
    low_lanes = iota((8, LANES), 1) < 64
    halves = []
    for f, values in enumerate((surface, eastward, northward)):
        for c in range(3):
            own = values[c][:8]
            low, high = ocean_shift(own, -MARGIN_O), ocean_shift(own, 64 - MARGIN_O)
            place = 8 * (3 * f + c)
            result[place : place + 8, :] = jnp.where(is_even, low[:, :LANES], high[:, LANES:])
            halves.append(jnp.where(is_even, low[:, LANES:], pltpu.roll(high[:, :LANES], 64, 1)))
    for m in range(5):
        merged = halves[m] if m == 4 else jnp.where(low_lanes, halves[m], pltpu.roll(halves[5 + m], 64, 1))
        result[72 + 8 * m : 80 + 8 * m, :] = merged
    for dest in range(PEERS):
        result_send[dest, 0:8, :] = result[pl.ds(dest, 8, stride=8), :]
        result_send[dest, 8:14, :] = result[pl.ds(64 + dest, 6, stride=8), :]

    def result_copy(step):
        dest = peer(step)
        return pltpu.make_async_remote_copy(
            src_ref=result_send.at[dest[2]],
            dst_ref=result_land.at[x],
            send_sem=result_sem.at[0, step],
            recv_sem=result_sem.at[1, step],
            device_id=dest,
            device_id_type=MESH,
        )

    for step in range(1, PEERS):
        result_copy(step).start()
    result_land[x] = result_send[x]
    lax.fori_loop(DURING_STRESS, QUARTER, one_step, angle)
    for step in range(1, PEERS):
        pack_copy(step, False).wait_send()
        pack_copy(step, True).wait_send()
    for n in range(2):

        @pl.when(vertical[n])
        def _():
            band_copy(n, 0).wait_send()
            band_copy(n, 1).wait_send()

    for n, (dy, dx) in enumerate(AROUND):

        @pl.when(exists(dy, dx))
        def _():
            stress_copy(n).wait_send()

    for n in range(2, 4):
        wait_halo(n)

    def fix_step(i, angle):
        finish_rows(i, angle)
        return next_angle(*angle)

    lax.fori_loop(0, QUARTER, fix_step, angle_at(0))
    for n in range(4):

        @pl.when(sends[n])
        def _():
            halo_copy(n).wait_send()

    for step in range(1, PEERS):
        result_copy(step).wait_recv()
    for q in range(PEERS // 2):
        left, right = result_land[2 * q], result_land[2 * q + 1]
        left_turned, right_turned = pltpu.roll(left, 64, 1), pltpu.roll(right, 64, 1)
        side = iota((5, LANES), 1) < 64
        middle = jnp.concatenate(
            [
                jnp.where(side, left[9:14], right_turned[9:14]),
                jnp.where(side[:4], left_turned[9:13], right[9:13]),
            ],
            axis=0,
        )
        for t, tile in enumerate((left, middle, right)):
            lanes = pl.ds((3 * q + t) * LANES, LANES)
            for f in range(3):
                ocean_out[f, :, lanes] = tile[3 * f : 3 * f + 3]

    for step in range(1, PEERS):
        result_copy(step).wait_send()


def hand_over(ocean_in, updated, out, ocean_out, store_sem, local_sem):
    handed = pltpu.make_async_copy(ocean_in, ocean_out, local_sem)
    handed.start()
    size = CELLS // CHUNKS
    copies = [
        pltpu.make_async_copy(updated.at[pl.ds(n * size, size)], out.at[pl.ds(n * size, size)], store_sem.at[n])
        for n in range(CHUNKS)
    ]
    for copy in copies:
        copy.start()
    for copy in copies:
        copy.wait()
    handed.wait()


def shards(mesh_shape, spectrum, sea_mask, ocean_state, depth):
    groups_y = mesh_shape["gy"]
    groups = groups_y * mesh_shape["sec"]
    cells = spectrum.reshape(CELLS, LANES)
    vmem = pl.BlockSpec(memory_space=pltpu.VMEM)
    anywhere = pl.BlockSpec(memory_space=pl.ANY)
    f32 = jnp.float32
    dma = pltpu.SemaphoreType.DMA
    ocean_part, updated = pl.pallas_call(
        functools.partial(coupled_kernel, groups_y, groups),
        out_shape=(
            jax.ShapeDtypeStruct(ocean_state.shape, f32),
            jax.ShapeDtypeStruct((CELLS, LANES), f32),
        ),
        in_specs=[anywhere] * 4,
        out_specs=(vmem, vmem),
        scratch_shapes=[
            pltpu.VMEM((7 * ROWS, LANES), f32),
            pltpu.VMEM((2, HALF, LANES), f32),
            pltpu.VMEM((2, 6, ROWS, LANES), f32),
            pltpu.VMEM((CELLS + 2 * PAD, LANES), f32),
            pltpu.VMEM((4 * NFREQ, ROWS, LANES), f32),
            pltpu.VMEM(ocean_state.shape, f32),
            pltpu.VMEM(depth.shape, f32),
            pltpu.VMEM(sea_mask.shape, jnp.int32),
            pltpu.VMEM((SLOTS, 1792), f32),
            pltpu.VMEM((8, 1280), f32),
            pltpu.VMEM((PEERS, 2, 8, LANES), f32),
            pltpu.VMEM((PEERS, 2, 8, LANES), f32),
            pltpu.VMEM((2, SLOTS * 8, LANES), f32),
            pltpu.VMEM((2, SLOTS * 8, LANES), f32),
            pltpu.VMEM((2, 2 * ROWS, LANES), f32),
            pltpu.VMEM((2, 2 * ROWS, LANES), f32),
            pltpu.VMEM((5, ROWS, LANES), f32),
            pltpu.VMEM((2, 4, 8, LANES), f32),
            pltpu.VMEM((2, 5, ROWS, LANES), f32),
            pltpu.VMEM((3, 2, 4, 8, LANES), f32),
            pltpu.VMEM((3, 2, 2 * ROWS, LANES), f32),
            pltpu.VMEM((112, LANES), f32),
            pltpu.VMEM((PEERS, SLOTS, LANES), f32),
            pltpu.VMEM((PEERS, SLOTS, LANES), f32),
            pltpu.VMEM((2, HALF, LANES), f32),
            pltpu.VMEM((6, ROWS, LANES), f32),
            dma((3,)),
            dma((4 * LOADS,)),
            dma((2, PEERS)),
            dma((2, PEERS)),
            dma((2, 4)),
            dma((2, 8)),
            dma((2, PEERS)),
            dma((2, 4)),
            dma((4,)),
        ],
        compiler_params=pltpu.CompilerParams(
            collective_id=0, has_side_effects=True, vmem_limit_bytes=VMEM_LIMIT
        ),
        name="coupled",
    )(*[pltpu.with_memory_space_constraint(a, pltpu.HBM) for a in (cells, sea_mask, ocean_state, depth)])
    spectrum_out, ocean_out = pl.pallas_call(
        hand_over,
        out_shape=(jax.ShapeDtypeStruct((CELLS, LANES), f32), jax.ShapeDtypeStruct(ocean_state.shape, f32)),
        in_specs=[anywhere, anywhere],
        out_specs=(anywhere, anywhere),
        scratch_shapes=[dma((CHUNKS,)), dma],
        compiler_params=pltpu.CompilerParams(vmem_limit_bytes=VMEM_LIMIT),
        name="hand_over",
    )(ocean_part, updated)
    return (spectrum_out.reshape(spectrum.shape), ocean_out)


def solution(mesh):
    return jax.shard_map(
        functools.partial(shards, dict(mesh.shape)),
        mesh=mesh,
        in_specs=(
            P(None, None, ("sec", "gy"), "gx"),
            P(("sec", "gy", "gx"), None),
            P(None, ("sec", "gy", "gx"), None),
            P(("sec", "gy", "gx"), None),
        ),
        out_specs=(P(None, None, ("sec", "gy"), "gx"), P(None, ("sec", "gy", "gx"), None)),
        check_vma=False,
    )
```

```python
import functools
import math

import jax
import jax.numpy as jnp
from jax import lax
from jax.experimental import pallas as pl
from jax.experimental.pallas import tpu as pltpu
from jax.sharding import PartitionSpec as P

ITERS = 4
GRAVITY_STEP = 0.3
CORIOLIS_STEP = 0.2
STRESS_GAIN = 2.0
TURN_GAIN = 0.2
SPEED_BASE = 0.35
SPEED_RATIO = 0.9

NDIR = 36
NFREQ = 20
ROWS = 16
LANES = 128
CELLS = NDIR * NFREQ * ROWS
PER_DIR = NFREQ * ROWS
QUARTER = NDIR // 4
PAD = 8
DURING_STRESS = 2
CHUNKS = 8
LOADS = 3
VMEM_LIMIT = 28 * 1024 * 1024
HALF = NDIR // 2 * NFREQ
PEERS = 8
SLOTS = 16
MARGIN_O = 24
MARGIN_W = 16
SPEEDS = [SPEED_BASE * SPEED_RATIO**j for j in range(NFREQ)]
STEP_ANGLE = 2.0 * math.pi / NDIR
MESH = pl.DeviceIdType.MESH
AROUND = [(1, 1), (1, -1), (-1, 1), (-1, -1), (1, 0), (-1, 0), (0, 1), (0, -1)]
FAR_FIRST = (4, 3, 5, 2, 6, 1, 7)


def iota(shape, dim):
    return lax.broadcasted_iota(jnp.int32, shape, dim)


def next_angle(cosine, sine):
    turn_c, turn_s = math.cos(STEP_ANGLE), math.sin(STEP_ANGLE)
    return cosine * turn_c - sine * turn_s, sine * turn_c + cosine * turn_s


def angle_at(i):
    return jnp.float32(math.cos((i + 0.5) * STEP_ANGLE)), jnp.float32(math.sin((i + 0.5) * STEP_ANGLE))


def exact_dot(values, weights):
    rows = values.shape[0]
    high = values.astype(jnp.bfloat16)
    rest = values - high.astype(jnp.float32)
    middle = rest.astype(jnp.bfloat16)
    low = (rest - middle.astype(jnp.float32)).astype(jnp.bfloat16)
    stacked = jnp.concatenate([high, middle, low], axis=0)
    product = jnp.dot(stacked, weights, preferred_element_type=jnp.float32)
    return product[:rows] + product[rows : 2 * rows] + product[2 * rows :]


def ocean_shift(values, amount):
    return pltpu.roll(values, amount % values.shape[1], 1)


def along_x(values):
    return (ocean_shift(values, -1) - ocean_shift(values, 1)) * 0.5


def along_y(classes):
    above = [classes[1], classes[2], pltpu.roll(classes[0], SLOTS - 1, 0)]
    below = [pltpu.roll(classes[2], 1, 0), classes[0], classes[1]]
    return [(above[c] - below[c]) * 0.5 for c in range(3)]


def wave_tools(fields, rows, cols, cells, beside, target):
    lane = iota((8, LANES), 1)
    row = iota((8, LANES), 0)

    def half(n, h):
        return fields[ROWS * n + 8 * h : ROWS * n + 8 * h + 8, :]

    def turn_part(h):
        return half(2, h) * jnp.abs(half(0, h))

    def cell(direction, j, offset):
        place = direction * PER_DIR + (PAD + j * ROWS + offset)
        return cells[pl.ds(pl.multiple_of(place, 8) if offset % 8 == 0 else place, 8), :]

    odd = lax.rem(lane, 2) == 1

    def rims(i, h):
        columns = []
        for place in (i, QUARTER + i):
            group, part = place // 3, lax.rem(place, 3)
            span = slice(8 * h, 8 * h + 8)
            merged = jnp.where(odd, cols[0, group, span, :], cols[1, group, span, :])
            columns.append(pltpu.roll(merged, lax.rem(LANES - part * (2 * NFREQ), LANES), 1))
        return columns

    def rim_at(columns, j):
        return [pltpu.roll(column, LANES - 1 - 2 * j, 1) for column in columns]

    def prepare(i, h, j, columns, rim):
        following = rim_at(columns, j + 1)
        for q in range(4):
            value = cell(q * QUARTER + i, j, 8 * h)
            if q in (0, 3):
                moved = jnp.where(lane == 0, rim[q // 2], pltpu.roll(value, 1, 1))
            else:
                moved = jnp.where(lane == LANES - 1, following[q // 2], pltpu.roll(value, LANES - 1, 1))
            beside[q * NFREQ + j, 8 * h : 8 * h + 8, :] = moved
        return following

    def update(i, angle):
        cosine, sine = angle
        following_step = jnp.minimum(i + 1, QUARTER - 1)
        for h in range(2):
            columns = rims(following_step, h)
            rim = rim_at(columns, 0)
            turn_left = half(0, h) > 0.0
            shift_up = half(1, h) > 0.0
            mask = half(2, h)
            turned = turn_part(h)
            stay = mask - turned
            shifted = mask * half(1, h)
            leave = mask * (cosine + sine)
            factors = []
            for q in range(4):
                speed_x, speed_y = (cosine, sine) if q % 2 == 0 else (sine, cosine)
                inner = half(5 if q in (0, 1) else 6, h) * speed_y
                if q in (0, 1) and h == 0:
                    inner = jnp.where(row == 0, 0.0, inner)
                if q in (2, 3) and h == 1:
                    inner = jnp.where(row == 7, 0.0, inner)
                factors.append((half(3 if q in (0, 3) else 4, h) * speed_x, inner))
            values = [cell(q * QUARTER + i, 0, 8 * h) for q in range(4)]
            faces = [None] * 4
            for j in range(NFREQ):
                keep = stay - SPEEDS[j] * leave
                for q in range(4):
                    direction = q * QUARTER + i
                    before, after = direction - 1, direction + 1
                    if q == 0:
                        before = jnp.where(i == 0, NDIR - 1, before)
                    if q == 3:
                        after = jnp.where(i == QUARTER - 1, 0, after)
                    along = cell(direction, j, 8 * h + (-1 if q in (0, 1) else 1))
                    moved = factors[q][0] * beside[q * NFREQ + j, 8 * h : 8 * h + 8, :] + factors[q][1] * along
                    total = keep * values[q] + SPEEDS[j] * moved
                    total = total + turned * jnp.where(turn_left, cell(before, j, 8 * h), cell(after, j, 8 * h))
                    if j > 0:
                        total = total + faces[q]
                    if j < NFREQ - 1:
                        following = cell(direction, j + 1, 8 * h)
                        faces[q] = shifted * jnp.where(shift_up, values[q], following)
                        total = total - faces[q]
                        values[q] = following
                    place = (direction * NFREQ + j) * ROWS + 8 * h
                    target[pl.ds(pl.multiple_of(place, 8), 8), :] = total
                rim = prepare(following_step, h, j, columns, rim)

    def prepare_first():
        for h in range(2):
            columns = rims(0, h)
            rim = rim_at(columns, 0)
            for j in range(NFREQ):
                rim = prepare(0, h, j, columns, rim)

    def finish_rows(i, angle):
        for q in range(4):
            speed_y = angle[1] if q % 2 == 0 else angle[0]
            from_south = q in (0, 1)
            edge = (5 * ROWS) if from_south else (7 * ROWS - 1)
            factor = fields[edge : edge + 1, :] * speed_y
            direction = q * QUARTER + i
            source = (direction if from_south else direction - 2 * QUARTER) * NFREQ
            for first in (0, 8, 16):
                count = min(8, NFREQ - first)
                speeds = jnp.zeros((count, LANES), jnp.float32)
                for r in range(count):
                    speeds = jnp.where(row[:count] == r, SPEEDS[first + r], speeds)
                span = pl.ds((direction * NFREQ + first) * ROWS + (0 if from_south else ROWS - 1), count, stride=ROWS)
                rim = rows[0 if from_south else 1, pl.ds(source + first, count), :]
                target[span, :] = target[span, :] + speeds * (factor * rim)

    return prepare_first, update, finish_rows


def coupled_kernel(
    groups_y,
    groups,
    spectrum,
    sea_mask,
    ocean_state,
    depth,
    ocean_out,
    updated,
    fields_out,
    rows_out,
    cols_out,
    cells,
    beside,
    state_in,
    depth_in,
    mask_in,
    raw,
    raw_mask,
    pack,
    pack_late,
    window,
    window_late,
    mask_window,
    turn_window,
    beside_send,
    across_send,
    beside_land,
    across_land,
    stress,
    result,
    result_send,
    result_land,
    rows_send,
    cols_send,
    input_sem,
    load_sem,
    pack_sem,
    late_sem,
    band_sem,
    stress_sem,
    result_sem,
    halo_sem,
    local_sem,
):
    x = lax.axis_index("gx")
    y = lax.axis_index("sec") * groups_y + lax.axis_index("gy")

    def exists(dy, dx):
        checks = []
        if dy > 0:
            checks.append(y < groups - 1)
        if dy < 0:
            checks.append(y > 0)
        if dx > 0:
            checks.append(x < PEERS - 1)
        if dx < 0:
            checks.append(x > 0)
        answer = checks[0]
        for check in checks[1:]:
            answer = jnp.logical_and(answer, check)
        return answer

    def device_at(row, column):
        return (row // groups_y, lax.rem(row, groups_y), column)

    def device(dy, dx):
        return device_at(y + dy, x + dx)

    def peer(step):
        return (lax.axis_index("sec"), lax.axis_index("gy"), lax.rem(x + step, PEERS))

    inputs = [
        pltpu.make_async_copy(ocean_state, state_in, input_sem.at[0]),
        pltpu.make_async_copy(depth, depth_in, input_sem.at[1]),
        pltpu.make_async_copy(sea_mask, mask_in, input_sem.at[2]),
    ]
    for copy in inputs:
        copy.start()

    barrier = pltpu.get_barrier_semaphore()
    greeted = PEERS - 1
    for dy, dx in AROUND:
        if dy != 0:
            here = exists(dy, dx)

            @pl.when(here)
            def _():
                pl.semaphore_signal(barrier, inc=1, device_id=device(dy, dx), device_id_type=MESH)

            greeted = greeted + here.astype(jnp.int32)

    for step in FAR_FIRST:
        pl.semaphore_signal(barrier, inc=1, device_id=peer(step), device_id_type=MESH)

    def load(q, part):
        size = QUARTER // LOADS * PER_DIR
        start = pl.multiple_of(q * (QUARTER * PER_DIR) + part * size, PER_DIR)
        return pltpu.make_async_copy(
            spectrum.at[pl.ds(start, size)],
            cells.at[pl.ds(pl.multiple_of(start + PAD, 8), size)],
            load_sem.at[part * 4 + q],
        )

    for part in range(LOADS):
        for q in range(4):
            load(q, part).start()

    raw[...] = jnp.zeros_like(raw)
    raw_mask[...] = jnp.zeros_like(raw_mask)
    width = state_in.shape[2]
    for copy in inputs:
        copy.wait()
    raw[0:3, :width] = state_in[1]
    raw[3:6, :width] = state_in[2]
    raw[8:11, :width] = state_in[0]
    raw[11:14, :width] = depth_in[...]
    raw_mask[6:8, : mask_in.shape[1]] = mask_in[...].astype(jnp.float32)
    even = ocean_shift(raw[...], MARGIN_O)
    odd = ocean_shift(raw[...], MARGIN_O - 64)
    mask_rows = ocean_shift(raw_mask[...], MARGIN_W)
    is_ocean = iota((8, LANES), 0) < 6
    for dest in range(PEERS):
        source = odd if dest % 2 else even
        origin = 384 * (dest // 2) + (128 if dest % 2 else 0)
        for tile in range(2):
            piece = source[:, origin + LANES * tile : origin + LANES * (tile + 1)]
            pack[dest, tile] = jnp.where(
                is_ocean, piece[:8], mask_rows[:, LANES * (dest + tile) : LANES * (dest + tile + 1)]
            )
            pack_late[dest, tile] = piece[8:]

    slot = pl.ds(pl.multiple_of(x * 8, 8), 8)

    def pack_copy(step, late):
        dest = peer(step)
        return pltpu.make_async_remote_copy(
            src_ref=(pack_late if late else pack).at[dest[2]],
            dst_ref=(window_late if late else window).at[:, slot, :],
            send_sem=(late_sem if late else pack_sem).at[0, step],
            recv_sem=(late_sem if late else pack_sem).at[1, step],
            device_id=dest,
            device_id_type=MESH,
        )

    pl.semaphore_wait(barrier, greeted)
    for step in FAR_FIRST:
        pack_copy(step, False).start()
    for step in FAR_FIRST:
        pack_copy(step, True).start()
    mask_window[...] = jnp.zeros_like(mask_window)
    cells[:PAD, :] = jnp.zeros((PAD, LANES), jnp.float32)
    cells[PAD + CELLS :, :] = jnp.zeros((PAD, LANES), jnp.float32)
    for ref in (window, window_late):
        ref[:, 11 * 8 : 13 * 8, :] = jnp.zeros((2, 16, LANES), jnp.float32)
    edge = jnp.zeros((2, 24, LANES), jnp.float32)

    @pl.when(y == 0)
    def _():
        window[:, 13 * 8 : 16 * 8, :] = edge
        window_late[:, 13 * 8 : 16 * 8, :] = edge
        across_land[:, 1] = jnp.zeros((3, 4, 8, LANES), jnp.float32)

    @pl.when(y == groups - 1)
    def _():
        window[:, 8 * 8 : 11 * 8, :] = edge
        window_late[:, 8 * 8 : 11 * 8, :] = edge
        across_land[:, 0] = jnp.zeros((3, 4, 8, LANES), jnp.float32)

    @pl.when(x == 0)
    def _():
        beside_land[1] = jnp.zeros((5, ROWS, LANES), jnp.float32)
        across_land[2] = jnp.zeros((2, 4, 8, LANES), jnp.float32)

    @pl.when(x == PEERS - 1)
    def _():
        beside_land[0] = jnp.zeros((5, ROWS, LANES), jnp.float32)
        across_land[1] = jnp.zeros((2, 4, 8, LANES), jnp.float32)

    window[:, slot, :] = pack[x]
    window_late[:, slot, :] = pack_late[x]

    lane = iota((ROWS, LANES), 1)
    row = iota((ROWS, LANES), 0)
    zero = jnp.zeros((ROWS, LANES), jnp.float32)

    def gather(i, carry):
        (cosine, sine), plain, fluxes = carry
        part = QUARTER // LOADS

        @pl.when(lax.rem(i, part) == 0)
        def _():
            for q in range(4):
                load(q, i // part).wait()

        totals, weighted, rims = [None] * 4, [None] * 4, [zero, zero]
        for j in range(NFREQ):
            values = []
            for q in range(4):
                base = (q * QUARTER + i) * PER_DIR + PAD
                values.append(cells[pl.ds(pl.multiple_of(base + j * ROWS, 8), ROWS), :])
                scaled = values[q] * SPEEDS[j]
                totals[q] = values[q] if j == 0 else totals[q] + values[q]
                weighted[q] = scaled if j == 0 else weighted[q] + scaled
            here = jnp.logical_or(lane == 2 * j + 1, lane == 2 * j + 2)
            for n, (east, west) in enumerate(((0, 1), (3, 2))):
                both = jnp.where(lane == LANES - 1, values[east], values[west])
                rims[n] = jnp.where(here, pltpu.roll(both, 2 * j + 2, 1), rims[n])
        for n in range(2):
            place = i + n * QUARTER
            group, part = place // 3, lax.rem(place, 3)
            earlier = jnp.where(part > 0, cols_send[group], zero)
            cols_send[group] = earlier + pltpu.roll(rims[n], part * (2 * NFREQ), 1)
        scale = 0.5 / (NDIR * NFREQ)
        cc, cs, ss = cosine * cosine * scale, cosine * sine * scale, sine * sine * scale
        pair = (totals[0] + totals[2]) - (totals[1] + totals[3])
        plain = (
            plain[0] + ((totals[0] + totals[2]) + (totals[1] + totals[3])),
            plain[1] + (cc - ss) * pair,
            plain[2] + (2.0 * cs) * pair,
        )
        straight, crossed = (cc, cs, ss), (ss, -cs, cc)
        west, east, south, north = fluxes
        west = tuple(
            west[s] + (cosine * straight[s]) * weighted[0] + (sine * crossed[s]) * weighted[3] for s in range(3)
        )
        east = tuple(
            east[s] + (cosine * straight[s]) * weighted[2] + (sine * crossed[s]) * weighted[1] for s in range(3)
        )
        south = tuple(
            south[s] + (sine * straight[s]) * weighted[0] + (cosine * crossed[s]) * weighted[1] for s in range(3)
        )
        north = tuple(
            north[s] + (sine * straight[s]) * weighted[2] + (cosine * crossed[s]) * weighted[3] for s in range(3)
        )
        return next_angle(cosine, sine), plain, (west, east, south, north)

    cols_send[...] = jnp.zeros_like(cols_send)
    triple = (zero, zero, zero)
    carry = (angle_at(0), triple, (triple, triple, triple, triple))
    _, plain, fluxes = lax.fori_loop(0, QUARTER, gather, carry)

    def pack_rows(n, carry):
        for m in range(5):
            start = n * 40 + m * 8
            span = pl.ds(pl.multiple_of(start, 8), 8)
            rows_send[0, span, :] = cells[pl.ds(start * ROWS + (PAD + ROWS - 1), 8, stride=ROWS), :]
            rows_send[1, span, :] = cells[pl.ds(start * ROWS + (PAD + HALF * ROWS), 8, stride=ROWS), :]
        return carry

    lax.fori_loop(0, HALF // 40, pack_rows, 0)

    sends = (exists(0, 1), exists(0, -1), exists(1, 0), exists(-1, 0))
    receives = (exists(0, -1), exists(0, 1), exists(-1, 0), exists(1, 0))

    def halo_ends(n):
        return (cols_send, cols_out.at[n]) if n < 2 else (rows_send.at[n - 2], rows_out.at[n - 2])

    def halo_copy(n):
        source, target = halo_ends(n)
        return pltpu.make_async_remote_copy(
            src_ref=source,
            dst_ref=target,
            send_sem=halo_sem.at[0, n],
            recv_sem=halo_sem.at[1, n],
            device_id=(device(0, 1), device(0, -1), device(1, 0), device(-1, 0))[n],
            device_id_type=MESH,
        )

    def halo_fill(n):
        source, target = halo_ends(n)
        return pltpu.make_async_copy(source, target, local_sem.at[n])

    def start_halo(n):
        @pl.when(sends[n])
        def _():
            halo_copy(n).start()

        @pl.when(jnp.logical_not(receives[n]))
        def _():
            halo_fill(n).start()

    def wait_halo(n):
        @pl.when(receives[n])
        def _():
            halo_copy(n).wait_recv()

        @pl.when(jnp.logical_not(receives[n]))
        def _():
            halo_fill(n).wait()

    start_halo(0)
    start_halo(1)

    for step in FAR_FIRST:
        pack_copy(step, False).wait_recv()

    def band_copy(n, late):
        source = pl.ds((5 if n == 0 else 0) * 8, 24)
        target = pl.ds((13 if n == 0 else 8) * 8, 24)
        ref = window_late if late else window
        return pltpu.make_async_remote_copy(
            src_ref=ref.at[:, source, :],
            dst_ref=ref.at[:, target, :],
            send_sem=band_sem.at[0, 2 * n + late],
            recv_sem=band_sem.at[1, 2 * n + late],
            device_id=device(1 if n == 0 else -1, 0),
            device_id_type=MESH,
        )

    vertical = (exists(1, 0), exists(-1, 0))
    from_side = (exists(-1, 0), exists(1, 0))
    for n in range(2):

        @pl.when(vertical[n])
        def _():
            band_copy(n, 0).start()

    def tiles_of(ref, rows):
        return jnp.concatenate([ref[t, rows, :] for t in range(2)], axis=1)

    def own_rows(first):
        return tiles_of(window, pl.ds(first, 8, stride=8))

    wide = (2 * LANES, 2 * LANES)
    spread = (iota(wide, 0) == (2 * iota(wide, 1)) // 3).astype(jnp.bfloat16)
    wave_masks = [own_rows(6), own_rows(7)]
    masks = jnp.dot(
        jnp.concatenate(wave_masks, axis=0).astype(jnp.bfloat16), spread, preferred_element_type=jnp.float32
    )
    near_mask = [masks[:8], masks[:8], masks[8:]]

    def restriction(width):
        fine, wave = iota((2 * LANES, width), 0), iota((2 * LANES, width), 1)
        wave = jnp.where(wave < 3 * LANES // 2, wave, wave - 2 * LANES) + MARGIN_W
        group = 3 * (wave // 2)
        ends = jnp.where(wave % 2 == 0, group, group + 2)
        return jnp.where(fine == ends, 2.0, jnp.where(fine == group + 1, 1.0, 0.0)).astype(jnp.bfloat16)

    near_east = [own_rows(c) * near_mask[c] for c in range(3)]
    near_north = [own_rows(3 + c) * near_mask[c] for c in range(3)]
    near_slope = [
        (near_east[1] - pltpu.roll(near_east[2], 1, 0)) * 0.5,
        (near_east[2] - near_east[0]) * 0.5,
        (pltpu.roll(near_east[0], 7, 0) - near_east[1]) * 0.5,
    ]
    vorticity = [along_x(near_north[c]) - near_slope[c] for c in range(3)]
    coarse = jnp.concatenate([2.0 * vorticity[0] + vorticity[1], vorticity[1] + 2.0 * vorticity[2]], axis=0)
    coarse = TURN_GAIN * jnp.tanh(exact_dot(coarse, restriction(LANES)) * (1.0 / 9.0))
    for c in range(2):
        turn_window[0, pl.ds(c, 8, stride=2), :] = coarse[8 * c : 8 * c + 8]
        placed = ocean_shift(wave_masks[c], -MARGIN_W)
        for t in range(2):
            mask_window[t, pl.ds(c, 8, stride=2), :] = placed[:, LANES * t : LANES * (t + 1)]

    def mask_products():
        around = tiles_of(mask_window, slice(None))
        return (
            around,
            around * pltpu.roll(around, 1, 1),
            around * pltpu.roll(around, 2 * LANES - 1, 1),
            around * pltpu.roll(around, 1, 0),
            around * pltpu.roll(around, 2 * ROWS - 1, 0),
        )

    near_products = [values[:ROWS, :LANES] for values in mask_products()]

    inside = jnp.logical_and(row > 0, row < ROWS - 1)
    turning = jnp.where(inside, turn_window[0, :ROWS, :], 0.0)
    turn_abs = jnp.abs(turning)
    scale = 0.25 / (NDIR * NFREQ)
    base, along, across = plain[0] * scale, plain[1] * 0.5, plain[2] * 0.5
    turn_c, turn_s = math.cos(2.0 * STEP_ANGLE), math.sin(2.0 * STEP_ANGLE)
    plain_along, plain_across = along, across
    signed = jnp.where(turning > 0.0, turn_s, -turn_s)
    along_turn = along * turn_c - across * signed
    across_turn = across * turn_c + along * signed
    stay = 1.0 - turn_abs
    along = stay * along + turn_abs * along_turn
    across = stay * across + turn_abs * across_turn
    local = [base + along, across, base - along]
    west, east, south, north = fluxes
    rims = zero
    for s in range(3):
        partial = near_products[0] * (local[s] - ((west[s] + east[s]) + (south[s] + north[s])))
        partial = partial + near_products[1] * jnp.where(lane == 0, 0.0, pltpu.roll(west[s], 1, 1))
        partial = partial + near_products[2] * jnp.where(lane == LANES - 1, 0.0, pltpu.roll(east[s], LANES - 1, 1))
        partial = partial + near_products[3] * jnp.where(row == 0, 0.0, pltpu.roll(south[s], 1, 0))
        partial = partial + near_products[4] * jnp.where(row == ROWS - 1, 0.0, pltpu.roll(north[s], ROWS - 1, 0))
        beside_send[s] = partial
        across_send[0, s] = partial[8:]
        across_send[0, s, 0:1, :] = south[s][ROWS - 1 :]
        across_send[1, s] = partial[:8]
        across_send[1, s, 7:8, :] = north[s][:1]
        beside_send[4, s : s + 1, :] = south[s][ROWS - 1 :]
        beside_send[4, 8 + s : 9 + s, :] = north[s][:1]
        rims = jnp.where(lane == LANES - 1 - s, pltpu.roll(west[s], (LANES - s) % LANES, 1) if s else west[s], rims)
        rims = jnp.where(lane == s, pltpu.roll(east[s], s, 1) if s else east[s], rims)
    for n, values in enumerate((plain_along, plain_across)):
        across_send[0, n, 1:2, :] = values[ROWS - 1 :]
        across_send[1, n, 6:7, :] = values[:1]
        beside_send[4, 3 + n : 4 + n, :] = values[ROWS - 1 :]
        beside_send[4, 11 + n : 12 + n, :] = values[:1]
    beside_send[3] = rims
    across_send[0, 3] = rims[8:]
    across_send[1, 3] = rims[:8]

    def stress_copy(n):
        dy, dx = AROUND[n]
        if dy == 0:
            source, target = beside_send, beside_land.at[{1: 1, -1: 0}[dx]]
        else:
            source = across_send.at[{1: 0, -1: 1}[dy]]
            target = across_land.at[{0: 0, 1: 2, -1: 1}[dx], {1: 1, -1: 0}[dy]]
        return pltpu.make_async_remote_copy(
            src_ref=source,
            dst_ref=target,
            send_sem=stress_sem.at[0, n],
            recv_sem=stress_sem.at[1, n],
            device_id=device(dy, dx),
            device_id_type=MESH,
        )

    for n, (dy, dx) in enumerate(AROUND):

        @pl.when(exists(dy, dx))
        def _():
            stress_copy(n).start()

    for step in FAR_FIRST:
        pack_copy(step, True).wait_recv()
    for n in range(2):

        @pl.when(vertical[n])
        def _():
            band_copy(n, 1).start()

    start_halo(2)
    start_halo(3)
    for n in range(2):

        @pl.when(from_side[n])
        def _():
            band_copy(n, 0).wait_recv()

    def all_rows(ref, first):
        return tiles_of(ref, pl.ds(first, SLOTS, stride=8))

    far_masks = [all_rows(window, 6), all_rows(window, 7)]
    masks = jnp.dot(
        jnp.concatenate(far_masks, axis=0).astype(jnp.bfloat16), spread, preferred_element_type=jnp.float32
    )
    ocean_mask = [masks[:SLOTS], masks[:SLOTS], masks[SLOTS:]]
    eastward = [all_rows(window, c) * ocean_mask[c] for c in range(3)]
    northward = [all_rows(window, 3 + c) * ocean_mask[c] for c in range(3)]
    east_y, north_y = along_y(eastward), along_y(northward)
    vorticity = [along_x(northward[c]) - east_y[c] for c in range(3)]
    divergence = [along_x(eastward[c]) + north_y[c] for c in range(3)]
    coarse = []
    for values in (vorticity, divergence):
        coarse.append(2.0 * values[0] + values[1])
        coarse.append(values[1] + 2.0 * values[2])
    coarse = exact_dot(jnp.concatenate(coarse, axis=0), restriction(2 * LANES)) * (1.0 / 9.0)
    coarse = TURN_GAIN * jnp.tanh(coarse)
    for c in range(2):
        placed = ocean_shift(far_masks[c], -MARGIN_W)
        for t in range(2):
            span = slice(LANES * t, LANES * (t + 1))
            mask_window[t, pl.ds(c, SLOTS, stride=2), :] = placed[:, span]
            turn_window[t, pl.ds(c, SLOTS, stride=2), :] = coarse[SLOTS * c : SLOTS * (c + 1), span]
        fields_out[pl.ds(ROWS + c, 8, stride=2), :] = coarse[SLOTS * (2 + c) : SLOTS * (2 + c) + 8, :LANES]
    fields_out[:ROWS, :] = turn_window[0, :ROWS, :]
    products = mask_products()
    for n, values in enumerate(products):
        fields_out[(2 + n) * ROWS : (3 + n) * ROWS, :] = values[:ROWS, :LANES]
    around, west_mask, east_mask, south_mask, north_mask = products

    prepare_first, update, finish_rows = wave_tools(fields_out, rows_out, cols_out, cells, beside, updated)
    for n in range(2):
        wait_halo(n)
    prepare_first()

    def one_step(i, angle):
        update(i, angle)
        return next_angle(*angle)

    angle = lax.fori_loop(0, DURING_STRESS, one_step, angle_at(0))

    for n in range(2):

        @pl.when(from_side[n])
        def _():
            band_copy(n, 1).wait_recv()

    surface = [all_rows(window_late, c) * ocean_mask[c] for c in range(3)]
    bottom = [all_rows(window_late, 3 + c) for c in range(3)]
    safe = [jnp.where(bottom[c] > 0.0, bottom[c], 1.0) for c in range(3)]
    inverse = [-STRESS_GAIN / safe[c] for c in range(3)]

    def raise_surface(surface, eastward, northward):
        flow_y = along_y([bottom[c] * northward[c] for c in range(3)])
        return [
            (surface[c] - GRAVITY_STEP * (along_x(bottom[c] * eastward[c]) + flow_y[c])) * ocean_mask[c]
            for c in range(3)
        ]

    def push(surface, eastward, northward):
        slope = along_y(surface)
        new_east = [
            eastward[c] + GRAVITY_STEP * (CORIOLIS_STEP * northward[c] - along_x(surface[c])) for c in range(3)
        ]
        new_north = [northward[c] + GRAVITY_STEP * (-CORIOLIS_STEP * eastward[c] - slope[c]) for c in range(3)]
        return new_east, new_north

    surface = raise_surface(surface, eastward, northward)
    pushed = push(surface, eastward, northward)
    wave_lane, fine = iota(wide, 0), iota(wide, 1)
    wave_lane = jnp.where(wave_lane < LANES + 64, wave_lane + MARGIN_W, wave_lane - 2 * LANES + MARGIN_W)
    first = 2 * (fine // 3)
    part = fine % 3
    hits = jnp.where(wave_lane == first, 1.0, 0.0) * jnp.where(part == 0, 1.0, jnp.where(part == 1, 0.5, 0.0)) + jnp.where(
        wave_lane == first + 1, 1.0, 0.0
    ) * jnp.where(part == 2, 1.0, jnp.where(part == 1, 0.5, 0.0))
    prolong = hits.astype(jnp.bfloat16)

    for n, (dy, dx) in enumerate(AROUND):

        @pl.when(exists(-dy, -dx))
        def _():
            stress_copy(n).wait_recv()

    side_lane = iota((2 * ROWS, LANES), 1) < 64

    def assemble(s):
        columns = [
            jnp.concatenate([body, across_land[n, 0, s], across_land[n, 1, s]], axis=0)
            for n, body in enumerate((beside_send[s], beside_land[0, s], beside_land[1, s]))
        ]
        return jnp.concatenate([columns[0], jnp.where(side_lane, columns[1], columns[2])], axis=1)

    def edge_row(place):
        rows = [ref[place : place + 1, :] for ref in (beside_send.at[4], beside_land.at[0, 4], beside_land.at[1, 4])]
        return jnp.concatenate([rows[0], jnp.where(side_lane[:1], rows[1], rows[2])], axis=1)

    around_row = iota((2 * ROWS, 2 * LANES), 0)
    around_lane = iota((2 * ROWS, 2 * LANES), 1)
    west_side = west_mask * jnp.where(around_lane % LANES == 0, 1.0, 0.0)
    east_side = east_mask * jnp.where(around_lane % LANES == LANES - 1, 1.0, 0.0)
    side_flux = assemble(3)
    pieces = []
    bodies = [assemble(s) for s in range(3)]

    def edge_rows(n):
        low, high = edge_row(11 + n), edge_row(3 + n)
        values = jnp.where(around_row == 0, low, jnp.where(around_row == ROWS - 1, high, 0.0))
        values = jnp.where(around_row == ROWS, bodies[n][22:23], values)
        return jnp.where(around_row == 2 * ROWS - 1, bodies[n][25:26], values)

    edge_along, edge_across = edge_rows(0), edge_rows(1)
    edge_turn = tiles_of(turn_window, slice(None))
    edge_signed = jnp.where(edge_turn > 0.0, turn_s, -turn_s)
    edge_scale = around * jnp.abs(edge_turn)
    along_change = edge_scale * (edge_along * (turn_c - 1.0) - edge_across * edge_signed)
    across_change = edge_scale * (edge_across * (turn_c - 1.0) + edge_along * edge_signed)
    changes = (along_change, across_change, -along_change)
    for s in range(3):
        body = bodies[s] + changes[s]
        from_south = jnp.where(
            around_row == 0, bodies[s][24:25], jnp.where(around_row == ROWS, edge_row(s), 0.0)
        )
        from_north = jnp.where(
            around_row == ROWS - 1, bodies[s][23:24], jnp.where(around_row == 2 * ROWS - 1, edge_row(8 + s), 0.0)
        )
        body = body + west_side * pltpu.roll(side_flux, s + 1, 1)
        body = body + east_side * pltpu.roll(side_flux, 2 * LANES - 1 - s, 1)
        body = body + south_mask * from_south + north_mask * from_north
        for t in range(2):
            stress[s, t] = body[:, LANES * t : LANES * (t + 1)]
        for c in range(2):
            pieces.append(
                jnp.concatenate([stress[s, t, pl.ds(c, SLOTS, stride=2), :] for t in range(2)], axis=1)
            )
    spread_stress = exact_dot(jnp.concatenate(pieces, axis=0), prolong)
    tensor = []
    for s in range(3):
        low = spread_stress[2 * SLOTS * s : 2 * SLOTS * s + SLOTS]
        high = spread_stress[2 * SLOTS * s + SLOTS : 2 * SLOTS * (s + 1)]
        tensor.append([low, 0.5 * low + 0.5 * high, high])
    cross_y, normal_y = along_y(tensor[1]), along_y(tensor[2])
    force_x = [inverse[c] * (along_x(tensor[0][c]) + cross_y[c]) for c in range(3)]
    force_y = [inverse[c] * (along_x(tensor[1][c]) + normal_y[c]) for c in range(3)]

    for step in range(ITERS):
        if step > 0:
            surface = raise_surface(surface, eastward, northward)
            pushed = push(surface, eastward, northward)
        eastward = [(pushed[0][c] + force_x[c]) * ocean_mask[c] for c in range(3)]
        northward = [(pushed[1][c] + force_y[c]) * ocean_mask[c] for c in range(3)]

    is_even = lax.rem(x, 2) == 0
    low_lanes = iota((8, LANES), 1) < 64
    halves = []
    for f, values in enumerate((surface, eastward, northward)):
        for c in range(3):
            own = values[c][:8]
            low, high = ocean_shift(own, -MARGIN_O), ocean_shift(own, 64 - MARGIN_O)
            place = 8 * (3 * f + c)
            result[place : place + 8, :] = jnp.where(is_even, low[:, :LANES], high[:, LANES:])
            halves.append(jnp.where(is_even, low[:, LANES:], pltpu.roll(high[:, :LANES], 64, 1)))
    for m in range(5):
        merged = halves[m] if m == 4 else jnp.where(low_lanes, halves[m], pltpu.roll(halves[5 + m], 64, 1))
        result[72 + 8 * m : 80 + 8 * m, :] = merged
    for dest in range(PEERS):
        result_send[dest, 0:8, :] = result[pl.ds(dest, 8, stride=8), :]
        result_send[dest, 8:14, :] = result[pl.ds(64 + dest, 6, stride=8), :]

    def result_copy(step):
        dest = peer(step)
        return pltpu.make_async_remote_copy(
            src_ref=result_send.at[dest[2]],
            dst_ref=result_land.at[x],
            send_sem=result_sem.at[0, step],
            recv_sem=result_sem.at[1, step],
            device_id=dest,
            device_id_type=MESH,
        )

    for step in FAR_FIRST:
        result_copy(step).start()
    result_land[x] = result_send[x]
    lax.fori_loop(DURING_STRESS, QUARTER, one_step, angle)
    for step in FAR_FIRST:
        pack_copy(step, False).wait_send()
        pack_copy(step, True).wait_send()
    for n in range(2):

        @pl.when(vertical[n])
        def _():
            band_copy(n, 0).wait_send()
            band_copy(n, 1).wait_send()

    for n, (dy, dx) in enumerate(AROUND):

        @pl.when(exists(dy, dx))
        def _():
            stress_copy(n).wait_send()

    for n in range(2, 4):
        wait_halo(n)

    def fix_step(i, angle):
        finish_rows(i, angle)
        return next_angle(*angle)

    lax.fori_loop(0, QUARTER, fix_step, angle_at(0))
    for n in range(4):

        @pl.when(sends[n])
        def _():
            halo_copy(n).wait_send()

    for step in FAR_FIRST:
        result_copy(step).wait_recv()
    for q in range(PEERS // 2):
        left, right = result_land[2 * q], result_land[2 * q + 1]
        left_turned, right_turned = pltpu.roll(left, 64, 1), pltpu.roll(right, 64, 1)
        side = iota((5, LANES), 1) < 64
        middle = jnp.concatenate(
            [
                jnp.where(side, left[9:14], right_turned[9:14]),
                jnp.where(side[:4], left_turned[9:13], right[9:13]),
            ],
            axis=0,
        )
        for t, tile in enumerate((left, middle, right)):
            lanes = pl.ds((3 * q + t) * LANES, LANES)
            for f in range(3):
                ocean_out[f, :, lanes] = tile[3 * f : 3 * f + 3]

    for step in FAR_FIRST:
        result_copy(step).wait_send()


def hand_over(ocean_in, updated, out, ocean_out, store_sem, local_sem):
    handed = pltpu.make_async_copy(ocean_in, ocean_out, local_sem)
    handed.start()
    size = CELLS // CHUNKS
    copies = [
        pltpu.make_async_copy(updated.at[pl.ds(n * size, size)], out.at[pl.ds(n * size, size)], store_sem.at[n])
        for n in range(CHUNKS)
    ]
    for copy in copies:
        copy.start()
    for copy in copies:
        copy.wait()
    handed.wait()


def shards(mesh_shape, spectrum, sea_mask, ocean_state, depth):
    groups_y = mesh_shape["gy"]
    groups = groups_y * mesh_shape["sec"]
    cells = spectrum.reshape(CELLS, LANES)
    vmem = pl.BlockSpec(memory_space=pltpu.VMEM)
    anywhere = pl.BlockSpec(memory_space=pl.ANY)
    f32 = jnp.float32
    dma = pltpu.SemaphoreType.DMA
    ocean_part, updated = pl.pallas_call(
        functools.partial(coupled_kernel, groups_y, groups),
        out_shape=(
            jax.ShapeDtypeStruct(ocean_state.shape, f32),
            jax.ShapeDtypeStruct((CELLS, LANES), f32),
        ),
        in_specs=[anywhere] * 4,
        out_specs=(vmem, vmem),
        scratch_shapes=[
            pltpu.VMEM((7 * ROWS, LANES), f32),
            pltpu.VMEM((2, HALF, LANES), f32),
            pltpu.VMEM((2, 6, ROWS, LANES), f32),
            pltpu.VMEM((CELLS + 2 * PAD, LANES), f32),
            pltpu.VMEM((4 * NFREQ, ROWS, LANES), f32),
            pltpu.VMEM(ocean_state.shape, f32),
            pltpu.VMEM(depth.shape, f32),
            pltpu.VMEM(sea_mask.shape, jnp.int32),
            pltpu.VMEM((SLOTS, 1792), f32),
            pltpu.VMEM((8, 1280), f32),
            pltpu.VMEM((PEERS, 2, 8, LANES), f32),
            pltpu.VMEM((PEERS, 2, 8, LANES), f32),
            pltpu.VMEM((2, SLOTS * 8, LANES), f32),
            pltpu.VMEM((2, SLOTS * 8, LANES), f32),
            pltpu.VMEM((2, 2 * ROWS, LANES), f32),
            pltpu.VMEM((2, 2 * ROWS, LANES), f32),
            pltpu.VMEM((5, ROWS, LANES), f32),
            pltpu.VMEM((2, 4, 8, LANES), f32),
            pltpu.VMEM((2, 5, ROWS, LANES), f32),
            pltpu.VMEM((3, 2, 4, 8, LANES), f32),
            pltpu.VMEM((3, 2, 2 * ROWS, LANES), f32),
            pltpu.VMEM((112, LANES), f32),
            pltpu.VMEM((PEERS, SLOTS, LANES), f32),
            pltpu.VMEM((PEERS, SLOTS, LANES), f32),
            pltpu.VMEM((2, HALF, LANES), f32),
            pltpu.VMEM((6, ROWS, LANES), f32),
            dma((3,)),
            dma((4 * LOADS,)),
            dma((2, PEERS)),
            dma((2, PEERS)),
            dma((2, 4)),
            dma((2, 8)),
            dma((2, PEERS)),
            dma((2, 4)),
            dma((4,)),
        ],
        compiler_params=pltpu.CompilerParams(
            collective_id=0, has_side_effects=True, vmem_limit_bytes=VMEM_LIMIT
        ),
        name="coupled",
    )(*[pltpu.with_memory_space_constraint(a, pltpu.HBM) for a in (cells, sea_mask, ocean_state, depth)])
    spectrum_out, ocean_out = pl.pallas_call(
        hand_over,
        out_shape=(jax.ShapeDtypeStruct((CELLS, LANES), f32), jax.ShapeDtypeStruct(ocean_state.shape, f32)),
        in_specs=[anywhere, anywhere],
        out_specs=(anywhere, anywhere),
        scratch_shapes=[dma((CHUNKS,)), dma],
        compiler_params=pltpu.CompilerParams(vmem_limit_bytes=VMEM_LIMIT),
        name="hand_over",
    )(ocean_part, updated)
    return (spectrum_out.reshape(spectrum.shape), ocean_out)


def solution(mesh):
    return jax.shard_map(
        functools.partial(shards, dict(mesh.shape)),
        mesh=mesh,
        in_specs=(
            P(None, None, ("sec", "gy"), "gx"),
            P(("sec", "gy", "gx"), None),
            P(None, ("sec", "gy", "gx"), None),
            P(("sec", "gy", "gx"), None),
        ),
        out_specs=(P(None, None, ("sec", "gy"), "gx"), P(None, ("sec", "gy", "gx"), None)),
        check_vma=False,
    )
```

```python
import functools
import math

import jax
import jax.numpy as jnp
from jax import lax
from jax.experimental import pallas as pl
from jax.experimental.pallas import tpu as pltpu
from jax.sharding import PartitionSpec as P

ITERS = 4
GRAVITY_STEP = 0.3
CORIOLIS_STEP = 0.2
STRESS_GAIN = 2.0
TURN_GAIN = 0.2
SPEED_BASE = 0.35
SPEED_RATIO = 0.9

NDIR = 36
NFREQ = 20
ROWS = 16
LANES = 128
CELLS = NDIR * NFREQ * ROWS
PER_DIR = NFREQ * ROWS
QUARTER = NDIR // 4
PAD = 8
DURING_STRESS = 2
CHUNKS = 8
LOADS = 3
VMEM_LIMIT = 28 * 1024 * 1024
HALF = NDIR // 2 * NFREQ
PEERS = 8
SLOTS = 16
MARGIN_O = 24
MARGIN_W = 16
SPEEDS = [SPEED_BASE * SPEED_RATIO**j for j in range(NFREQ)]
STEP_ANGLE = 2.0 * math.pi / NDIR
MESH = pl.DeviceIdType.MESH
AROUND = [(1, 1), (1, -1), (-1, 1), (-1, -1), (1, 0), (-1, 0), (0, 1), (0, -1)]
FAR_FIRST = (4, 3, 5, 2, 6, 1, 7)


def iota(shape, dim):
    return lax.broadcasted_iota(jnp.int32, shape, dim)


def next_angle(cosine, sine):
    turn_c, turn_s = math.cos(STEP_ANGLE), math.sin(STEP_ANGLE)
    return cosine * turn_c - sine * turn_s, sine * turn_c + cosine * turn_s


def angle_at(i):
    return jnp.float32(math.cos((i + 0.5) * STEP_ANGLE)), jnp.float32(math.sin((i + 0.5) * STEP_ANGLE))


def exact_dot(values, weights):
    rows = values.shape[0]
    high = values.astype(jnp.bfloat16)
    rest = values - high.astype(jnp.float32)
    middle = rest.astype(jnp.bfloat16)
    low = (rest - middle.astype(jnp.float32)).astype(jnp.bfloat16)
    stacked = jnp.concatenate([high, middle, low], axis=0)
    product = jnp.dot(stacked, weights, preferred_element_type=jnp.float32)
    return product[:rows] + product[rows : 2 * rows] + product[2 * rows :]


def ocean_shift(values, amount):
    return pltpu.roll(values, amount % values.shape[1], 1)


def along_x(values):
    return (ocean_shift(values, -1) - ocean_shift(values, 1)) * 0.5


def along_y(classes):
    above = [classes[1], classes[2], pltpu.roll(classes[0], SLOTS - 1, 0)]
    below = [pltpu.roll(classes[2], 1, 0), classes[0], classes[1]]
    return [(above[c] - below[c]) * 0.5 for c in range(3)]


def wave_tools(fields, rows, cols, cells, beside, target):
    lane = iota((8, LANES), 1)
    row = iota((8, LANES), 0)

    def half(n, h):
        return fields[ROWS * n + 8 * h : ROWS * n + 8 * h + 8, :]

    def turn_part(h):
        return half(2, h) * jnp.abs(half(0, h))

    def cell(direction, j, offset):
        place = direction * PER_DIR + (PAD + j * ROWS + offset)
        return cells[pl.ds(pl.multiple_of(place, 8) if offset % 8 == 0 else place, 8), :]

    odd = lax.rem(lane, 2) == 1

    def rims(i, h):
        columns = []
        for place in (i, QUARTER + i):
            group, part = place // 3, lax.rem(place, 3)
            span = slice(8 * h, 8 * h + 8)
            merged = jnp.where(odd, cols[0, group, span, :], cols[1, group, span, :])
            columns.append(pltpu.roll(merged, lax.rem(LANES - part * (2 * NFREQ), LANES), 1))
        return columns

    def rim_at(columns, j):
        return [pltpu.roll(column, LANES - 1 - 2 * j, 1) for column in columns]

    def prepare(i, h, j, columns, rim):
        following = rim_at(columns, j + 1)
        for q in range(4):
            value = cell(q * QUARTER + i, j, 8 * h)
            if q in (0, 3):
                moved = jnp.where(lane == 0, rim[q // 2], pltpu.roll(value, 1, 1))
            else:
                moved = jnp.where(lane == LANES - 1, following[q // 2], pltpu.roll(value, LANES - 1, 1))
            beside[q * NFREQ + j, 8 * h : 8 * h + 8, :] = moved
        return following

    def update(i, angle):
        cosine, sine = angle
        following_step = jnp.minimum(i + 1, QUARTER - 1)
        for h in range(2):
            columns = rims(following_step, h)
            rim = rim_at(columns, 0)
            turn_left = half(0, h) > 0.0
            shift_up = half(1, h) > 0.0
            mask = half(2, h)
            turned = turn_part(h)
            stay = mask - turned
            shifted = mask * half(1, h)
            leave = mask * (cosine + sine)
            factors = []
            for q in range(4):
                speed_x, speed_y = (cosine, sine) if q % 2 == 0 else (sine, cosine)
                inner = half(5 if q in (0, 1) else 6, h) * speed_y
                if q in (0, 1) and h == 0:
                    inner = jnp.where(row == 0, 0.0, inner)
                if q in (2, 3) and h == 1:
                    inner = jnp.where(row == 7, 0.0, inner)
                factors.append((half(3 if q in (0, 3) else 4, h) * speed_x, inner))
            values = [cell(q * QUARTER + i, 0, 8 * h) for q in range(4)]
            faces = [None] * 4
            for j in range(NFREQ):
                keep = stay - SPEEDS[j] * leave
                for q in range(4):
                    direction = q * QUARTER + i
                    before, after = direction - 1, direction + 1
                    if q == 0:
                        before = jnp.where(i == 0, NDIR - 1, before)
                    if q == 3:
                        after = jnp.where(i == QUARTER - 1, 0, after)
                    along = cell(direction, j, 8 * h + (-1 if q in (0, 1) else 1))
                    moved = factors[q][0] * beside[q * NFREQ + j, 8 * h : 8 * h + 8, :] + factors[q][1] * along
                    total = keep * values[q] + SPEEDS[j] * moved
                    total = total + turned * jnp.where(turn_left, cell(before, j, 8 * h), cell(after, j, 8 * h))
                    if j > 0:
                        total = total + faces[q]
                    if j < NFREQ - 1:
                        following = cell(direction, j + 1, 8 * h)
                        faces[q] = shifted * jnp.where(shift_up, values[q], following)
                        total = total - faces[q]
                        values[q] = following
                    place = (direction * NFREQ + j) * ROWS + 8 * h
                    target[pl.ds(pl.multiple_of(place, 8), 8), :] = total
                rim = prepare(following_step, h, j, columns, rim)

    def prepare_first():
        for h in range(2):
            columns = rims(0, h)
            rim = rim_at(columns, 0)
            for j in range(NFREQ):
                rim = prepare(0, h, j, columns, rim)

    def finish_rows(i, angle):
        for q in range(4):
            speed_y = angle[1] if q % 2 == 0 else angle[0]
            from_south = q in (0, 1)
            edge = (5 * ROWS) if from_south else (7 * ROWS - 1)
            factor = fields[edge : edge + 1, :] * speed_y
            direction = q * QUARTER + i
            source = (direction if from_south else direction - 2 * QUARTER) * NFREQ
            for first, done in ((0, 0), (8, 0), (NFREQ - 8, 4)):
                speeds = jnp.zeros((8, LANES), jnp.float32)
                for r in range(done, 8):
                    speeds = jnp.where(row == r, SPEEDS[first + r], speeds)
                span = pl.ds((direction * NFREQ + first) * ROWS + (0 if from_south else ROWS - 1), 8, stride=ROWS)
                rim = rows[0 if from_south else 1, pl.ds(source + first, 8), :]
                target[span, :] = target[span, :] + speeds * (factor * rim)

    return prepare_first, update, finish_rows


def coupled_kernel(
    groups_y,
    groups,
    spectrum,
    sea_mask,
    ocean_state,
    depth,
    ocean_out,
    updated,
    fields_out,
    rows_out,
    cols_out,
    cells,
    beside,
    state_in,
    depth_in,
    mask_in,
    raw,
    raw_mask,
    pack,
    pack_late,
    window,
    window_late,
    mask_window,
    turn_window,
    beside_send,
    across_send,
    beside_land,
    across_land,
    stress,
    result,
    result_send,
    result_land,
    rows_send,
    cols_send,
    input_sem,
    load_sem,
    pack_sem,
    late_sem,
    band_sem,
    stress_sem,
    result_sem,
    halo_sem,
    local_sem,
):
    x = lax.axis_index("gx")
    y = lax.axis_index("sec") * groups_y + lax.axis_index("gy")

    def exists(dy, dx):
        checks = []
        if dy > 0:
            checks.append(y < groups - 1)
        if dy < 0:
            checks.append(y > 0)
        if dx > 0:
            checks.append(x < PEERS - 1)
        if dx < 0:
            checks.append(x > 0)
        answer = checks[0]
        for check in checks[1:]:
            answer = jnp.logical_and(answer, check)
        return answer

    def device_at(row, column):
        return (row // groups_y, lax.rem(row, groups_y), column)

    def device(dy, dx):
        return device_at(y + dy, x + dx)

    def peer(step):
        return (lax.axis_index("sec"), lax.axis_index("gy"), lax.rem(x + step, PEERS))

    inputs = [
        pltpu.make_async_copy(ocean_state, state_in, input_sem.at[0]),
        pltpu.make_async_copy(depth, depth_in, input_sem.at[1]),
        pltpu.make_async_copy(sea_mask, mask_in, input_sem.at[2]),
    ]
    for copy in inputs:
        copy.start()

    barrier = pltpu.get_barrier_semaphore()
    greeted = PEERS - 1
    for dy, dx in AROUND:
        if dy != 0:
            here = exists(dy, dx)

            @pl.when(here)
            def _():
                pl.semaphore_signal(barrier, inc=1, device_id=device(dy, dx), device_id_type=MESH)

            greeted = greeted + here.astype(jnp.int32)

    for step in FAR_FIRST:
        pl.semaphore_signal(barrier, inc=1, device_id=peer(step), device_id_type=MESH)

    def load(q, part):
        size = QUARTER // LOADS * PER_DIR
        start = pl.multiple_of(q * (QUARTER * PER_DIR) + part * size, PER_DIR)
        return pltpu.make_async_copy(
            spectrum.at[pl.ds(start, size)],
            cells.at[pl.ds(pl.multiple_of(start + PAD, 8), size)],
            load_sem.at[part * 4 + q],
        )

    for part in range(LOADS):
        for q in range(4):
            load(q, part).start()

    raw[...] = jnp.zeros_like(raw)
    raw_mask[...] = jnp.zeros_like(raw_mask)
    width = state_in.shape[2]
    for copy in inputs:
        copy.wait()
    raw[0:3, :width] = state_in[1]
    raw[3:6, :width] = state_in[2]
    raw[8:11, :width] = state_in[0]
    raw[11:14, :width] = depth_in[...]
    raw_mask[6:8, : mask_in.shape[1]] = mask_in[...].astype(jnp.float32)
    even = ocean_shift(raw[...], MARGIN_O)
    odd = ocean_shift(raw[...], MARGIN_O - 64)
    mask_rows = ocean_shift(raw_mask[...], MARGIN_W)
    is_ocean = iota((8, LANES), 0) < 6
    for dest in range(PEERS):
        source = odd if dest % 2 else even
        origin = 384 * (dest // 2) + (128 if dest % 2 else 0)
        for tile in range(2):
            piece = source[:, origin + LANES * tile : origin + LANES * (tile + 1)]
            pack[dest, tile] = jnp.where(
                is_ocean, piece[:8], mask_rows[:, LANES * (dest + tile) : LANES * (dest + tile + 1)]
            )
            pack_late[dest, tile] = piece[8:]

    slot = pl.ds(pl.multiple_of(x * 8, 8), 8)

    def pack_copy(step, late):
        dest = peer(step)
        return pltpu.make_async_remote_copy(
            src_ref=(pack_late if late else pack).at[dest[2]],
            dst_ref=(window_late if late else window).at[:, slot, :],
            send_sem=(late_sem if late else pack_sem).at[0, step],
            recv_sem=(late_sem if late else pack_sem).at[1, step],
            device_id=dest,
            device_id_type=MESH,
        )

    pl.semaphore_wait(barrier, greeted)
    for step in FAR_FIRST:
        pack_copy(step, False).start()
    for step in FAR_FIRST:
        pack_copy(step, True).start()
    mask_window[...] = jnp.zeros_like(mask_window)
    cells[:PAD, :] = jnp.zeros((PAD, LANES), jnp.float32)
    cells[PAD + CELLS :, :] = jnp.zeros((PAD, LANES), jnp.float32)
    for ref in (window, window_late):
        ref[:, 11 * 8 : 13 * 8, :] = jnp.zeros((2, 16, LANES), jnp.float32)
    edge = jnp.zeros((2, 24, LANES), jnp.float32)

    @pl.when(y == 0)
    def _():
        window[:, 13 * 8 : 16 * 8, :] = edge
        window_late[:, 13 * 8 : 16 * 8, :] = edge
        across_land[:, 1] = jnp.zeros((3, 4, 8, LANES), jnp.float32)

    @pl.when(y == groups - 1)
    def _():
        window[:, 8 * 8 : 11 * 8, :] = edge
        window_late[:, 8 * 8 : 11 * 8, :] = edge
        across_land[:, 0] = jnp.zeros((3, 4, 8, LANES), jnp.float32)

    @pl.when(x == 0)
    def _():
        beside_land[1] = jnp.zeros((5, ROWS, LANES), jnp.float32)
        across_land[2] = jnp.zeros((2, 4, 8, LANES), jnp.float32)

    @pl.when(x == PEERS - 1)
    def _():
        beside_land[0] = jnp.zeros((5, ROWS, LANES), jnp.float32)
        across_land[1] = jnp.zeros((2, 4, 8, LANES), jnp.float32)

    window[:, slot, :] = pack[x]
    window_late[:, slot, :] = pack_late[x]

    lane = iota((ROWS, LANES), 1)
    row = iota((ROWS, LANES), 0)
    zero = jnp.zeros((ROWS, LANES), jnp.float32)

    def gather(i, carry):
        (cosine, sine), plain, fluxes = carry
        part = QUARTER // LOADS

        @pl.when(lax.rem(i, part) == 0)
        def _():
            for q in range(4):
                load(q, i // part).wait()

        totals, weighted, rims = [None] * 4, [None] * 4, [zero, zero]
        for j in range(NFREQ):
            values = []
            for q in range(4):
                base = (q * QUARTER + i) * PER_DIR + PAD
                values.append(cells[pl.ds(pl.multiple_of(base + j * ROWS, 8), ROWS), :])
                scaled = values[q] * SPEEDS[j]
                totals[q] = values[q] if j == 0 else totals[q] + values[q]
                weighted[q] = scaled if j == 0 else weighted[q] + scaled
            here = jnp.logical_or(lane == 2 * j + 1, lane == 2 * j + 2)
            for n, (east, west) in enumerate(((0, 1), (3, 2))):
                both = jnp.where(lane == LANES - 1, values[east], values[west])
                rims[n] = jnp.where(here, pltpu.roll(both, 2 * j + 2, 1), rims[n])
        for n in range(2):
            place = i + n * QUARTER
            group, part = place // 3, lax.rem(place, 3)
            earlier = jnp.where(part > 0, cols_send[group], zero)
            cols_send[group] = earlier + pltpu.roll(rims[n], part * (2 * NFREQ), 1)
        scale = 0.5 / (NDIR * NFREQ)
        cc, cs, ss = cosine * cosine * scale, cosine * sine * scale, sine * sine * scale
        pair = (totals[0] + totals[2]) - (totals[1] + totals[3])
        plain = (
            plain[0] + ((totals[0] + totals[2]) + (totals[1] + totals[3])),
            plain[1] + (cc - ss) * pair,
            plain[2] + (2.0 * cs) * pair,
        )
        straight, crossed = (cc, cs, ss), (ss, -cs, cc)
        west, east, south, north = fluxes
        west = tuple(
            west[s] + (cosine * straight[s]) * weighted[0] + (sine * crossed[s]) * weighted[3] for s in range(3)
        )
        east = tuple(
            east[s] + (cosine * straight[s]) * weighted[2] + (sine * crossed[s]) * weighted[1] for s in range(3)
        )
        south = tuple(
            south[s] + (sine * straight[s]) * weighted[0] + (cosine * crossed[s]) * weighted[1] for s in range(3)
        )
        north = tuple(
            north[s] + (sine * straight[s]) * weighted[2] + (cosine * crossed[s]) * weighted[3] for s in range(3)
        )
        return next_angle(cosine, sine), plain, (west, east, south, north)

    cols_send[...] = jnp.zeros_like(cols_send)
    triple = (zero, zero, zero)
    carry = (angle_at(0), triple, (triple, triple, triple, triple))
    _, plain, fluxes = lax.fori_loop(0, QUARTER, gather, carry)

    def pack_rows(n, carry):
        for m in range(5):
            start = n * 40 + m * 8
            span = pl.ds(pl.multiple_of(start, 8), 8)
            rows_send[0, span, :] = cells[pl.ds(start * ROWS + (PAD + ROWS - 1), 8, stride=ROWS), :]
            rows_send[1, span, :] = cells[pl.ds(start * ROWS + (PAD + HALF * ROWS), 8, stride=ROWS), :]
        return carry

    lax.fori_loop(0, HALF // 40, pack_rows, 0)

    sends = (exists(0, 1), exists(0, -1), exists(1, 0), exists(-1, 0))
    receives = (exists(0, -1), exists(0, 1), exists(-1, 0), exists(1, 0))

    def halo_ends(n):
        return (cols_send, cols_out.at[n]) if n < 2 else (rows_send.at[n - 2], rows_out.at[n - 2])

    def halo_copy(n):
        source, target = halo_ends(n)
        return pltpu.make_async_remote_copy(
            src_ref=source,
            dst_ref=target,
            send_sem=halo_sem.at[0, n],
            recv_sem=halo_sem.at[1, n],
            device_id=(device(0, 1), device(0, -1), device(1, 0), device(-1, 0))[n],
            device_id_type=MESH,
        )

    def halo_fill(n):
        source, target = halo_ends(n)
        return pltpu.make_async_copy(source, target, local_sem.at[n])

    def start_halo(n):
        @pl.when(sends[n])
        def _():
            halo_copy(n).start()

        @pl.when(jnp.logical_not(receives[n]))
        def _():
            halo_fill(n).start()

    def wait_halo(n):
        @pl.when(receives[n])
        def _():
            halo_copy(n).wait_recv()

        @pl.when(jnp.logical_not(receives[n]))
        def _():
            halo_fill(n).wait()

    start_halo(0)
    start_halo(1)

    for step in FAR_FIRST:
        pack_copy(step, False).wait_recv()

    def band_copy(n, late):
        source = pl.ds((5 if n == 0 else 0) * 8, 24)
        target = pl.ds((13 if n == 0 else 8) * 8, 24)
        ref = window_late if late else window
        return pltpu.make_async_remote_copy(
            src_ref=ref.at[:, source, :],
            dst_ref=ref.at[:, target, :],
            send_sem=band_sem.at[0, 2 * n + late],
            recv_sem=band_sem.at[1, 2 * n + late],
            device_id=device(1 if n == 0 else -1, 0),
            device_id_type=MESH,
        )

    vertical = (exists(1, 0), exists(-1, 0))
    from_side = (exists(-1, 0), exists(1, 0))
    for n in range(2):

        @pl.when(vertical[n])
        def _():
            band_copy(n, 0).start()

    def tiles_of(ref, rows):
        return jnp.concatenate([ref[t, rows, :] for t in range(2)], axis=1)

    def own_rows(first):
        return tiles_of(window, pl.ds(first, 8, stride=8))

    wide = (2 * LANES, 2 * LANES)
    spread = (iota(wide, 0) == (2 * iota(wide, 1)) // 3).astype(jnp.bfloat16)
    wave_masks = [own_rows(6), own_rows(7)]
    masks = jnp.dot(
        jnp.concatenate(wave_masks, axis=0).astype(jnp.bfloat16), spread, preferred_element_type=jnp.float32
    )
    near_mask = [masks[:8], masks[:8], masks[8:]]

    def restriction(width):
        fine, wave = iota((2 * LANES, width), 0), iota((2 * LANES, width), 1)
        wave = jnp.where(wave < 3 * LANES // 2, wave, wave - 2 * LANES) + MARGIN_W
        group = 3 * (wave // 2)
        ends = jnp.where(wave % 2 == 0, group, group + 2)
        return jnp.where(fine == ends, 2.0, jnp.where(fine == group + 1, 1.0, 0.0)).astype(jnp.bfloat16)

    near_east = [own_rows(c) * near_mask[c] for c in range(3)]
    near_north = [own_rows(3 + c) * near_mask[c] for c in range(3)]
    near_slope = [
        (near_east[1] - pltpu.roll(near_east[2], 1, 0)) * 0.5,
        (near_east[2] - near_east[0]) * 0.5,
        (pltpu.roll(near_east[0], 7, 0) - near_east[1]) * 0.5,
    ]
    vorticity = [along_x(near_north[c]) - near_slope[c] for c in range(3)]
    coarse = jnp.concatenate([2.0 * vorticity[0] + vorticity[1], vorticity[1] + 2.0 * vorticity[2]], axis=0)
    coarse = TURN_GAIN * jnp.tanh(exact_dot(coarse, restriction(LANES)) * (1.0 / 9.0))
    for c in range(2):
        turn_window[0, pl.ds(c, 8, stride=2), :] = coarse[8 * c : 8 * c + 8]
        placed = ocean_shift(wave_masks[c], -MARGIN_W)
        for t in range(2):
            mask_window[t, pl.ds(c, 8, stride=2), :] = placed[:, LANES * t : LANES * (t + 1)]

    def mask_products():
        around = tiles_of(mask_window, slice(None))
        return (
            around,
            around * pltpu.roll(around, 1, 1),
            around * pltpu.roll(around, 2 * LANES - 1, 1),
            around * pltpu.roll(around, 1, 0),
            around * pltpu.roll(around, 2 * ROWS - 1, 0),
        )

    near_products = [values[:ROWS, :LANES] for values in mask_products()]

    inside = jnp.logical_and(row > 0, row < ROWS - 1)
    turning = jnp.where(inside, turn_window[0, :ROWS, :], 0.0)
    turn_abs = jnp.abs(turning)
    scale = 0.25 / (NDIR * NFREQ)
    base, along, across = plain[0] * scale, plain[1] * 0.5, plain[2] * 0.5
    turn_c, turn_s = math.cos(2.0 * STEP_ANGLE), math.sin(2.0 * STEP_ANGLE)
    plain_along, plain_across = along, across
    signed = jnp.where(turning > 0.0, turn_s, -turn_s)
    along_turn = along * turn_c - across * signed
    across_turn = across * turn_c + along * signed
    stay = 1.0 - turn_abs
    along = stay * along + turn_abs * along_turn
    across = stay * across + turn_abs * across_turn
    local = [base + along, across, base - along]
    west, east, south, north = fluxes
    rims = zero
    for s in range(3):
        partial = near_products[0] * (local[s] - ((west[s] + east[s]) + (south[s] + north[s])))
        partial = partial + near_products[1] * jnp.where(lane == 0, 0.0, pltpu.roll(west[s], 1, 1))
        partial = partial + near_products[2] * jnp.where(lane == LANES - 1, 0.0, pltpu.roll(east[s], LANES - 1, 1))
        partial = partial + near_products[3] * jnp.where(row == 0, 0.0, pltpu.roll(south[s], 1, 0))
        partial = partial + near_products[4] * jnp.where(row == ROWS - 1, 0.0, pltpu.roll(north[s], ROWS - 1, 0))
        beside_send[s] = partial
        across_send[0, s] = partial[8:]
        across_send[0, s, 0:1, :] = south[s][ROWS - 1 :]
        across_send[1, s] = partial[:8]
        across_send[1, s, 7:8, :] = north[s][:1]
        beside_send[4, s : s + 1, :] = south[s][ROWS - 1 :]
        beside_send[4, 8 + s : 9 + s, :] = north[s][:1]
        rims = jnp.where(lane == LANES - 1 - s, pltpu.roll(west[s], (LANES - s) % LANES, 1) if s else west[s], rims)
        rims = jnp.where(lane == s, pltpu.roll(east[s], s, 1) if s else east[s], rims)
    for n, values in enumerate((plain_along, plain_across)):
        across_send[0, n, 1:2, :] = values[ROWS - 1 :]
        across_send[1, n, 6:7, :] = values[:1]
        beside_send[4, 3 + n : 4 + n, :] = values[ROWS - 1 :]
        beside_send[4, 11 + n : 12 + n, :] = values[:1]
    beside_send[3] = rims
    across_send[0, 3] = rims[8:]
    across_send[1, 3] = rims[:8]

    def stress_copy(n):
        dy, dx = AROUND[n]
        if dy == 0:
            source, target = beside_send, beside_land.at[{1: 1, -1: 0}[dx]]
        else:
            source = across_send.at[{1: 0, -1: 1}[dy]]
            target = across_land.at[{0: 0, 1: 2, -1: 1}[dx], {1: 1, -1: 0}[dy]]
        return pltpu.make_async_remote_copy(
            src_ref=source,
            dst_ref=target,
            send_sem=stress_sem.at[0, n],
            recv_sem=stress_sem.at[1, n],
            device_id=device(dy, dx),
            device_id_type=MESH,
        )

    for n, (dy, dx) in enumerate(AROUND):

        @pl.when(exists(dy, dx))
        def _():
            stress_copy(n).start()

    for step in FAR_FIRST:
        pack_copy(step, True).wait_recv()
    for n in range(2):

        @pl.when(vertical[n])
        def _():
            band_copy(n, 1).start()

    start_halo(2)
    start_halo(3)
    for n in range(2):

        @pl.when(from_side[n])
        def _():
            band_copy(n, 0).wait_recv()

    def all_rows(ref, first):
        return tiles_of(ref, pl.ds(first, SLOTS, stride=8))

    far_masks = [all_rows(window, 6), all_rows(window, 7)]
    masks = jnp.dot(
        jnp.concatenate(far_masks, axis=0).astype(jnp.bfloat16), spread, preferred_element_type=jnp.float32
    )
    ocean_mask = [masks[:SLOTS], masks[:SLOTS], masks[SLOTS:]]
    eastward = [all_rows(window, c) * ocean_mask[c] for c in range(3)]
    northward = [all_rows(window, 3 + c) * ocean_mask[c] for c in range(3)]
    east_y, north_y = along_y(eastward), along_y(northward)
    vorticity = [along_x(northward[c]) - east_y[c] for c in range(3)]
    divergence = [along_x(eastward[c]) + north_y[c] for c in range(3)]
    coarse = []
    for values in (vorticity, divergence):
        coarse.append(2.0 * values[0] + values[1])
        coarse.append(values[1] + 2.0 * values[2])
    coarse = exact_dot(jnp.concatenate(coarse, axis=0), restriction(2 * LANES)) * (1.0 / 9.0)
    coarse = TURN_GAIN * jnp.tanh(coarse)
    for c in range(2):
        placed = ocean_shift(far_masks[c], -MARGIN_W)
        for t in range(2):
            span = slice(LANES * t, LANES * (t + 1))
            mask_window[t, pl.ds(c, SLOTS, stride=2), :] = placed[:, span]
            turn_window[t, pl.ds(c, SLOTS, stride=2), :] = coarse[SLOTS * c : SLOTS * (c + 1), span]
        fields_out[pl.ds(ROWS + c, 8, stride=2), :] = coarse[SLOTS * (2 + c) : SLOTS * (2 + c) + 8, :LANES]
    fields_out[:ROWS, :] = turn_window[0, :ROWS, :]
    products = mask_products()
    for n, values in enumerate(products):
        fields_out[(2 + n) * ROWS : (3 + n) * ROWS, :] = values[:ROWS, :LANES]
    around, west_mask, east_mask, south_mask, north_mask = products

    prepare_first, update, finish_rows = wave_tools(fields_out, rows_out, cols_out, cells, beside, updated)
    for n in range(2):
        wait_halo(n)
    prepare_first()

    def one_step(i, angle):
        update(i, angle)
        return next_angle(*angle)

    angle = lax.fori_loop(0, DURING_STRESS, one_step, angle_at(0))

    for n in range(2):

        @pl.when(from_side[n])
        def _():
            band_copy(n, 1).wait_recv()

    surface = [all_rows(window_late, c) * ocean_mask[c] for c in range(3)]
    bottom = [all_rows(window_late, 3 + c) for c in range(3)]
    safe = [jnp.where(bottom[c] > 0.0, bottom[c], 1.0) for c in range(3)]
    inverse = [-STRESS_GAIN / safe[c] for c in range(3)]

    def raise_surface(surface, eastward, northward):
        flow_y = along_y([bottom[c] * northward[c] for c in range(3)])
        return [
            (surface[c] - GRAVITY_STEP * (along_x(bottom[c] * eastward[c]) + flow_y[c])) * ocean_mask[c]
            for c in range(3)
        ]

    def push(surface, eastward, northward):
        slope = along_y(surface)
        new_east = [
            eastward[c] + GRAVITY_STEP * (CORIOLIS_STEP * northward[c] - along_x(surface[c])) for c in range(3)
        ]
        new_north = [northward[c] + GRAVITY_STEP * (-CORIOLIS_STEP * eastward[c] - slope[c]) for c in range(3)]
        return new_east, new_north

    surface = raise_surface(surface, eastward, northward)
    pushed = push(surface, eastward, northward)
    wave_lane, fine = iota(wide, 0), iota(wide, 1)
    wave_lane = jnp.where(wave_lane < LANES + 64, wave_lane + MARGIN_W, wave_lane - 2 * LANES + MARGIN_W)
    first = 2 * (fine // 3)
    part = fine % 3
    hits = jnp.where(wave_lane == first, 1.0, 0.0) * jnp.where(part == 0, 1.0, jnp.where(part == 1, 0.5, 0.0)) + jnp.where(
        wave_lane == first + 1, 1.0, 0.0
    ) * jnp.where(part == 2, 1.0, jnp.where(part == 1, 0.5, 0.0))
    prolong = hits.astype(jnp.bfloat16)

    for n, (dy, dx) in enumerate(AROUND):

        @pl.when(exists(-dy, -dx))
        def _():
            stress_copy(n).wait_recv()

    side_lane = iota((2 * ROWS, LANES), 1) < 64

    def assemble(s):
        columns = [
            jnp.concatenate([body, across_land[n, 0, s], across_land[n, 1, s]], axis=0)
            for n, body in enumerate((beside_send[s], beside_land[0, s], beside_land[1, s]))
        ]
        return jnp.concatenate([columns[0], jnp.where(side_lane, columns[1], columns[2])], axis=1)

    def edge_row(place):
        rows = [ref[place : place + 1, :] for ref in (beside_send.at[4], beside_land.at[0, 4], beside_land.at[1, 4])]
        return jnp.concatenate([rows[0], jnp.where(side_lane[:1], rows[1], rows[2])], axis=1)

    around_row = iota((2 * ROWS, 2 * LANES), 0)
    around_lane = iota((2 * ROWS, 2 * LANES), 1)
    west_side = west_mask * jnp.where(around_lane % LANES == 0, 1.0, 0.0)
    east_side = east_mask * jnp.where(around_lane % LANES == LANES - 1, 1.0, 0.0)
    side_flux = assemble(3)
    pieces = []
    bodies = [assemble(s) for s in range(3)]

    def edge_rows(n):
        low, high = edge_row(11 + n), edge_row(3 + n)
        values = jnp.where(around_row == 0, low, jnp.where(around_row == ROWS - 1, high, 0.0))
        values = jnp.where(around_row == ROWS, bodies[n][22:23], values)
        return jnp.where(around_row == 2 * ROWS - 1, bodies[n][25:26], values)

    edge_along, edge_across = edge_rows(0), edge_rows(1)
    edge_turn = tiles_of(turn_window, slice(None))
    edge_signed = jnp.where(edge_turn > 0.0, turn_s, -turn_s)
    edge_scale = around * jnp.abs(edge_turn)
    along_change = edge_scale * (edge_along * (turn_c - 1.0) - edge_across * edge_signed)
    across_change = edge_scale * (edge_across * (turn_c - 1.0) + edge_along * edge_signed)
    changes = (along_change, across_change, -along_change)
    for s in range(3):
        body = bodies[s] + changes[s]
        from_south = jnp.where(
            around_row == 0, bodies[s][24:25], jnp.where(around_row == ROWS, edge_row(s), 0.0)
        )
        from_north = jnp.where(
            around_row == ROWS - 1, bodies[s][23:24], jnp.where(around_row == 2 * ROWS - 1, edge_row(8 + s), 0.0)
        )
        body = body + west_side * pltpu.roll(side_flux, s + 1, 1)
        body = body + east_side * pltpu.roll(side_flux, 2 * LANES - 1 - s, 1)
        body = body + south_mask * from_south + north_mask * from_north
        for t in range(2):
            stress[s, t] = body[:, LANES * t : LANES * (t + 1)]
        for c in range(2):
            pieces.append(
                jnp.concatenate([stress[s, t, pl.ds(c, SLOTS, stride=2), :] for t in range(2)], axis=1)
            )
    spread_stress = exact_dot(jnp.concatenate(pieces, axis=0), prolong)
    tensor = []
    for s in range(3):
        low = spread_stress[2 * SLOTS * s : 2 * SLOTS * s + SLOTS]
        high = spread_stress[2 * SLOTS * s + SLOTS : 2 * SLOTS * (s + 1)]
        tensor.append([low, 0.5 * low + 0.5 * high, high])
    cross_y, normal_y = along_y(tensor[1]), along_y(tensor[2])
    force_x = [inverse[c] * (along_x(tensor[0][c]) + cross_y[c]) for c in range(3)]
    force_y = [inverse[c] * (along_x(tensor[1][c]) + normal_y[c]) for c in range(3)]

    for step in range(ITERS):
        if step > 0:
            surface = raise_surface(surface, eastward, northward)
            pushed = push(surface, eastward, northward)
        eastward = [(pushed[0][c] + force_x[c]) * ocean_mask[c] for c in range(3)]
        northward = [(pushed[1][c] + force_y[c]) * ocean_mask[c] for c in range(3)]

    is_even = lax.rem(x, 2) == 0
    low_lanes = iota((8, LANES), 1) < 64
    halves = []
    for f, values in enumerate((surface, eastward, northward)):
        for c in range(3):
            own = values[c][:8]
            low, high = ocean_shift(own, -MARGIN_O), ocean_shift(own, 64 - MARGIN_O)
            place = 8 * (3 * f + c)
            result[place : place + 8, :] = jnp.where(is_even, low[:, :LANES], high[:, LANES:])
            halves.append(jnp.where(is_even, low[:, LANES:], pltpu.roll(high[:, :LANES], 64, 1)))
    for m in range(5):
        merged = halves[m] if m == 4 else jnp.where(low_lanes, halves[m], pltpu.roll(halves[5 + m], 64, 1))
        result[72 + 8 * m : 80 + 8 * m, :] = merged
    for dest in range(PEERS):
        result_send[dest, 0:8, :] = result[pl.ds(dest, 8, stride=8), :]
        result_send[dest, 8:14, :] = result[pl.ds(64 + dest, 6, stride=8), :]

    def result_copy(step):
        dest = peer(step)
        return pltpu.make_async_remote_copy(
            src_ref=result_send.at[dest[2]],
            dst_ref=result_land.at[x],
            send_sem=result_sem.at[0, step],
            recv_sem=result_sem.at[1, step],
            device_id=dest,
            device_id_type=MESH,
        )

    for step in FAR_FIRST:
        result_copy(step).start()
    result_land[x] = result_send[x]
    lax.fori_loop(DURING_STRESS, QUARTER, one_step, angle)
    for step in FAR_FIRST:
        pack_copy(step, False).wait_send()
        pack_copy(step, True).wait_send()
    for n in range(2):

        @pl.when(vertical[n])
        def _():
            band_copy(n, 0).wait_send()
            band_copy(n, 1).wait_send()

    for n, (dy, dx) in enumerate(AROUND):

        @pl.when(exists(dy, dx))
        def _():
            stress_copy(n).wait_send()

    for n in range(2, 4):
        wait_halo(n)

    def fix_step(i, angle):
        finish_rows(i, angle)
        return next_angle(*angle)

    lax.fori_loop(0, QUARTER, fix_step, angle_at(0))
    for n in range(4):

        @pl.when(sends[n])
        def _():
            halo_copy(n).wait_send()

    for step in FAR_FIRST:
        result_copy(step).wait_recv()
    for q in range(PEERS // 2):
        left, right = result_land[2 * q], result_land[2 * q + 1]
        left_turned, right_turned = pltpu.roll(left, 64, 1), pltpu.roll(right, 64, 1)
        side = iota((5, LANES), 1) < 64
        middle = jnp.concatenate(
            [
                jnp.where(side, left[9:14], right_turned[9:14]),
                jnp.where(side[:4], left_turned[9:13], right[9:13]),
            ],
            axis=0,
        )
        for t, tile in enumerate((left, middle, right)):
            lanes = pl.ds((3 * q + t) * LANES, LANES)
            for f in range(3):
                ocean_out[f, :, lanes] = tile[3 * f : 3 * f + 3]

    for step in FAR_FIRST:
        result_copy(step).wait_send()


def hand_over(ocean_in, updated, out, ocean_out, store_sem, local_sem):
    handed = pltpu.make_async_copy(ocean_in, ocean_out, local_sem)
    handed.start()
    size = CELLS // CHUNKS
    copies = [
        pltpu.make_async_copy(updated.at[pl.ds(n * size, size)], out.at[pl.ds(n * size, size)], store_sem.at[n])
        for n in range(CHUNKS)
    ]
    for copy in copies:
        copy.start()
    for copy in copies:
        copy.wait()
    handed.wait()


def shards(mesh_shape, spectrum, sea_mask, ocean_state, depth):
    groups_y = mesh_shape["gy"]
    groups = groups_y * mesh_shape["sec"]
    cells = spectrum.reshape(CELLS, LANES)
    vmem = pl.BlockSpec(memory_space=pltpu.VMEM)
    anywhere = pl.BlockSpec(memory_space=pl.ANY)
    f32 = jnp.float32
    dma = pltpu.SemaphoreType.DMA
    ocean_part, updated = pl.pallas_call(
        functools.partial(coupled_kernel, groups_y, groups),
        out_shape=(
            jax.ShapeDtypeStruct(ocean_state.shape, f32),
            jax.ShapeDtypeStruct((CELLS, LANES), f32),
        ),
        in_specs=[anywhere] * 4,
        out_specs=(vmem, vmem),
        scratch_shapes=[
            pltpu.VMEM((7 * ROWS, LANES), f32),
            pltpu.VMEM((2, HALF, LANES), f32),
            pltpu.VMEM((2, 6, ROWS, LANES), f32),
            pltpu.VMEM((CELLS + 2 * PAD, LANES), f32),
            pltpu.VMEM((4 * NFREQ, ROWS, LANES), f32),
            pltpu.VMEM(ocean_state.shape, f32),
            pltpu.VMEM(depth.shape, f32),
            pltpu.VMEM(sea_mask.shape, jnp.int32),
            pltpu.VMEM((SLOTS, 1792), f32),
            pltpu.VMEM((8, 1280), f32),
            pltpu.VMEM((PEERS, 2, 8, LANES), f32),
            pltpu.VMEM((PEERS, 2, 8, LANES), f32),
            pltpu.VMEM((2, SLOTS * 8, LANES), f32),
            pltpu.VMEM((2, SLOTS * 8, LANES), f32),
            pltpu.VMEM((2, 2 * ROWS, LANES), f32),
            pltpu.VMEM((2, 2 * ROWS, LANES), f32),
            pltpu.VMEM((5, ROWS, LANES), f32),
            pltpu.VMEM((2, 4, 8, LANES), f32),
            pltpu.VMEM((2, 5, ROWS, LANES), f32),
            pltpu.VMEM((3, 2, 4, 8, LANES), f32),
            pltpu.VMEM((3, 2, 2 * ROWS, LANES), f32),
            pltpu.VMEM((128, LANES), f32),
            pltpu.VMEM((PEERS, SLOTS, LANES), f32),
            pltpu.VMEM((PEERS, SLOTS, LANES), f32),
            pltpu.VMEM((2, HALF, LANES), f32),
            pltpu.VMEM((6, ROWS, LANES), f32),
            dma((3,)),
            dma((4 * LOADS,)),
            dma((2, PEERS)),
            dma((2, PEERS)),
            dma((2, 4)),
            dma((2, 8)),
            dma((2, PEERS)),
            dma((2, 4)),
            dma((4,)),
        ],
        compiler_params=pltpu.CompilerParams(
            collective_id=0, has_side_effects=True, vmem_limit_bytes=VMEM_LIMIT
        ),
        name="coupled",
    )(*[pltpu.with_memory_space_constraint(a, pltpu.HBM) for a in (cells, sea_mask, ocean_state, depth)])
    spectrum_out, ocean_out = pl.pallas_call(
        hand_over,
        out_shape=(jax.ShapeDtypeStruct((CELLS, LANES), f32), jax.ShapeDtypeStruct(ocean_state.shape, f32)),
        in_specs=[anywhere, anywhere],
        out_specs=(anywhere, anywhere),
        scratch_shapes=[dma((CHUNKS,)), dma],
        compiler_params=pltpu.CompilerParams(vmem_limit_bytes=VMEM_LIMIT),
        name="hand_over",
    )(ocean_part, updated)
    return (spectrum_out.reshape(spectrum.shape), ocean_out)


def solution(mesh):
    return jax.shard_map(
        functools.partial(shards, dict(mesh.shape)),
        mesh=mesh,
        in_specs=(
            P(None, None, ("sec", "gy"), "gx"),
            P(("sec", "gy", "gx"), None),
            P(None, ("sec", "gy", "gx"), None),
            P(("sec", "gy", "gx"), None),
        ),
        out_specs=(P(None, None, ("sec", "gy"), "gx"), P(None, ("sec", "gy", "gx"), None)),
        check_vma=False,
    )
```
